128 devices in a mesh: ctx: 32 (over z, x, y_lo), fsdp: 4 (over y_hi, core).
Axes of the slice: x: 4, y: 4 (y_hi: 2, y_lo: 2; y = y_hi * 2 + y_lo), z: 4, core: 2. Of those that a mesh axis runs over, the one named last changes fastest.
Arguments:
- tokens: bfloat16 [4, 4096, 1088], P('fsdp', 'ctx'), may hold values from -6 to 6
- cotangent: bfloat16 [4, 4096, 1088], P('fsdp', 'ctx'), may hold values from -6 to 6
- ln1_scale: bfloat16 [1088], P('fsdp'), may hold values from 0.5 to 1.5
- ln1_bias: bfloat16 [1088], P('fsdp'), may hold values from -1.5 to 1.5
- w_qkv: bfloat16 [1088, 3264], P('fsdp'), may hold values from -0.1875 to 0.1875
- bias_q: bfloat16 [1088], P('fsdp'), may hold values from -1.5 to 1.5
- bias_v: bfloat16 [1088], P('fsdp'), may hold values from -1.5 to 1.5
- w_out: bfloat16 [1088, 1088], P('fsdp'), may hold values from -3 to 3
- bias_out: bfloat16 [1088], P('fsdp'), may hold values from -1.5 to 1.5
- ln2_scale: bfloat16 [1088], P('fsdp'), may hold values from 0.5 to 1.5
- ln2_bias: bfloat16 [1088], P('fsdp'), may hold values from -1.5 to 1.5
- w_fc: bfloat16 [1088, 4352], P('fsdp'), may hold values from -0.1875 to 0.1875
- bias_fc: bfloat16 [4352], P('fsdp'), may hold values from -1.5 to 1.5
- w_down: bfloat16 [4352, 1088], P('fsdp'), may hold values from -0.09375 to 0.09375
- bias_down: bfloat16 [1088], P('fsdp'), may hold values from -1.5 to 1.5
Outputs:
- outputs: bfloat16 [4, 4096, 1088], P('fsdp', 'ctx')
- grad_tokens: float32 [4, 4096, 1088], P('fsdp', 'ctx')
- d_ln1_scale: float32 [1088], P('fsdp')
- d_ln1_bias: float32 [1088], P('fsdp')
- d_w_qkv: float32 [1088, 3264], P('fsdp')
- d_bias_q: float32 [1088], P('fsdp')
- d_bias_v: float32 [1088], P('fsdp')
- d_w_out: float32 [1088, 1088], P('fsdp')
- d_bias_out: float32 [1088], P('fsdp')
- d_ln2_scale: float32 [1088], P('fsdp')
- d_ln2_bias: float32 [1088], P('fsdp')
- d_w_fc: float32 [1088, 4352], P('fsdp')
- d_bias_fc: float32 [4352], P('fsdp')
- d_w_down: float32 [4352, 1088], P('fsdp')
- d_bias_down: float32 [1088], P('fsdp')
The draws below stay inside these ranges and needn't reach their ends.
All inputs are finite; a program needn't handle non-finite values.
Results may differ from the reference program's by a relative error of at most 0.025.
Values may be sent and summed in bfloat16 or wider, within the bound.
A program may use at most 256 MiB of HBM per device.

```python
import math
import jax
import jax.numpy as jnp
from jax import lax

D = 1088
HEADS = 17
HEAD_DIM = 64
FF = 4352
TOK_DEV = 128
LEN = 4096
SEQS = 4
N_CTX = 32


def levels(stream_key, dims, cuts, smallest, high):
    def one(axis_at, parts):
        steps = jax.random.uniform(jax.random.fold_in(jax.random.fold_in(stream_key, 6), axis_at), (parts,), jnp.float32, smallest / len(cuts), high / len(cuts))
        return jnp.repeat(jnp.exp(steps), dims[axis_at] // parts).reshape((-1,) + (1,) * (len(dims) - axis_at - 1))

    factor_of = one(*cuts[0])
    for cut in cuts[1:]:
        factor_of = factor_of * one(*cut)
    return factor_of


def centred(key, extent, scale, most, shards=(), kind=jnp.bfloat16):
    values = jax.random.normal(key, extent, jnp.float32) * scale
    if len(shards) > 0:
        values = levels(key, extent, shards, -0.22, 0.18) * values
    return jnp.clip(values, min=-most, max=most).astype(kind)


def setup_inputs(seed: int = 0) -> dict:
    key_list = jax.random.split(jax.random.key(seed), 16)
    return {
        "tokens": centred(key_list[0], (SEQS, LEN, D), 1.0, 6.0, ((0, 4), (1, 32))),
        "cotangent": centred(key_list[1], (SEQS, LEN, D), 1.0, 6.0, ((0, 4), (1, 32))),
        "ln1_scale": jnp.clip(1.0 + 0.1 * jax.random.normal(key_list[2], (D,), jnp.float32), 0.5, 1.5).astype(jnp.bfloat16),
        "ln1_bias": centred(key_list[3], (D,), 0.3, 1.5, ((0, 4),)),
        "w_qkv": centred(key_list[4], (D, 3 * D), D ** -0.5, 0.1875, ((0, 4),)),
        "bias_q": centred(key_list[5], (D,), 0.3, 1.5, ((0, 4),)),
        "bias_v": centred(key_list[6], (D,), 0.3, 1.5, ((0, 4),)),
        "w_out": centred(key_list[7], (D, D), (max(1, D * 16 // (TOK_DEV * N_CTX))) ** -0.5, 3.0, ((0, 4),)),
        "bias_out": centred(key_list[8], (D,), 0.3, 1.5, ((0, 4),)),
        "ln2_scale": jnp.clip(1.0 + 0.1 * jax.random.normal(key_list[9], (D,), jnp.float32), 0.5, 1.5).astype(jnp.bfloat16),
        "ln2_bias": centred(key_list[10], (D,), 0.3, 1.5, ((0, 4),)),
        "w_fc": centred(key_list[11], (D, FF), D ** -0.5, 0.1875, ((0, 4),)),
        "bias_fc": centred(key_list[12], (FF,), 0.3, 1.5, ((0, 4),)),
        "w_down": centred(key_list[13], (FF, D), FF ** -0.5, 0.09375, ((0, 4),)),
        "bias_down": centred(key_list[14], (D,), 0.3, 1.5, ((0, 4),)),
    }


@jax.custom_vjp
def low(v):
    return lax.optimization_barrier(v.astype(jnp.bfloat16)).astype(jnp.float32)

@jax.custom_vjp
def low_back(v):
    return v

def low_keep(v):
    return (low(v), None)

def low_pass(kept, grad):
    return (grad,)

def back_keep(v):
    return (v, None)

def back_low(kept, grad):
    return (low(grad),)
low.defvjp(low_keep, low_pass)
low_back.defvjp(back_keep, back_low)

def norm_rows(values, gain_vec, offset):
    centre = values - lax.optimization_barrier(jnp.mean(values, axis=-1, keepdims=True))
    spread = lax.optimization_barrier(jnp.mean(centre * centre, axis=-1, keepdims=True))
    return centre * lax.rsqrt(spread + 1e-05) * gain_vec + offset

def gelu_tanh(values):
    return 0.5 * values * (1.0 + jnp.tanh(0.7978845608028654 * (values + 0.044715 * values * values * values)))

def stored_positions(row_count, per_device):
    row_ids = jnp.arange(row_count, dtype=jnp.int32)
    device = row_ids // per_device
    within = row_ids % per_device
    half_size = per_device // 2
    devices = row_count // per_device
    block_id = jnp.where(within < half_size, device, 2 * devices - 1 - device)
    return (block_id * half_size + within % half_size).astype(jnp.int32)

def attend(queries, key_rows, value_rows, places):
    length = queries.shape[0]
    row_block = math.gcd(512, length)
    scaling = 1.0 / math.sqrt(HEAD_DIM)
    heads_q = queries.reshape(length // row_block, row_block, HEADS, HEAD_DIM)
    block_places = places.reshape(length // row_block, row_block)
    heads_k = key_rows.reshape(length, HEADS, HEAD_DIM)
    heads_v = value_rows.reshape(length, HEADS, HEAD_DIM)

    @jax.checkpoint
    def one_block(entry_pair):
        block_q, block_pos = entry_pair
        scores = jnp.einsum('qhd,khd->hqk', block_q, heads_k, precision=lax.Precision.HIGHEST) * scaling
        scores = low_back(scores)
        allowed = places[None, None, :] <= block_pos[None, :, None]
        scores = jnp.where(allowed, scores, -1e+30)
        row_max = lax.optimization_barrier(jnp.max(scores, axis=-1, keepdims=True))
        expd = jnp.exp(scores - row_max)
        probabilities = expd / lax.optimization_barrier(jnp.sum(expd, axis=-1, keepdims=True))
        result = jnp.einsum('hqk,khd->qhd', low(probabilities), heads_v, precision=lax.Precision.HIGHEST)
        return result.reshape(row_block, HEADS * HEAD_DIM)
    return lax.map(one_block, (heads_q, block_places)).reshape(length, HEADS * HEAD_DIM)

def block_layer(tokens, ln1_scale, ln1_bias, w_qkv, bias_q, bias_v, w_out, bias_out, ln2_scale, ln2_bias, w_fc, bias_fc, w_down, bias_down):
    model_width = tokens.shape[1]
    places = stored_positions(tokens.shape[0], TOK_DEV)
    normed = low(norm_rows(tokens, ln1_scale, ln1_bias))
    joint_rows = jnp.dot(normed, w_qkv, precision=lax.Precision.HIGHEST)
    queries = low_back(low(joint_rows[:, :model_width] + bias_q))
    key_rows = low_back(low(joint_rows[:, model_width:2 * model_width]))
    value_rows = low_back(low(joint_rows[:, 2 * model_width:] + bias_v))
    attended = low_back(low(attend(queries, key_rows, value_rows, places)))
    branch = low_back(jnp.dot(attended, w_out, precision=lax.Precision.HIGHEST) + bias_out)
    middle = tokens + branch
    normed2 = low(norm_rows(middle, ln2_scale, ln2_bias))
    hidden_pre = low_back(jnp.dot(normed2, w_fc, precision=lax.Precision.HIGHEST) + bias_fc)
    active = low(gelu_tanh(hidden_pre))
    out_branch = low_back(jnp.dot(active, w_down, precision=lax.Precision.HIGHEST) + bias_down)
    return middle + out_branch

def reference(tokens, cotangent, ln1_scale, ln1_bias, w_qkv, bias_q, bias_v, w_out, bias_out, ln2_scale, ln2_bias, w_fc, bias_fc, w_down, bias_down):
    params = tuple((weight.astype(jnp.float32) for weight in (ln1_scale, ln1_bias, w_qkv, bias_q, bias_v, w_out, bias_out, ln2_scale, ln2_bias, w_fc, bias_fc, w_down, bias_down)))

    def one_sequence(totals, entry_pair):
        seq_tokens, seq_cot = entry_pair
        result, pullback = jax.vjp(block_layer, seq_tokens.astype(jnp.float32), *params)
        gradients = pullback(seq_cot.astype(jnp.float32))
        totals = tuple((accum + extra for accum, extra in zip(totals, gradients[1:])))
        return (totals, (result.astype(jnp.bfloat16), gradients[0]))
    initial = tuple((jnp.zeros(weight.shape, jnp.float32) for weight in params))
    totals, (outputs, grad_tokens) = lax.scan(one_sequence, initial, (tokens, cotangent))
    return (outputs, grad_tokens, totals[0], totals[1], totals[2], totals[3], totals[4], totals[5], totals[6], totals[7], totals[8], totals[9], totals[10], totals[11], totals[12])
```

```python
import functools
import math

import jax
import jax.numpy as jnp
from jax import lax
from jax.experimental import pallas as pl
from jax.experimental.pallas import tpu as pltpu
from jax.sharding import PartitionSpec as P

MESH = pl.DeviceIdType.MESH
HEAD_DIM = 64
HEADS = 17
BLOCK = 64
STEP = 512


def head_place(head, core):
    return jnp.where(head < 16, 2 * head + core, 1 - core)


def held_head(place, core):
    own = lax.rem(place, 2) == core
    head = jnp.where(own, place // 2, 16)
    return own | (place == 1 - core), head


def greet_ctx(me, count):
    barrier = pltpu.get_barrier_semaphore()

    def greet(step, carry):
        pl.semaphore_signal(
            barrier, inc=1, device_id={"ctx": lax.rem(me + step, count)}, device_id_type=MESH
        )
        return carry

    lax.fori_loop(1, count, greet, 0)
    pl.semaphore_wait(barrier, count - 1)


def rows_of(place, half, count):
    block = place if half == 0 else 2 * count - 1 - place
    return pl.ds(pl.multiple_of(block * BLOCK, BLOCK), BLOCK)


def spread_kernel(count, x_ref, out_ref, send_sem, recv_sem, own_sem):
    me = lax.axis_index("ctx")
    core = lax.rem(lax.axis_index("fsdp"), 2)
    has, _ = held_head(me, core)
    greet_ctx(me, count)

    def remote(head, source, half):
        return pltpu.make_async_remote_copy(
            src_ref=x_ref.at[head, pl.ds(half * BLOCK, BLOCK)],
            dst_ref=out_ref.at[rows_of(source, half, count)],
            send_sem=send_sem.at[head, half],
            recv_sem=recv_sem.at[source, half],
            device_id={"ctx": head_place(head, core)},
            device_id_type=MESH,
        )

    def own(head, half):
        return pltpu.make_async_copy(
            x_ref.at[head, pl.ds(half * BLOCK, BLOCK)],
            out_ref.at[rows_of(me, half, count)],
            own_sem.at[half],
        )

    def send(head, carry):
        target = head_place(head, core)
        for half in range(2):

            @pl.when(target != me)
            def _():
                remote(head, me, half).start()

            @pl.when(target == me)
            def _():
                own(head, half).start()

        return carry

    lax.fori_loop(0, HEADS, send, 0)

    def sent(head, carry):
        target = head_place(head, core)
        for half in range(2):

            @pl.when(target != me)
            def _():
                remote(head, me, half).wait_send()

            @pl.when(target == me)
            def _():
                own(head, half).wait()

        return carry

    lax.fori_loop(0, HEADS, sent, 0)

    @pl.when(has)
    def _():
        def arrived(source, carry):
            for half in range(2):

                @pl.when(source != me)
                def _():
                    remote(0, source, half).wait_recv()

            return carry

        lax.fori_loop(0, count, arrived, 0)


def collect_kernel(count, y_ref, out_ref, send_sem, recv_sem, own_sem):
    me = lax.axis_index("ctx")
    core = lax.rem(lax.axis_index("fsdp"), 2)
    has, mine = held_head(me, core)
    greet_ctx(me, count)

    def remote(head, target, half):
        return pltpu.make_async_remote_copy(
            src_ref=y_ref.at[rows_of(target, half, count)],
            dst_ref=out_ref.at[head, pl.ds(half * BLOCK, BLOCK)],
            send_sem=send_sem.at[target, half],
            recv_sem=recv_sem.at[head, half],
            device_id={"ctx": target},
            device_id_type=MESH,
        )

    def own(half):
        return pltpu.make_async_copy(
            y_ref.at[rows_of(me, half, count)],
            out_ref.at[mine, pl.ds(half * BLOCK, BLOCK)],
            own_sem.at[half],
        )

    @pl.when(has)
    def _():
        def send(step, carry):
            target = lax.rem(me + step, count)
            for half in range(2):
                remote(mine, target, half).start()
            return carry

        lax.fori_loop(1, count, send, 0)
        for half in range(2):
            own(half).start()

        def sent(step, carry):
            target = lax.rem(me + step, count)
            for half in range(2):
                remote(mine, target, half).wait_send()
            return carry

        lax.fori_loop(1, count, sent, 0)
        for half in range(2):
            own(half).wait()

    def arrived(head, carry):
        for half in range(2):

            @pl.when(head_place(head, core) != me)
            def _():
                remote(head, 0, half).wait_recv()

        return carry

    lax.fori_loop(0, HEADS, arrived, 0)


def spread_heads(packed, count, collective):
    width = packed.shape[2]
    return pl.pallas_call(
        functools.partial(spread_kernel, count),
        out_shape=jax.ShapeDtypeStruct((2 * BLOCK * count, width), packed.dtype),
        in_specs=[pl.BlockSpec(memory_space=pl.ANY)],
        out_specs=pl.BlockSpec(memory_space=pl.ANY),
        scratch_shapes=[
            pltpu.SemaphoreType.DMA((HEADS, 2)),
            pltpu.SemaphoreType.DMA((count, 2)),
            pltpu.SemaphoreType.DMA((2,)),
        ],
        compiler_params=pltpu.CompilerParams(collective_id=collective, has_side_effects=True),
        cost_estimate=pl.CostEstimate(flops=0, bytes_accessed=4 << 20, transcendentals=0),
    )(packed)


def collect_heads(rows, count, collective):
    width = rows.shape[1]
    return pl.pallas_call(
        functools.partial(collect_kernel, count),
        out_shape=jax.ShapeDtypeStruct((HEADS, 2 * BLOCK, width), rows.dtype),
        in_specs=[pl.BlockSpec(memory_space=pl.ANY)],
        out_specs=pl.BlockSpec(memory_space=pl.ANY),
        scratch_shapes=[
            pltpu.SemaphoreType.DMA((count, 2)),
            pltpu.SemaphoreType.DMA((HEADS, 2)),
            pltpu.SemaphoreType.DMA((2,)),
        ],
        compiler_params=pltpu.CompilerParams(collective_id=collective, has_side_effects=True),
        cost_estimate=pl.CostEstimate(flops=0, bytes_accessed=4 << 20, transcendentals=0),
    )(rows)


def dot_nt(left, right):
    return lax.dot_general(
        left, right, (((1,), (1,)), ((), ())), preferred_element_type=jnp.float32
    )


def dot_nn(left, right):
    return jnp.dot(left, right, preferred_element_type=jnp.float32)


def causal(scores):
    keys = lax.broadcasted_iota(jnp.int32, scores.shape, 0)
    asks = lax.broadcasted_iota(jnp.int32, scores.shape, 1)
    return keys <= asks


def attend_forward(x_ref, out_ref, wide_ref, lse_ref, q_ref, k_ref, vt_ref):
    has, _ = held_head(lax.axis_index("ctx"), lax.rem(lax.axis_index("fsdp"), 2))
    blocks = x_ref.shape[0] // STEP

    @pl.when(has)
    def _():
        def prepare(at, carry):
            rows = pl.ds(pl.multiple_of(at * STEP, STEP), STEP)
            q_ref[rows, :] = x_ref[rows, 0:64] * jnp.bfloat16(0.125)
            k_ref[rows, :] = x_ref[rows, 64:128]
            vt_ref[:, rows] = x_ref[rows, 128:256].T[0:64, :]
            return carry

        lax.fori_loop(0, blocks, prepare, 0)

        def one_block(at, carry):
            asks = pl.ds(pl.multiple_of(at * STEP, STEP), STEP)
            query = q_ref[asks, :]

            def update(state, place, masked):
                top, total, accum = state
                keys = pl.ds(pl.multiple_of(place * STEP, STEP), STEP)
                scores = dot_nt(k_ref[keys, :], query)
                if masked:
                    scores = jnp.where(causal(scores), scores, -1e30)
                new_top = jnp.maximum(top, jnp.max(scores, axis=0, keepdims=True))
                factor = jnp.exp(top - new_top)
                weights = jnp.exp(scores - new_top)
                total = total * factor + jnp.sum(weights, axis=0, keepdims=True)
                accum = accum * factor + dot_nn(vt_ref[:, keys], weights.astype(jnp.bfloat16))
                return new_top, total, accum

            state = (
                jnp.full((1, STEP), -1e30, jnp.float32),
                jnp.zeros((1, STEP), jnp.float32),
                jnp.zeros((64, STEP), jnp.float32),
            )
            state = update(state, at, True)
            state = lax.fori_loop(0, at, lambda place, held: update(held, place, False), state)
            top, total, accum = state
            result = accum / total
            wide_ref[:, asks] = result
            lse_ref[:, asks] = top + jnp.log(total)
            full = jnp.concatenate([result, jnp.zeros_like(result)], axis=0)
            out_ref[asks, :] = full.T.astype(jnp.bfloat16)
            return carry

        lax.fori_loop(0, blocks, one_block, 0)


def attend_backward(
    x_ref, g_ref, wide_ref, lse_ref, out_ref, q_ref, k_ref, kt_ref, v_ref, go_ref, dq_ref, delta_ref
):
    has, _ = held_head(lax.axis_index("ctx"), lax.rem(lax.axis_index("fsdp"), 2))
    blocks = x_ref.shape[0] // STEP

    @pl.when(has)
    def _():
        def prepare(at, carry):
            rows = pl.ds(pl.multiple_of(at * STEP, STEP), STEP)
            q_ref[rows, :] = x_ref[rows, 0:64] * jnp.bfloat16(0.125)
            k_ref[rows, :] = x_ref[rows, 64:128]
            kt_ref[:, rows] = x_ref[rows, 0:128].T[64:128, :]
            v_ref[rows, :] = x_ref[rows, 128:192]
            go_ref[rows, :] = g_ref[rows, 0:64]
            turned = g_ref[rows, :].T[0:64, :].astype(jnp.float32)
            delta_ref[:, rows] = jnp.sum(turned * wide_ref[:, rows], axis=0, keepdims=True)
            dq_ref[:, rows] = jnp.zeros((64, STEP), jnp.float32)
            return carry

        lax.fori_loop(0, blocks, prepare, 0)

        def one_block(place, carry):
            keys = pl.ds(pl.multiple_of(place * STEP, STEP), STEP)
            key = k_ref[keys, :]
            turned_key = kt_ref[:, keys]
            value = v_ref[keys, :]

            def update(state, at, masked):
                grad_key, grad_value = state
                asks = pl.ds(pl.multiple_of(at * STEP, STEP), STEP)
                query = q_ref[asks, :]
                grad = go_ref[asks, :]
                probs = jnp.exp(dot_nt(key, query) - lse_ref[:, asks])
                if masked:
                    probs = jnp.where(causal(probs), probs, 0.0)
                grad_probs = dot_nt(value, grad)
                grad_scores = (probs * (grad_probs - delta_ref[:, asks])).astype(jnp.bfloat16)
                grad_value = grad_value + dot_nn(probs.astype(jnp.bfloat16), grad)
                grad_key = grad_key + dot_nn(grad_scores, query)
                dq_ref[:, asks] += dot_nn(turned_key, grad_scores)
                return grad_key, grad_value

            state = (jnp.zeros((STEP, 64), jnp.float32), jnp.zeros((STEP, 64), jnp.float32))
            state = update(state, place, True)
            grad_key, grad_value = lax.fori_loop(
                place + 1, blocks, lambda at, held: update(held, at, False), state
            )
            out_ref[keys, 64:128] = grad_key.astype(jnp.bfloat16)
            out_ref[keys, 128:192] = grad_value.astype(jnp.bfloat16)
            return carry

        lax.fori_loop(0, blocks, one_block, 0)

        def finish(at, carry):
            rows = pl.ds(pl.multiple_of(at * STEP, STEP), STEP)
            half = dq_ref[:, rows] * 0.125
            full = jnp.concatenate([half, jnp.zeros_like(half)], axis=0).T
            out_ref[rows, 0:64] = full[:, 0:64].astype(jnp.bfloat16)
            return carry

        lax.fori_loop(0, blocks, finish, 0)


def run_forward(rows):
    length = rows.shape[0]
    return pl.pallas_call(
        attend_forward,
        out_shape=(
            jax.ShapeDtypeStruct((length, 128), jnp.bfloat16),
            jax.ShapeDtypeStruct((64, length), jnp.float32),
            jax.ShapeDtypeStruct((1, length), jnp.float32),
        ),
        scratch_shapes=[
            pltpu.VMEM((length, 64), jnp.bfloat16),
            pltpu.VMEM((length, 64), jnp.bfloat16),
            pltpu.VMEM((64, length), jnp.bfloat16),
        ],
        compiler_params=pltpu.CompilerParams(vmem_limit_bytes=40 << 20),
        cost_estimate=pl.CostEstimate(
            flops=2 * length * length * 64,
            bytes_accessed=length * 512 * 2,
            transcendentals=length * length // 2,
        ),
    )(rows)


def run_backward(rows, grads, wide, lse):
    length = rows.shape[0]
    return pl.pallas_call(
        attend_backward,
        out_shape=jax.ShapeDtypeStruct((length, 256), jnp.bfloat16),
        scratch_shapes=[
            pltpu.VMEM((length, 64), jnp.bfloat16),
            pltpu.VMEM((length, 64), jnp.bfloat16),
            pltpu.VMEM((64, length), jnp.bfloat16),
            pltpu.VMEM((length, 64), jnp.bfloat16),
            pltpu.VMEM((length, 64), jnp.bfloat16),
            pltpu.VMEM((64, length), jnp.float32),
            pltpu.VMEM((1, length), jnp.float32),
        ],
        compiler_params=pltpu.CompilerParams(vmem_limit_bytes=40 << 20),
        cost_estimate=pl.CostEstimate(
            flops=5 * length * length * 64,
            bytes_accessed=length * 512 * 3,
            transcendentals=length * length // 2,
        ),
    )(rows, grads, wide, lse)


def pack_heads(*parts):
    rows = parts[0].shape[0]
    turned = [part.reshape(rows, HEADS, HEAD_DIM) for part in parts]
    if len(parts) % 2:
        turned.append(jnp.zeros((rows, HEADS, HEAD_DIM), parts[0].dtype))
    return jnp.transpose(jnp.concatenate(turned, axis=2), (1, 0, 2))


def unpack_heads(packed, at):
    part = packed[:, :, at * HEAD_DIM : (at + 1) * HEAD_DIM]
    return jnp.transpose(part, (1, 0, 2)).reshape(part.shape[1], HEADS * HEAD_DIM)


def norm_rows(values, gain_vec, offset):
    centre = values - jnp.mean(values, axis=-1, keepdims=True)
    spread = jnp.mean(centre * centre, axis=-1, keepdims=True)
    return centre * lax.rsqrt(spread + 1e-05) * gain_vec + offset


def gelu_tanh(values):
    return (
        0.5
        * values
        * (1.0 + jnp.tanh(0.7978845608028654 * (values + 0.044715 * values * values * values)))
    )


def local(
    tokens,
    cotangent,
    ln1_scale,
    ln1_bias,
    w_qkv,
    bias_q,
    bias_v,
    w_out,
    bias_out,
    ln2_scale,
    ln2_bias,
    w_fc,
    bias_fc,
    w_down,
    bias_down,
):
    ctx_count = lax.axis_size("ctx")
    model_width = tokens.shape[2]
    gathered = (
        lax.all_gather(ln1_scale, "fsdp", axis=0, tiled=True),
        lax.all_gather(ln1_bias, "fsdp", axis=0, tiled=True),
        lax.all_gather(w_qkv, "fsdp", axis=0, tiled=True),
        lax.all_gather(bias_q, "fsdp", axis=0, tiled=True),
        lax.all_gather(bias_v, "fsdp", axis=0, tiled=True),
        lax.all_gather(w_out, "fsdp", axis=0, tiled=True),
        lax.all_gather(bias_out, "fsdp", axis=0, tiled=True),
        lax.all_gather(ln2_scale, "fsdp", axis=0, tiled=True),
        lax.all_gather(ln2_bias, "fsdp", axis=0, tiled=True),
        lax.all_gather(w_fc, "fsdp", axis=0, tiled=True),
        lax.all_gather(bias_fc, "fsdp", axis=0, tiled=True),
        lax.all_gather(w_down, "fsdp", axis=0, tiled=True),
        lax.all_gather(bias_down, "fsdp", axis=0, tiled=True),
    )
    (
        g_scale1,
        g_shift1,
        full_qkv,
        full_bq,
        full_bv,
        full_out,
        full_bout,
        g_scale2,
        g_shift2,
        full_fc,
        full_bfc,
        full_down,
        full_bdown,
    ) = gathered
    scale_one = g_scale1.astype(jnp.float32)
    shift_one = g_shift1.astype(jnp.float32)
    scale_two = g_scale2.astype(jnp.float32)
    shift_two = g_shift2.astype(jnp.float32)
    inputs32 = tokens[0].astype(jnp.float32)
    norm_one, norm_one_pull = jax.vjp(norm_rows, inputs32, scale_one, shift_one)
    normed = norm_one.astype(jnp.bfloat16)
    joint_rows = jnp.dot(normed, full_qkv, preferred_element_type=jnp.float32)
    queries = (joint_rows[:, :model_width] + full_bq.astype(jnp.float32)).astype(jnp.bfloat16)
    key_rows = joint_rows[:, model_width : 2 * model_width].astype(jnp.bfloat16)
    value_rows = (joint_rows[:, 2 * model_width :] + full_bv.astype(jnp.float32)).astype(
        jnp.bfloat16
    )
    head_rows = spread_heads(pack_heads(queries, key_rows, value_rows), ctx_count, 1)
    out_rows, wide_out, lse_rows = run_forward(head_rows)
    attended = unpack_heads(collect_heads(out_rows, ctx_count, 2), 0)
    branch = jnp.dot(attended, full_out, preferred_element_type=jnp.float32) + full_bout.astype(
        jnp.float32
    )
    middle = inputs32 + branch
    norm_two, norm_two_pull = jax.vjp(norm_rows, middle, scale_two, shift_two)
    normed2 = norm_two.astype(jnp.bfloat16)
    hidden_pre = jnp.dot(normed2, full_fc, preferred_element_type=jnp.float32) + full_bfc.astype(
        jnp.float32
    )
    gelu_value, gelu_pull = jax.vjp(gelu_tanh, hidden_pre)
    active = gelu_value.astype(jnp.bfloat16)
    out_branch = jnp.dot(active, full_down, preferred_element_type=jnp.float32) + full_bdown.astype(
        jnp.float32
    )
    result = (middle + out_branch).astype(jnp.bfloat16)
    upstream = cotangent[0].astype(jnp.float32)
    grad_branch2 = cotangent[0]
    d_down = jnp.einsum("tf,td->fd", active, grad_branch2, preferred_element_type=jnp.float32)
    d_bdown = jnp.sum(upstream, axis=0)
    grad_active = jnp.einsum(
        "td,fd->tf", grad_branch2, full_down, preferred_element_type=jnp.float32
    )
    grad_hidden = gelu_pull(grad_active)[0].astype(jnp.bfloat16)
    d_fc = jnp.einsum("td,tf->df", normed2, grad_hidden, preferred_element_type=jnp.float32)
    d_bfc = jnp.sum(grad_hidden.astype(jnp.float32), axis=0)
    grad_normed2 = jnp.einsum("tf,df->td", grad_hidden, full_fc, preferred_element_type=jnp.float32)
    grad_mid_part, d_scale2, d_shift2 = norm_two_pull(grad_normed2)
    grad_middle = upstream + grad_mid_part
    grad_branch = grad_middle.astype(jnp.bfloat16)
    d_out = jnp.einsum("td,te->de", attended, grad_branch, preferred_element_type=jnp.float32)
    d_bout = jnp.sum(grad_branch.astype(jnp.float32), axis=0)
    grad_attended = jnp.einsum(
        "te,de->td", grad_branch, full_out, preferred_element_type=jnp.float32
    ).astype(jnp.bfloat16)
    grad_rows = spread_heads(pack_heads(grad_attended, jnp.zeros_like(grad_attended)), ctx_count, 3)
    joint_rows_grad = run_backward(head_rows, grad_rows, wide_out, lse_rows)
    packed_grads = collect_heads(joint_rows_grad, ctx_count, 4)
    grad_q16 = unpack_heads(packed_grads, 0)
    grad_k16 = unpack_heads(packed_grads, 1)
    grad_v16 = unpack_heads(packed_grads, 2)
    grad_joint = jnp.concatenate([grad_q16, grad_k16, grad_v16], axis=1)
    d_qkv = jnp.einsum("td,te->de", normed, grad_joint, preferred_element_type=jnp.float32)
    d_bq = jnp.sum(grad_q16.astype(jnp.float32), axis=0)
    d_bv = jnp.sum(grad_v16.astype(jnp.float32), axis=0)
    grad_normed = jnp.einsum("te,de->td", grad_joint, full_qkv, preferred_element_type=jnp.float32)
    grad_in_part, d_scale1, d_shift1 = norm_one_pull(grad_normed)
    grad_inputs = grad_middle + grad_in_part
    shard_terms = (
        lax.psum_scatter(
            d_scale1.astype(jnp.bfloat16), "fsdp", scatter_dimension=0, tiled=True
        ).astype(jnp.float32),
        lax.psum_scatter(
            d_shift1.astype(jnp.bfloat16), "fsdp", scatter_dimension=0, tiled=True
        ).astype(jnp.float32),
        lax.psum_scatter(
            d_qkv.astype(jnp.bfloat16), "fsdp", scatter_dimension=0, tiled=True
        ).astype(jnp.float32),
        lax.psum_scatter(d_bq.astype(jnp.bfloat16), "fsdp", scatter_dimension=0, tiled=True).astype(
            jnp.float32
        ),
        lax.psum_scatter(d_bv.astype(jnp.bfloat16), "fsdp", scatter_dimension=0, tiled=True).astype(
            jnp.float32
        ),
        lax.psum_scatter(
            d_out.astype(jnp.bfloat16), "fsdp", scatter_dimension=0, tiled=True
        ).astype(jnp.float32),
        lax.psum_scatter(
            d_bout.astype(jnp.bfloat16), "fsdp", scatter_dimension=0, tiled=True
        ).astype(jnp.float32),
        lax.psum_scatter(
            d_scale2.astype(jnp.bfloat16), "fsdp", scatter_dimension=0, tiled=True
        ).astype(jnp.float32),
        lax.psum_scatter(
            d_shift2.astype(jnp.bfloat16), "fsdp", scatter_dimension=0, tiled=True
        ).astype(jnp.float32),
        lax.psum_scatter(d_fc.astype(jnp.bfloat16), "fsdp", scatter_dimension=0, tiled=True).astype(
            jnp.float32
        ),
        lax.psum_scatter(
            d_bfc.astype(jnp.bfloat16), "fsdp", scatter_dimension=0, tiled=True
        ).astype(jnp.float32),
        lax.psum_scatter(
            d_down.astype(jnp.bfloat16), "fsdp", scatter_dimension=0, tiled=True
        ).astype(jnp.float32),
        lax.psum_scatter(
            d_bdown.astype(jnp.bfloat16), "fsdp", scatter_dimension=0, tiled=True
        ).astype(jnp.float32),
    )
    totals = (
        lax.psum(shard_terms[0].astype(jnp.bfloat16), "ctx").astype(jnp.float32),
        lax.psum(shard_terms[1].astype(jnp.bfloat16), "ctx").astype(jnp.float32),
        lax.psum(shard_terms[2].astype(jnp.bfloat16), "ctx").astype(jnp.float32),
        lax.psum(shard_terms[3].astype(jnp.bfloat16), "ctx").astype(jnp.float32),
        lax.psum(shard_terms[4].astype(jnp.bfloat16), "ctx").astype(jnp.float32),
        lax.psum(shard_terms[5].astype(jnp.bfloat16), "ctx").astype(jnp.float32),
        lax.psum(shard_terms[6].astype(jnp.bfloat16), "ctx").astype(jnp.float32),
        lax.psum(shard_terms[7].astype(jnp.bfloat16), "ctx").astype(jnp.float32),
        lax.psum(shard_terms[8].astype(jnp.bfloat16), "ctx").astype(jnp.float32),
        lax.psum(shard_terms[9].astype(jnp.bfloat16), "ctx").astype(jnp.float32),
        lax.psum(shard_terms[10].astype(jnp.bfloat16), "ctx").astype(jnp.float32),
        lax.psum(shard_terms[11].astype(jnp.bfloat16), "ctx").astype(jnp.float32),
        lax.psum(shard_terms[12].astype(jnp.bfloat16), "ctx").astype(jnp.float32),
    )
    return (result[None], grad_inputs[None]) + tuple(totals)


def solution(mesh):
    placed = (
        P("fsdp", "ctx", None),
        P("fsdp", "ctx", None),
        P("fsdp"),
        P("fsdp"),
        P("fsdp", None),
        P("fsdp"),
        P("fsdp"),
        P("fsdp", None),
        P("fsdp"),
        P("fsdp"),
        P("fsdp"),
        P("fsdp", None),
        P("fsdp"),
        P("fsdp", None),
        P("fsdp"),
    )
    return jax.shard_map(
        local,
        mesh=mesh,
        in_specs=placed,
        out_specs=(
            P("fsdp", "ctx", None),
            P("fsdp", "ctx", None),
            P("fsdp"),
            P("fsdp"),
            P("fsdp", None),
            P("fsdp"),
            P("fsdp"),
            P("fsdp", None),
            P("fsdp"),
            P("fsdp"),
            P("fsdp"),
            P("fsdp", None),
            P("fsdp"),
            P("fsdp", None),
            P("fsdp"),
        ),
        check_vma=False,
    )
```

```python
import functools
import math

import jax
import jax.numpy as jnp
from jax import lax
from jax.experimental import pallas as pl
from jax.experimental.pallas import tpu as pltpu
from jax.sharding import PartitionSpec as P

MESH = pl.DeviceIdType.MESH
HEAD_DIM = 64
HEADS = 17
BLOCK = 64
STEP = 512


def head_place(head, core):
    return jnp.where(head < 16, 2 * head + core, 1 - core)


def held_head(place, core):
    own = lax.rem(place, 2) == core
    head = jnp.where(own, place // 2, 16)
    return own | (place == 1 - core), head


def greet_ctx(me, count):
    barrier = pltpu.get_barrier_semaphore()

    def greet(step, carry):
        pl.semaphore_signal(
            barrier, inc=1, device_id={"ctx": lax.rem(me + step, count)}, device_id_type=MESH
        )
        return carry

    lax.fori_loop(1, count, greet, 0)
    pl.semaphore_wait(barrier, count - 1)


def rows_of(place, half, count):
    block = place if half == 0 else 2 * count - 1 - place
    return pl.ds(pl.multiple_of(block * BLOCK, BLOCK), BLOCK)


def spread_kernel(count, x_ref, out_ref, send_sem, recv_sem, own_sem):
    me = lax.axis_index("ctx")
    core = lax.rem(lax.axis_index("fsdp"), 2)
    has, _ = held_head(me, core)
    greet_ctx(me, count)

    def remote(head, source, half):
        return pltpu.make_async_remote_copy(
            src_ref=x_ref.at[head, pl.ds(half * BLOCK, BLOCK)],
            dst_ref=out_ref.at[rows_of(source, half, count)],
            send_sem=send_sem.at[head, half],
            recv_sem=recv_sem.at[source, half],
            device_id={"ctx": head_place(head, core)},
            device_id_type=MESH,
        )

    def own(head, half):
        return pltpu.make_async_copy(
            x_ref.at[head, pl.ds(half * BLOCK, BLOCK)],
            out_ref.at[rows_of(me, half, count)],
            own_sem.at[half],
        )

    def send(head, carry):
        target = head_place(head, core)
        for half in range(2):

            @pl.when(target != me)
            def _():
                remote(head, me, half).start()

            @pl.when(target == me)
            def _():
                own(head, half).start()

        return carry

    lax.fori_loop(0, HEADS, send, 0)

    def sent(head, carry):
        target = head_place(head, core)
        for half in range(2):

            @pl.when(target != me)
            def _():
                remote(head, me, half).wait_send()

            @pl.when(target == me)
            def _():
                own(head, half).wait()

        return carry

    lax.fori_loop(0, HEADS, sent, 0)

    @pl.when(has)
    def _():
        def arrived(source, carry):
            for half in range(2):

                @pl.when(source != me)
                def _():
                    remote(0, source, half).wait_recv()

            return carry

        lax.fori_loop(0, count, arrived, 0)


def collect_kernel(count, y_ref, out_ref, send_sem, recv_sem, own_sem):
    me = lax.axis_index("ctx")
    core = lax.rem(lax.axis_index("fsdp"), 2)
    has, mine = held_head(me, core)
    greet_ctx(me, count)

    def remote(head, target, half):
        return pltpu.make_async_remote_copy(
            src_ref=y_ref.at[rows_of(target, half, count)],
            dst_ref=out_ref.at[head, pl.ds(half * BLOCK, BLOCK)],
            send_sem=send_sem.at[target, half],
            recv_sem=recv_sem.at[head, half],
            device_id={"ctx": target},
            device_id_type=MESH,
        )

    def own(half):
        return pltpu.make_async_copy(
            y_ref.at[rows_of(me, half, count)],
            out_ref.at[mine, pl.ds(half * BLOCK, BLOCK)],
            own_sem.at[half],
        )

    @pl.when(has)
    def _():
        def send(step, carry):
            target = lax.rem(me + step, count)
            for half in range(2):
                remote(mine, target, half).start()
            return carry

        lax.fori_loop(1, count, send, 0)
        for half in range(2):
            own(half).start()

        def sent(step, carry):
            target = lax.rem(me + step, count)
            for half in range(2):
                remote(mine, target, half).wait_send()
            return carry

        lax.fori_loop(1, count, sent, 0)
        for half in range(2):
            own(half).wait()

    def arrived(head, carry):
        for half in range(2):

            @pl.when(head_place(head, core) != me)
            def _():
                remote(head, 0, half).wait_recv()

        return carry

    lax.fori_loop(0, HEADS, arrived, 0)


def spread_heads(packed, count, collective):
    width = packed.shape[2]
    return pl.pallas_call(
        functools.partial(spread_kernel, count),
        out_shape=jax.ShapeDtypeStruct((2 * BLOCK * count, width), packed.dtype),
        in_specs=[pl.BlockSpec(memory_space=pl.ANY)],
        out_specs=pl.BlockSpec(memory_space=pl.ANY),
        scratch_shapes=[
            pltpu.SemaphoreType.DMA((HEADS, 2)),
            pltpu.SemaphoreType.DMA((count, 2)),
            pltpu.SemaphoreType.DMA((2,)),
        ],
        compiler_params=pltpu.CompilerParams(collective_id=collective, has_side_effects=True),
        cost_estimate=pl.CostEstimate(flops=0, bytes_accessed=4 << 20, transcendentals=0),
    )(packed)


def collect_heads(rows, count, collective):
    width = rows.shape[1]
    return pl.pallas_call(
        functools.partial(collect_kernel, count),
        out_shape=jax.ShapeDtypeStruct((HEADS, 2 * BLOCK, width), rows.dtype),
        in_specs=[pl.BlockSpec(memory_space=pl.ANY)],
        out_specs=pl.BlockSpec(memory_space=pl.ANY),
        scratch_shapes=[
            pltpu.SemaphoreType.DMA((count, 2)),
            pltpu.SemaphoreType.DMA((HEADS, 2)),
            pltpu.SemaphoreType.DMA((2,)),
        ],
        compiler_params=pltpu.CompilerParams(collective_id=collective, has_side_effects=True),
        cost_estimate=pl.CostEstimate(flops=0, bytes_accessed=4 << 20, transcendentals=0),
    )(rows)


def dot_nt(left, right):
    return lax.dot_general(
        left, right, (((1,), (1,)), ((), ())), preferred_element_type=jnp.float32
    )


def dot_nn(left, right):
    return jnp.dot(left, right, preferred_element_type=jnp.float32)


def causal(scores):
    keys = lax.broadcasted_iota(jnp.int32, scores.shape, 0)
    asks = lax.broadcasted_iota(jnp.int32, scores.shape, 1)
    return keys <= asks


def attend_forward(x_ref, out_ref, wide_ref, lse_ref, q_ref, k_ref, vt_ref):
    has, _ = held_head(lax.axis_index("ctx"), lax.rem(lax.axis_index("fsdp"), 2))
    blocks = x_ref.shape[0] // STEP

    @pl.when(has)
    def _():
        def prepare(at, carry):
            rows = pl.ds(pl.multiple_of(at * STEP, STEP), STEP)
            q_ref[rows, :] = x_ref[rows, 0:64] * jnp.bfloat16(0.125)
            k_ref[rows, :] = x_ref[rows, 64:128]
            vt_ref[:, rows] = x_ref[rows, 128:256].T[0:64, :]
            return carry

        lax.fori_loop(0, blocks, prepare, 0)

        def one_block(at, carry):
            asks = pl.ds(pl.multiple_of(at * STEP, STEP), STEP)
            query = q_ref[asks, :]

            def update(state, place, masked):
                top, total, accum = state
                keys = pl.ds(pl.multiple_of(place * STEP, STEP), STEP)
                scores = dot_nt(k_ref[keys, :], query)
                if masked:
                    scores = jnp.where(causal(scores), scores, -1e30)
                new_top = jnp.maximum(top, jnp.max(scores, axis=0, keepdims=True))
                factor = jnp.exp(top - new_top)
                weights = jnp.exp(scores - new_top)
                total = total * factor + jnp.sum(weights, axis=0, keepdims=True)
                accum = accum * factor + dot_nn(vt_ref[:, keys], weights.astype(jnp.bfloat16))
                return new_top, total, accum

            state = (
                jnp.full((1, STEP), -1e30, jnp.float32),
                jnp.zeros((1, STEP), jnp.float32),
                jnp.zeros((64, STEP), jnp.float32),
            )
            state = update(state, at, True)
            state = lax.fori_loop(0, at, lambda place, held: update(held, place, False), state)
            top, total, accum = state
            result = accum / total
            wide_ref[:, asks] = result
            lse_ref[:, asks] = top + jnp.log(total)
            full = jnp.concatenate([result, jnp.zeros_like(result)], axis=0)
            out_ref[asks, :] = full.T.astype(jnp.bfloat16)
            return carry

        lax.fori_loop(0, blocks, one_block, 0)


def attend_backward(
    x_ref, g_ref, wide_ref, lse_ref, out_ref, q_ref, k_ref, kt_ref, v_ref, go_ref, dq_ref, delta_ref
):
    has, _ = held_head(lax.axis_index("ctx"), lax.rem(lax.axis_index("fsdp"), 2))
    blocks = x_ref.shape[0] // STEP

    @pl.when(has)
    def _():
        def prepare(at, carry):
            rows = pl.ds(pl.multiple_of(at * STEP, STEP), STEP)
            q_ref[rows, :] = x_ref[rows, 0:64] * jnp.bfloat16(0.125)
            k_ref[rows, :] = x_ref[rows, 64:128]
            kt_ref[:, rows] = x_ref[rows, 0:128].T[64:128, :]
            v_ref[rows, :] = x_ref[rows, 128:192]
            go_ref[rows, :] = g_ref[rows, 0:64]
            turned = g_ref[rows, :].T[0:64, :].astype(jnp.float32)
            delta_ref[:, rows] = jnp.sum(turned * wide_ref[:, rows], axis=0, keepdims=True)
            dq_ref[:, rows] = jnp.zeros((64, STEP), jnp.float32)
            return carry

        lax.fori_loop(0, blocks, prepare, 0)

        def one_block(place, carry):
            keys = pl.ds(pl.multiple_of(place * STEP, STEP), STEP)
            key = k_ref[keys, :]
            turned_key = kt_ref[:, keys]
            value = v_ref[keys, :]

            def update(state, at, masked):
                grad_key, grad_value = state
                asks = pl.ds(pl.multiple_of(at * STEP, STEP), STEP)
                query = q_ref[asks, :]
                grad = go_ref[asks, :]
                probs = jnp.exp(dot_nt(key, query) - lse_ref[:, asks])
                if masked:
                    probs = jnp.where(causal(probs), probs, 0.0)
                grad_probs = dot_nt(value, grad)
                grad_scores = (probs * (grad_probs - delta_ref[:, asks])).astype(jnp.bfloat16)
                grad_value = grad_value + dot_nn(probs.astype(jnp.bfloat16), grad)
                grad_key = grad_key + dot_nn(grad_scores, query)
                dq_ref[:, asks] += dot_nn(turned_key, grad_scores)
                return grad_key, grad_value

            state = (jnp.zeros((STEP, 64), jnp.float32), jnp.zeros((STEP, 64), jnp.float32))
            state = update(state, place, True)
            grad_key, grad_value = lax.fori_loop(
                place + 1, blocks, lambda at, held: update(held, at, False), state
            )
            out_ref[keys, 64:128] = grad_key.astype(jnp.bfloat16)
            out_ref[keys, 128:192] = grad_value.astype(jnp.bfloat16)
            return carry

        lax.fori_loop(0, blocks, one_block, 0)

        def finish(at, carry):
            rows = pl.ds(pl.multiple_of(at * STEP, STEP), STEP)
            half = dq_ref[:, rows] * 0.125
            full = jnp.concatenate([half, jnp.zeros_like(half)], axis=0).T
            out_ref[rows, 0:64] = full[:, 0:64].astype(jnp.bfloat16)
            return carry

        lax.fori_loop(0, blocks, finish, 0)


def run_forward(rows):
    length = rows.shape[0]
    return pl.pallas_call(
        attend_forward,
        out_shape=(
            jax.ShapeDtypeStruct((length, 128), jnp.bfloat16),
            jax.ShapeDtypeStruct((64, length), jnp.float32),
            jax.ShapeDtypeStruct((1, length), jnp.float32),
        ),
        scratch_shapes=[
            pltpu.VMEM((length, 64), jnp.bfloat16),
            pltpu.VMEM((length, 64), jnp.bfloat16),
            pltpu.VMEM((64, length), jnp.bfloat16),
        ],
        compiler_params=pltpu.CompilerParams(vmem_limit_bytes=40 << 20),
        cost_estimate=pl.CostEstimate(
            flops=2 * length * length * 64,
            bytes_accessed=length * 512 * 2,
            transcendentals=length * length // 2,
        ),
    )(rows)


def run_backward(rows, grads, wide, lse):
    length = rows.shape[0]
    return pl.pallas_call(
        attend_backward,
        out_shape=jax.ShapeDtypeStruct((length, 256), jnp.bfloat16),
        scratch_shapes=[
            pltpu.VMEM((length, 64), jnp.bfloat16),
            pltpu.VMEM((length, 64), jnp.bfloat16),
            pltpu.VMEM((64, length), jnp.bfloat16),
            pltpu.VMEM((length, 64), jnp.bfloat16),
            pltpu.VMEM((length, 64), jnp.bfloat16),
            pltpu.VMEM((64, length), jnp.float32),
            pltpu.VMEM((1, length), jnp.float32),
        ],
        compiler_params=pltpu.CompilerParams(vmem_limit_bytes=40 << 20),
        cost_estimate=pl.CostEstimate(
            flops=5 * length * length * 64,
            bytes_accessed=length * 512 * 3,
            transcendentals=length * length // 2,
        ),
    )(rows, grads, wide, lse)


def pack_heads(*parts):
    rows = parts[0].shape[0]
    turned = [part.reshape(rows, HEADS, HEAD_DIM) for part in parts]
    if len(parts) % 2:
        turned.append(jnp.zeros((rows, HEADS, HEAD_DIM), parts[0].dtype))
    return jnp.transpose(jnp.concatenate(turned, axis=2), (1, 0, 2))


def unpack_heads(packed, at):
    part = packed[:, :, at * HEAD_DIM : (at + 1) * HEAD_DIM]
    return jnp.transpose(part, (1, 0, 2)).reshape(part.shape[1], HEADS * HEAD_DIM)


UNITS = 17
PIECE = 6528
TAIL = 896


def places():
    ctx = lax.axis_index("ctx")
    fsdp = lax.axis_index("fsdp")
    return ctx // 8, lax.rem(ctx // 2, 4), lax.rem(ctx, 2), fsdp // 2, lax.rem(fsdp, 2)


def device_at(z, x, y_low, y_high, core):
    return (z * 8 + x * 2 + y_low, y_high * 2 + core)


def z_peer(step):
    z, x, y_low, y_high, core = places()
    return device_at(lax.rem(z + step, 4), x, y_low, y_high, core)


def x_peer(step):
    z, x, y_low, y_high, core = places()
    return device_at(z, lax.rem(x + step, 4), y_low, y_high, core)


def near_peer():
    z, x, y_low, y_high, core = places()
    return device_at(z, x, 1 - y_low, y_high, core)


def cross_peer():
    z, x, y_low, y_high, core = places()
    return device_at(z, x, 1 - y_low, 1 - y_high, core)


def far_peer():
    z, x, y_low, y_high, core = places()
    return device_at(z, x, y_low, 1 - y_high, core)


def twin_peer():
    z, x, y_low, y_high, core = places()
    return device_at(z, x, y_low, y_high, 1 - core)


def ring_peers():
    return [z_peer(step) for step in (1, 2, 3)] + [x_peer(step) for step in (1, 2, 3)]


def greet(peers):
    barrier = pltpu.get_barrier_semaphore()
    for peer in peers:
        pl.semaphore_signal(barrier, inc=1, device_id=peer, device_id_type=MESH)
    pl.semaphore_wait(barrier, len(peers))


class Sender:
    def __init__(self, send_sem, recv_sem):
        self.send_sem = send_sem
        self.recv_sem = recv_sem
        self.used = 0
        self.started = []

    def push(self, source, target, peer):
        copy = pltpu.make_async_remote_copy(
            src_ref=source,
            dst_ref=target,
            send_sem=self.send_sem.at[self.used],
            recv_sem=self.recv_sem.at[self.used],
            device_id=peer,
            device_id_type=MESH,
        )
        self.used += 1
        copy.start()
        self.started.append(copy)
        return copy

    def finish(self):
        for copy in self.started:
            copy.wait_send()


GATHER_COPIES = 4 * 19 + 3


def gather_kernel(*refs):
    sources, small = refs[0:4], refs[4]
    targets, small_out = refs[5:9], refs[9]
    own_sem, send_sem, recv_sem = refs[10:13]
    z, x, y_low, y_high, core = places()
    mine = y_high * 2 + core
    cross = (1 - y_high) * 2 + core
    other = y_high * 2 + 1 - core
    other_cross = (1 - y_high) * 2 + 1 - core
    greet(ring_peers() + [cross_peer(), far_peer(), twin_peer()] + [far_twin()])
    sender = Sender(send_sem, recv_sem)
    starts = ((2 * z, 2), (8 + 2 * x, 2), (16, 1))
    owns = []
    for at in range(4):
        owns.append(pltpu.make_async_copy(sources[at], targets[at].at[mine], own_sem.at[at]))
    owns.append(pltpu.make_async_copy(small, small_out.at[mine], own_sem.at[4]))
    small_in = [
        sender.push(small, small_out.at[mine], twin_peer()),
        sender.push(small, small_out.at[mine], far_peer()),
        sender.push(small, small_out.at[mine], far_twin()),
    ]
    crossed = []
    for at in range(4):
        crossed.append(
            [
                sender.push(
                    sources[at].at[pl.ds(start, size)],
                    targets[at].at[mine, pl.ds(start, size)],
                    cross_peer(),
                )
                for start, size in starts
            ]
        )
    for own in owns:
        own.start()
    twin_in = []
    for at in range(4):
        twin_in.append(sender.push(sources[at], targets[at].at[mine], twin_peer()))
    ringed = []
    for at in range(4):
        here = []
        for part, (start, size) in enumerate(starts):
            crossed[at][part].wait_recv()
            piece = targets[at].at[cross, pl.ds(start, size)]
            for step in (1, 3, 2):
                if part < 2:
                    peer = z_peer(step) if part == 0 else x_peer(step)
                    here.append((part, step, sender.push(piece, piece, peer)))
            twin_in.append(sender.push(piece, piece, twin_peer()))
        ringed.append(here)
    for at in range(4):
        for part, step, copy in ringed[at]:
            copy.wait_recv()
            if part == 0:
                start = 2 * lax.rem(z - step + 4, 4)
            else:
                start = 8 + 2 * lax.rem(x - step + 4, 4)
            piece = targets[at].at[cross, pl.ds(start, 2)]
            twin_in.append(sender.push(piece, piece, twin_peer()))
    for copy in small_in:
        copy.wait_recv()
    for copy in twin_in:
        copy.wait_recv()
    for own in owns:
        own.wait()
    sender.finish()


def far_twin():
    z, x, y_low, y_high, core = places()
    return device_at(z, x, y_low, 1 - y_high, 1 - core)


def gather_weights(parts, small, collective):
    shapes = [jax.ShapeDtypeStruct((4,) + part.shape, part.dtype) for part in parts + [small]]
    return pl.pallas_call(
        gather_kernel,
        out_shape=shapes,
        in_specs=[pl.BlockSpec(memory_space=pl.ANY)] * 5,
        out_specs=[pl.BlockSpec(memory_space=pl.ANY)] * 5,
        scratch_shapes=[
            pltpu.SemaphoreType.DMA((5,)),
            pltpu.SemaphoreType.DMA((GATHER_COPIES,)),
            pltpu.SemaphoreType.DMA((GATHER_COPIES,)),
        ],
        compiler_params=pltpu.CompilerParams(collective_id=collective, has_side_effects=True),
        cost_estimate=pl.CostEstimate(flops=0, bytes_accessed=60 << 20, transcendentals=0),
    )(*parts, small)


def first_kernel(*refs):
    parts, tail = refs[0:4], refs[4]
    by_z, by_x, tail_out = refs[5:9], refs[9:13], refs[13]
    send_sem, recv_sem = refs[14:16]
    z, x, y_low, y_high, core = places()
    greet(ring_peers())
    sender = Sender(send_sem, recv_sem)
    for step in (2, 1, 3):
        to_z, to_x = lax.rem(z + step, 4), lax.rem(x + step, 4)
        for at in range(4):
            sender.push(
                parts[at].at[:, pl.ds(2 * to_z, 2)], by_z[at].at[step - 1], z_peer(step)
            )
            sender.push(
                parts[at].at[:, pl.ds(8 + 2 * to_x, 2)], by_x[at].at[step - 1], x_peer(step)
            )
        sender.push(tail.at[:, to_z], tail_out.at[step - 1], z_peer(step))
    for copy in sender.started:
        copy.wait_recv()
    sender.finish()


def first_exchange(parts, tail, collective):
    shapes = [
        jax.ShapeDtypeStruct((3, 2, 2) + part.shape[2:], part.dtype) for part in parts + parts
    ]
    shapes.append(jax.ShapeDtypeStruct((3, 2, 4, 16, TAIL), tail.dtype))
    results = pl.pallas_call(
        first_kernel,
        out_shape=shapes,
        in_specs=[pl.BlockSpec(memory_space=pl.ANY)] * 5,
        out_specs=[pl.BlockSpec(memory_space=pl.ANY)] * 9,
        scratch_shapes=[pltpu.SemaphoreType.DMA((27,)), pltpu.SemaphoreType.DMA((27,))],
        compiler_params=pltpu.CompilerParams(collective_id=collective, has_side_effects=True),
        cost_estimate=pl.CostEstimate(flops=0, bytes_accessed=40 << 20, transcendentals=0),
    )(*parts, tail)
    return results[0:4], results[4:8], results[8]


LAST_COPIES = 9 + 3 + 9 + 36


def last_kernel(
    tz_ref,
    tx_ref,
    td_ref,
    gz_ref,
    gx_ref,
    gd_ref,
    rz_ref,
    rx_ref,
    rd_ref,
    sum_ref,
    in_ref,
    total_ref,
    own_sem,
    send_sem,
    recv_sem,
):
    z, x, y_low, y_high, core = places()
    greet(ring_peers() + [near_peer(), cross_peer(), far_peer()])
    sender = Sender(send_sem, recv_sem)
    spans = ((0, PIECE), (PIECE, PIECE), (2 * PIECE, TAIL))
    chunk = 1088
    for step in (2, 1, 3):
        to_z, to_x = lax.rem(z + step, 4), lax.rem(x + step, 4)
        sender.push(tz_ref.at[to_x], rz_ref.at[step - 1], x_peer(step))
        sender.push(tx_ref.at[to_z], rx_ref.at[step - 1], z_peer(step))
        sender.push(td_ref.at[to_x], rd_ref.at[step - 1], x_peer(step))
    for copy in sender.started:
        copy.wait_recv()

    groups = ((tz_ref, x, rz_ref), (tx_ref, z, rx_ref), (td_ref, x, rd_ref))
    for (terms, mine, others), (start, size) in zip(groups, spans):
        for low in range(0, size, PIECE // 3):
            high = min(low + PIECE // 3, size)
            total = terms[mine, :, :, low:high].astype(jnp.float32)
            for step in range(3):
                total = total + others[step, :, :, low:high].astype(jnp.float32)
            sum_ref[:, :, start + low : start + high] = total.astype(jnp.bfloat16)

    met = [
        sender.push(sum_ref.at[0], in_ref.at[0], near_peer()),
        sender.push(sum_ref.at[1], in_ref.at[1], cross_peer()),
        sender.push(sum_ref.at[1], in_ref.at[2], far_peer()),
    ]
    for copy in met:
        copy.wait_recv()
    for start, size in spans:
        for low in range(start, start + size, PIECE // 3):
            high = min(low + PIECE // 3, start + size)
            near = sum_ref[0, :, low:high].astype(jnp.float32) + in_ref[0, :, low:high].astype(
                jnp.float32
            )
            away = in_ref[1, :, low:high].astype(jnp.float32) + in_ref[2, :, low:high].astype(
                jnp.float32
            )
            total_ref[:, low:high] = (near + away).astype(jnp.bfloat16)

    pieces = [total_ref.at[:, pl.ds(start, size)] for start, size in spans]
    firsts = (gz_ref.at[z, x], gx_ref.at[x, z], gd_ref.at[z, x])
    owns = [
        pltpu.make_async_copy(pieces[at], firsts[at], own_sem.at[at]) for at in range(3)
    ]
    for own in owns:
        own.start()
    passed = []
    for step in (1, 3, 2):
        for at in range(3):
            peer = z_peer(step) if at == 1 else x_peer(step)
            passed.append((at, step, sender.push(pieces[at], firsts[at], peer)))
    ends = []
    for step in (1, 3, 2):
        for at in range(3):
            peer = x_peer(step) if at == 1 else z_peer(step)
            ends.append(sender.push(pieces[at], firsts[at], peer))
    for at, step, copy in passed:
        copy.wait_recv()
        from_x, from_z = lax.rem(x - step + 4, 4), lax.rem(z - step + 4, 4)
        place = (gz_ref.at[z, from_x], gx_ref.at[x, from_z], gd_ref.at[z, from_x])[at]
        for other in (1, 3, 2):
            peer = x_peer(other) if at == 1 else z_peer(other)
            ends.append(sender.push(place, place, peer))
    for copy in ends:
        copy.wait_recv()
    for own in owns:
        own.wait()
    sender.finish()


def last_exchange(tz, tx, td, collective):
    return pl.pallas_call(
        last_kernel,
        out_shape=(
            jax.ShapeDtypeStruct((4, 4, 16, PIECE), jnp.bfloat16),
            jax.ShapeDtypeStruct((4, 4, 16, PIECE), jnp.bfloat16),
            jax.ShapeDtypeStruct((4, 4, 16, TAIL), jnp.bfloat16),
        ),
        in_specs=[pl.BlockSpec(memory_space=pltpu.VMEM)] * 3,
        out_specs=[pl.BlockSpec(memory_space=pl.ANY)] * 3,
        scratch_shapes=[
            pltpu.VMEM((3, 2, 16, PIECE), jnp.bfloat16),
            pltpu.VMEM((3, 2, 16, PIECE), jnp.bfloat16),
            pltpu.VMEM((3, 2, 16, TAIL), jnp.bfloat16),
            pltpu.VMEM((2, 16, 2 * PIECE + TAIL), jnp.bfloat16),
            pltpu.VMEM((3, 16, 2 * PIECE + TAIL), jnp.bfloat16),
            pltpu.VMEM((16, 2 * PIECE + TAIL), jnp.bfloat16),
            pltpu.SemaphoreType.DMA((3,)),
            pltpu.SemaphoreType.DMA((LAST_COPIES,)),
            pltpu.SemaphoreType.DMA((LAST_COPIES,)),
        ],
        compiler_params=pltpu.CompilerParams(
            collective_id=collective, has_side_effects=True, vmem_limit_bytes=40 << 20
        ),
        cost_estimate=pl.CostEstimate(flops=0, bytes_accessed=16 << 20, transcendentals=0),
    )(tz, tx, td)


def flat_units(parts):
    lead = parts[0].shape[:-2]
    down = parts[3].reshape(lead + (4, 16, 1088))
    down = jnp.moveaxis(down, -3, -2).reshape(lead + (16, 4352))
    return jnp.concatenate([parts[0], parts[1], parts[2], down], axis=-1)


def wide_units(flat):
    lead = flat.shape[:-2]
    down = flat[..., 8704:].reshape(lead + (16, 4, 1088))
    down = jnp.moveaxis(down, -2, -3).reshape(lead + (64, 1088))
    return flat[..., :3264], flat[..., 3264:4352], flat[..., 4352:8704], down


def reduce_grads(parts, small, collective):
    z, x, y_low, y_high, core = places()
    parts = [part.reshape(2, UNITS, part.shape[1] // UNITS, part.shape[2]) for part in parts]
    last = flat_units([part[:, 16] for part in parts])
    extra = jnp.pad(small, ((0, 0), (0, 16 * 1280 - small.shape[1]))).reshape(2, 16, 1280)
    tail = jnp.concatenate([last, extra.astype(jnp.bfloat16)], axis=-1)
    tail = jnp.transpose(tail.reshape(2, 16, 4, 4, TAIL), (0, 2, 3, 1, 4))
    by_z, by_x, by_tail = first_exchange(parts, tail, collective)

    def added(own, others):
        total = own.astype(jnp.float32)
        for step in range(3):
            total = total + others[step].astype(jnp.float32)
        return total.astype(jnp.bfloat16)

    def first_sum(start, others):
        sums = []
        for part, other in zip(parts, others):
            size = (2, 2) + part.shape[2:]
            sums.append(added(lax.dynamic_slice(part, (0, start, 0, 0), size), other))
        flat = flat_units(sums).reshape(2, 2, 16, 2, PIECE)
        return jnp.transpose(flat, (1, 3, 0, 2, 4)).reshape(4, 2, 16, PIECE)

    tz = first_sum(2 * z, by_z)
    tx = first_sum(8 + 2 * x, by_x)
    td = added(lax.dynamic_index_in_dim(tail, z, 1, keepdims=False), by_tail)
    gz, gx, gd = last_exchange(tz, tx, jnp.transpose(td, (1, 0, 2, 3)), collective + 1)

    def units(whole):
        turned = jnp.transpose(whole.reshape(8, 2, 16, PIECE), (0, 2, 1, 3))
        return turned.reshape(8, 16, 2 * PIECE)

    tail_all = jnp.transpose(gd, (2, 0, 1, 3)).reshape(1, 16, 16 * TAIL)
    flat = jnp.concatenate([units(gz), units(gx), tail_all[:, :, : 2 * PIECE]], axis=0)
    outs = wide_units(flat)
    widths = [(272, 3264), (272, 1088), (272, 4352), (1088, 1088)]
    outs = [out.reshape(shape).astype(jnp.float32) for out, shape in zip(outs, widths)]
    extras = tail_all[0, :, 2 * PIECE :].reshape(-1)[:3264].astype(jnp.float32)
    return outs, extras


def norm_rows(values, gain_vec, offset):
    centre = values - jnp.mean(values, axis=-1, keepdims=True)
    spread = jnp.mean(centre * centre, axis=-1, keepdims=True)
    return centre * lax.rsqrt(spread + 1e-05) * gain_vec + offset


def gelu_tanh(values):
    return (
        0.5
        * values
        * (1.0 + jnp.tanh(0.7978845608028654 * (values + 0.044715 * values * values * values)))
    )


def local(
    tokens,
    cotangent,
    ln1_scale,
    ln1_bias,
    w_qkv,
    bias_q,
    bias_v,
    w_out,
    bias_out,
    ln2_scale,
    ln2_bias,
    w_fc,
    bias_fc,
    w_down,
    bias_down,
):
    ctx_count = lax.axis_size("ctx")
    model_width = tokens.shape[2]
    vectors = (
        ln1_scale,
        ln1_bias,
        bias_q,
        bias_v,
        bias_out,
        ln2_scale,
        ln2_bias,
        bias_down,
        bias_fc,
    )
    small = jnp.pad(jnp.concatenate(vectors), (0, 4096 - 3264)).reshape(16, 256)
    own_parts = [
        part.reshape(UNITS, part.shape[0] // UNITS, part.shape[1])
        for part in (w_qkv, w_out, w_fc, w_down)
    ]
    full_qkv, full_out, full_fc, full_down, full_small = gather_weights(own_parts, small, 5)
    full_qkv = full_qkv.reshape(1088, 3264)
    full_out = full_out.reshape(1088, 1088)
    full_fc = full_fc.reshape(1088, 4352)
    full_down = full_down.reshape(4352, 1088)
    full_small = full_small.reshape(4, 4096)
    (g_scale1, g_shift1, full_bq, full_bv, full_bout, g_scale2, g_shift2, full_bdown) = [
        full_small[:, at * 272 : (at + 1) * 272].reshape(1088) for at in range(8)
    ]
    full_bfc = full_small[:, 2176:3264].reshape(4352)
    z, x, y_low, y_high, core = places()

    def swap(values):
        return lax.ppermute(values, "fsdp", [(0, 1), (1, 0), (2, 3), (3, 2)])

    def split(values):
        quarters = values.reshape(values.shape[0], 2, 2, -1)
        first, second = quarters[:, :, 0], quarters[:, :, 1]
        keep = jnp.where(core == 0, first, second)
        give = jnp.where(core == 0, second, first)
        keep = jnp.where(y_high == 0, keep, keep[:, ::-1])
        give = jnp.where(y_high == 0, give, give[:, ::-1])
        return keep.reshape(values.shape[0], -1), give.reshape(values.shape[0], -1)

    def left_rows(values):
        keep, give = split(values)
        return jnp.concatenate([keep, swap(give)], axis=0)

    def right_rows(values):
        return jnp.concatenate([values, swap(values)], axis=0)

    def weight_terms(left, right):
        terms = lax.dot_general(
            left_rows(left),
            right_rows(right),
            (((0,), (0,)), ((), ())),
            preferred_element_type=jnp.float32,
        ).astype(jnp.bfloat16)
        return terms.reshape(2, terms.shape[0] // 2, terms.shape[1])

    scale_one = g_scale1.astype(jnp.float32)
    shift_one = g_shift1.astype(jnp.float32)
    scale_two = g_scale2.astype(jnp.float32)
    shift_two = g_shift2.astype(jnp.float32)
    inputs32 = tokens[0].astype(jnp.float32)
    norm_one, norm_one_pull = jax.vjp(norm_rows, inputs32, scale_one, shift_one)
    normed = norm_one.astype(jnp.bfloat16)
    joint_rows = jnp.dot(normed, full_qkv, preferred_element_type=jnp.float32)
    queries = (joint_rows[:, :model_width] + full_bq.astype(jnp.float32)).astype(jnp.bfloat16)
    key_rows = joint_rows[:, model_width : 2 * model_width].astype(jnp.bfloat16)
    value_rows = (joint_rows[:, 2 * model_width :] + full_bv.astype(jnp.float32)).astype(
        jnp.bfloat16
    )
    head_rows = spread_heads(pack_heads(queries, key_rows, value_rows), ctx_count, 1)
    out_rows, wide_out, lse_rows = run_forward(head_rows)
    attended = unpack_heads(collect_heads(out_rows, ctx_count, 2), 0)
    branch = jnp.dot(attended, full_out, preferred_element_type=jnp.float32) + full_bout.astype(
        jnp.float32
    )
    middle = inputs32 + branch
    norm_two, norm_two_pull = jax.vjp(norm_rows, middle, scale_two, shift_two)
    normed2 = norm_two.astype(jnp.bfloat16)
    hidden_pre = jnp.dot(normed2, full_fc, preferred_element_type=jnp.float32) + full_bfc.astype(
        jnp.float32
    )
    gelu_value, gelu_pull = jax.vjp(gelu_tanh, hidden_pre)
    active = gelu_value.astype(jnp.bfloat16)
    out_branch = jnp.dot(active, full_down, preferred_element_type=jnp.float32) + full_bdown.astype(
        jnp.float32
    )
    result = (middle + out_branch).astype(jnp.bfloat16)
    upstream = cotangent[0].astype(jnp.float32)
    grad_branch2 = cotangent[0]
    d_down = weight_terms(active, grad_branch2)
    d_bdown = jnp.sum(upstream, axis=0)
    grad_active = jnp.einsum(
        "td,fd->tf", grad_branch2, full_down, preferred_element_type=jnp.float32
    )
    grad_hidden = gelu_pull(grad_active)[0].astype(jnp.bfloat16)
    d_fc = weight_terms(normed2, grad_hidden)
    d_bfc = jnp.sum(grad_hidden.astype(jnp.float32), axis=0)
    grad_normed2 = jnp.einsum("tf,df->td", grad_hidden, full_fc, preferred_element_type=jnp.float32)
    grad_mid_part, d_scale2, d_shift2 = norm_two_pull(grad_normed2)
    grad_middle = upstream + grad_mid_part
    grad_branch = grad_middle.astype(jnp.bfloat16)
    d_out = weight_terms(attended, grad_branch)
    d_bout = jnp.sum(grad_branch.astype(jnp.float32), axis=0)
    grad_attended = jnp.einsum(
        "te,de->td", grad_branch, full_out, preferred_element_type=jnp.float32
    ).astype(jnp.bfloat16)
    grad_rows = spread_heads(pack_heads(grad_attended, jnp.zeros_like(grad_attended)), ctx_count, 3)
    joint_rows_grad = run_backward(head_rows, grad_rows, wide_out, lse_rows)
    packed_grads = collect_heads(joint_rows_grad, ctx_count, 4)
    grad_q16 = unpack_heads(packed_grads, 0)
    grad_k16 = unpack_heads(packed_grads, 1)
    grad_v16 = unpack_heads(packed_grads, 2)
    grad_joint = jnp.concatenate([grad_q16, grad_k16, grad_v16], axis=1)
    d_qkv = weight_terms(normed, grad_joint)
    d_bq = jnp.sum(grad_q16.astype(jnp.float32), axis=0)
    d_bv = jnp.sum(grad_v16.astype(jnp.float32), axis=0)
    grad_normed = jnp.einsum("te,de->td", grad_joint, full_qkv, preferred_element_type=jnp.float32)
    grad_in_part, d_scale1, d_shift1 = norm_one_pull(grad_normed)
    grad_inputs = grad_middle + grad_in_part
    narrow = (d_scale1, d_shift1, d_bq, d_bv, d_bout, d_scale2, d_shift2, d_bdown, d_bfc)
    sums = jnp.concatenate([vector.reshape(4, -1) for vector in narrow], axis=1)
    keep, give = split(sums.reshape(1, -1))
    sums = (keep + swap(give)).reshape(2, 3264)
    (t_qkv, t_out, t_fc, t_down), extras = reduce_grads((d_qkv, d_out, d_fc, d_down), sums, 6)
    (t_scale1, t_shift1, t_bq, t_bv, t_bout, t_scale2, t_shift2, t_bdown) = [
        extras[at * 272 : (at + 1) * 272] for at in range(8)
    ]
    t_bfc = extras[2176:]
    return (
        result[None],
        grad_inputs[None],
        t_scale1,
        t_shift1,
        t_qkv,
        t_bq,
        t_bv,
        t_out,
        t_bout,
        t_scale2,
        t_shift2,
        t_fc,
        t_bfc,
        t_down,
        t_bdown,
    )


def solution(mesh):
    placed = (
        P("fsdp", "ctx", None),
        P("fsdp", "ctx", None),
        P("fsdp"),
        P("fsdp"),
        P("fsdp", None),
        P("fsdp"),
        P("fsdp"),
        P("fsdp", None),
        P("fsdp"),
        P("fsdp"),
        P("fsdp"),
        P("fsdp", None),
        P("fsdp"),
        P("fsdp", None),
        P("fsdp"),
    )
    return jax.shard_map(
        local,
        mesh=mesh,
        in_specs=placed,
        out_specs=(
            P("fsdp", "ctx", None),
            P("fsdp", "ctx", None),
            P("fsdp"),
            P("fsdp"),
            P("fsdp", None),
            P("fsdp"),
            P("fsdp"),
            P("fsdp", None),
            P("fsdp"),
            P("fsdp"),
            P("fsdp"),
            P("fsdp", None),
            P("fsdp"),
            P("fsdp", None),
            P("fsdp"),
        ),
        check_vma=False,
    )
```

```python
import functools
import math

import jax
import jax.numpy as jnp
from jax import lax
from jax.experimental import pallas as pl
from jax.experimental.pallas import tpu as pltpu
from jax.sharding import PartitionSpec as P

MESH = pl.DeviceIdType.MESH
HEAD_DIM = 64
HEADS = 17
BLOCK = 64
STEP = 512


def head_place(head, core):
    return jnp.where(head < 16, 2 * head + core, 1 - core)


def held_head(place, core):
    own = lax.rem(place, 2) == core
    head = jnp.where(own, place // 2, 16)
    return own | (place == 1 - core), head


def greet_ctx(me, count):
    barrier = pltpu.get_barrier_semaphore()

    def greet(step, carry):
        pl.semaphore_signal(
            barrier, inc=1, device_id={"ctx": lax.rem(me + step, count)}, device_id_type=MESH
        )
        return carry

    lax.fori_loop(1, count, greet, 0)
    pl.semaphore_wait(barrier, count - 1)


def rows_of(place, half, count):
    block = place if half == 0 else 2 * count - 1 - place
    return pl.ds(pl.multiple_of(block * BLOCK, BLOCK), BLOCK)


def spread_kernel(count, x_ref, out_ref, send_sem, recv_sem, own_sem):
    me = lax.axis_index("ctx")
    core = lax.rem(lax.axis_index("fsdp"), 2)
    has, _ = held_head(me, core)
    greet_ctx(me, count)

    def remote(head, source, half):
        return pltpu.make_async_remote_copy(
            src_ref=x_ref.at[head, pl.ds(half * BLOCK, BLOCK)],
            dst_ref=out_ref.at[rows_of(source, half, count)],
            send_sem=send_sem.at[head, half],
            recv_sem=recv_sem.at[source, half],
            device_id={"ctx": head_place(head, core)},
            device_id_type=MESH,
        )

    def own(head, half):
        return pltpu.make_async_copy(
            x_ref.at[head, pl.ds(half * BLOCK, BLOCK)],
            out_ref.at[rows_of(me, half, count)],
            own_sem.at[half],
        )

    def send(head, carry):
        target = head_place(head, core)
        for half in range(2):

            @pl.when(target != me)
            def _():
                remote(head, me, half).start()

            @pl.when(target == me)
            def _():
                own(head, half).start()

        return carry

    lax.fori_loop(0, HEADS, send, 0)

    def sent(head, carry):
        target = head_place(head, core)
        for half in range(2):

            @pl.when(target != me)
            def _():
                remote(head, me, half).wait_send()

            @pl.when(target == me)
            def _():
                own(head, half).wait()

        return carry

    lax.fori_loop(0, HEADS, sent, 0)

    @pl.when(has)
    def _():
        def arrived(source, carry):
            for half in range(2):

                @pl.when(source != me)
                def _():
                    remote(0, source, half).wait_recv()

            return carry

        lax.fori_loop(0, count, arrived, 0)


def collect_kernel(count, y_ref, out_ref, send_sem, recv_sem, own_sem):
    me = lax.axis_index("ctx")
    core = lax.rem(lax.axis_index("fsdp"), 2)
    has, mine = held_head(me, core)
    greet_ctx(me, count)

    def remote(head, target, half):
        return pltpu.make_async_remote_copy(
            src_ref=y_ref.at[rows_of(target, half, count)],
            dst_ref=out_ref.at[head, pl.ds(half * BLOCK, BLOCK)],
            send_sem=send_sem.at[target, half],
            recv_sem=recv_sem.at[head, half],
            device_id={"ctx": target},
            device_id_type=MESH,
        )

    def own(half):
        return pltpu.make_async_copy(
            y_ref.at[rows_of(me, half, count)],
            out_ref.at[mine, pl.ds(half * BLOCK, BLOCK)],
            own_sem.at[half],
        )

    @pl.when(has)
    def _():
        def send(step, carry):
            target = lax.rem(me + step, count)
            for half in range(2):
                remote(mine, target, half).start()
            return carry

        lax.fori_loop(1, count, send, 0)
        for half in range(2):
            own(half).start()

        def sent(step, carry):
            target = lax.rem(me + step, count)
            for half in range(2):
                remote(mine, target, half).wait_send()
            return carry

        lax.fori_loop(1, count, sent, 0)
        for half in range(2):
            own(half).wait()

    def arrived(head, carry):
        for half in range(2):

            @pl.when(head_place(head, core) != me)
            def _():
                remote(head, 0, half).wait_recv()

        return carry

    lax.fori_loop(0, HEADS, arrived, 0)


def spread_heads(packed, count, collective):
    width = packed.shape[2]
    return pl.pallas_call(
        functools.partial(spread_kernel, count),
        out_shape=jax.ShapeDtypeStruct((2 * BLOCK * count, width), packed.dtype),
        in_specs=[pl.BlockSpec(memory_space=pl.ANY)],
        out_specs=pl.BlockSpec(memory_space=pl.ANY),
        scratch_shapes=[
            pltpu.SemaphoreType.DMA((HEADS, 2)),
            pltpu.SemaphoreType.DMA((count, 2)),
            pltpu.SemaphoreType.DMA((2,)),
        ],
        compiler_params=pltpu.CompilerParams(collective_id=collective, has_side_effects=True),
        cost_estimate=pl.CostEstimate(flops=0, bytes_accessed=4 << 20, transcendentals=0),
    )(packed)


def collect_heads(rows, count, collective):
    width = rows.shape[1]
    return pl.pallas_call(
        functools.partial(collect_kernel, count),
        out_shape=jax.ShapeDtypeStruct((HEADS, 2 * BLOCK, width), rows.dtype),
        in_specs=[pl.BlockSpec(memory_space=pl.ANY)],
        out_specs=pl.BlockSpec(memory_space=pl.ANY),
        scratch_shapes=[
            pltpu.SemaphoreType.DMA((count, 2)),
            pltpu.SemaphoreType.DMA((HEADS, 2)),
            pltpu.SemaphoreType.DMA((2,)),
        ],
        compiler_params=pltpu.CompilerParams(collective_id=collective, has_side_effects=True),
        cost_estimate=pl.CostEstimate(flops=0, bytes_accessed=4 << 20, transcendentals=0),
    )(rows)


def dot_nt(left, right):
    return lax.dot_general(
        left, right, (((1,), (1,)), ((), ())), preferred_element_type=jnp.float32
    )


def dot_nn(left, right):
    return jnp.dot(left, right, preferred_element_type=jnp.float32)


def causal(scores):
    keys = lax.broadcasted_iota(jnp.int32, scores.shape, 0)
    asks = lax.broadcasted_iota(jnp.int32, scores.shape, 1)
    return keys <= asks


def attend_forward(x_ref, out_ref, wide_ref, lse_ref, q_ref, k_ref, vt_ref):
    has, _ = held_head(lax.axis_index("ctx"), lax.rem(lax.axis_index("fsdp"), 2))
    blocks = x_ref.shape[0] // STEP

    @pl.when(has)
    def _():
        def prepare(at, carry):
            rows = pl.ds(pl.multiple_of(at * STEP, STEP), STEP)
            q_ref[rows, :] = x_ref[rows, 0:64] * jnp.bfloat16(0.125)
            k_ref[rows, :] = x_ref[rows, 64:128]
            vt_ref[:, rows] = x_ref[rows, 128:256].T[0:64, :]
            return carry

        lax.fori_loop(0, blocks, prepare, 0)

        def one_block(at, carry):
            asks = pl.ds(pl.multiple_of(at * STEP, STEP), STEP)
            query = q_ref[asks, :]

            def update(state, place, masked):
                top, total, accum = state
                keys = pl.ds(pl.multiple_of(place * STEP, STEP), STEP)
                scores = dot_nt(k_ref[keys, :], query)
                if masked:
                    scores = jnp.where(causal(scores), scores, -1e30)
                new_top = jnp.maximum(top, jnp.max(scores, axis=0, keepdims=True))
                factor = jnp.exp(top - new_top)
                weights = jnp.exp(scores - new_top)
                total = total * factor + jnp.sum(weights, axis=0, keepdims=True)
                accum = accum * factor + dot_nn(vt_ref[:, keys], weights.astype(jnp.bfloat16))
                return new_top, total, accum

            state = (
                jnp.full((1, STEP), -1e30, jnp.float32),
                jnp.zeros((1, STEP), jnp.float32),
                jnp.zeros((64, STEP), jnp.float32),
            )
            state = update(state, at, True)
            state = lax.fori_loop(0, at, lambda place, held: update(held, place, False), state)
            top, total, accum = state
            result = accum / total
            wide_ref[:, asks] = result
            lse_ref[:, asks] = top + jnp.log(total)
            full = jnp.concatenate([result, jnp.zeros_like(result)], axis=0)
            out_ref[asks, :] = full.T.astype(jnp.bfloat16)
            return carry

        lax.fori_loop(0, blocks, one_block, 0)


def attend_backward(
    x_ref,
    g_ref,
    wide_ref,
    lse_ref,
    fc_ref,
    down_ref,
    out_ref,
    fc_z_ref,
    down_z_ref,
    fc_x_ref,
    down_x_ref,
    q_ref,
    k_ref,
    kt_ref,
    v_ref,
    go_ref,
    dq_ref,
    delta_ref,
    send_sem,
    recv_sem,
):
    has, _ = held_head(lax.axis_index("ctx"), lax.rem(lax.axis_index("fsdp"), 2))
    blocks = x_ref.shape[0] // STEP
    greet(ring_peers())
    sender = Sender(send_sem, recv_sem)
    push_rings(sender, down_ref, down_z_ref, down_x_ref)
    push_rings(sender, fc_ref, fc_z_ref, fc_x_ref)

    @pl.when(has)
    def _():
        def prepare(at, carry):
            rows = pl.ds(pl.multiple_of(at * STEP, STEP), STEP)
            q_ref[rows, :] = x_ref[rows, 0:64] * jnp.bfloat16(0.125)
            k_ref[rows, :] = x_ref[rows, 64:128]
            kt_ref[:, rows] = x_ref[rows, 0:128].T[64:128, :]
            v_ref[rows, :] = x_ref[rows, 128:192]
            go_ref[rows, :] = g_ref[rows, 0:64]
            turned = g_ref[rows, :].T[0:64, :].astype(jnp.float32)
            delta_ref[:, rows] = jnp.sum(turned * wide_ref[:, rows], axis=0, keepdims=True)
            dq_ref[:, rows] = jnp.zeros((64, STEP), jnp.float32)
            return carry

        lax.fori_loop(0, blocks, prepare, 0)

        def one_block(place, carry):
            keys = pl.ds(pl.multiple_of(place * STEP, STEP), STEP)
            key = k_ref[keys, :]
            turned_key = kt_ref[:, keys]
            value = v_ref[keys, :]

            def update(state, at, masked):
                grad_key, grad_value = state
                asks = pl.ds(pl.multiple_of(at * STEP, STEP), STEP)
                query = q_ref[asks, :]
                grad = go_ref[asks, :]
                probs = jnp.exp(dot_nt(key, query) - lse_ref[:, asks])
                if masked:
                    probs = jnp.where(causal(probs), probs, 0.0)
                grad_probs = dot_nt(value, grad)
                grad_scores = (probs * (grad_probs - delta_ref[:, asks])).astype(jnp.bfloat16)
                grad_value = grad_value + dot_nn(probs.astype(jnp.bfloat16), grad)
                grad_key = grad_key + dot_nn(grad_scores, query)
                dq_ref[:, asks] += dot_nn(turned_key, grad_scores)
                return grad_key, grad_value

            state = (jnp.zeros((STEP, 64), jnp.float32), jnp.zeros((STEP, 64), jnp.float32))
            state = update(state, place, True)
            grad_key, grad_value = lax.fori_loop(
                place + 1, blocks, lambda at, held: update(held, at, False), state
            )
            out_ref[keys, 64:128] = grad_key.astype(jnp.bfloat16)
            out_ref[keys, 128:192] = grad_value.astype(jnp.bfloat16)
            return carry

        lax.fori_loop(0, blocks, one_block, 0)

        def finish(at, carry):
            rows = pl.ds(pl.multiple_of(at * STEP, STEP), STEP)
            half = dq_ref[:, rows] * 0.125
            full = jnp.concatenate([half, jnp.zeros_like(half)], axis=0).T
            out_ref[rows, 0:64] = full[:, 0:64].astype(jnp.bfloat16)
            return carry

        lax.fori_loop(0, blocks, finish, 0)

    for copy in sender.started:
        copy.wait_recv()
    sender.finish()


def run_forward(rows):
    length = rows.shape[0]
    return pl.pallas_call(
        attend_forward,
        out_shape=(
            jax.ShapeDtypeStruct((length, 128), jnp.bfloat16),
            jax.ShapeDtypeStruct((64, length), jnp.float32),
            jax.ShapeDtypeStruct((1, length), jnp.float32),
        ),
        scratch_shapes=[
            pltpu.VMEM((length, 64), jnp.bfloat16),
            pltpu.VMEM((length, 64), jnp.bfloat16),
            pltpu.VMEM((64, length), jnp.bfloat16),
        ],
        compiler_params=pltpu.CompilerParams(vmem_limit_bytes=40 << 20),
        cost_estimate=pl.CostEstimate(
            flops=2 * length * length * 64,
            bytes_accessed=length * 512 * 2,
            transcendentals=length * length // 2,
        ),
    )(rows)


def run_backward(rows, grads, wide, lse, fc, down, collective):
    length = rows.shape[0]
    inside = pl.BlockSpec(memory_space=pltpu.VMEM)
    outside = pl.BlockSpec(memory_space=pl.ANY)
    received = [
        jax.ShapeDtypeStruct((3, 2, 2) + part.shape[2:], part.dtype)
        for part in (fc, down, fc, down)
    ]
    results = pl.pallas_call(
        attend_backward,
        out_shape=[jax.ShapeDtypeStruct((length, 256), jnp.bfloat16)] + received,
        in_specs=[inside] * 4 + [outside] * 2,
        out_specs=[inside] + [outside] * 4,
        scratch_shapes=[
            pltpu.VMEM((length, 64), jnp.bfloat16),
            pltpu.VMEM((length, 64), jnp.bfloat16),
            pltpu.VMEM((64, length), jnp.bfloat16),
            pltpu.VMEM((length, 64), jnp.bfloat16),
            pltpu.VMEM((length, 64), jnp.bfloat16),
            pltpu.VMEM((64, length), jnp.float32),
            pltpu.VMEM((1, length), jnp.float32),
            pltpu.SemaphoreType.DMA((12,)),
            pltpu.SemaphoreType.DMA((12,)),
        ],
        compiler_params=pltpu.CompilerParams(
            collective_id=collective, has_side_effects=True, vmem_limit_bytes=40 << 20
        ),
        cost_estimate=pl.CostEstimate(
            flops=5 * length * length * 64,
            bytes_accessed=length * 512 * 3,
            transcendentals=length * length // 2,
        ),
    )(rows, grads, wide, lse, fc, down)
    return results[0], results[1:3], results[3:5]


def pack_heads(*parts):
    rows = parts[0].shape[0]
    turned = [part.reshape(rows, HEADS, HEAD_DIM) for part in parts]
    if len(parts) % 2:
        turned.append(jnp.zeros((rows, HEADS, HEAD_DIM), parts[0].dtype))
    return jnp.transpose(jnp.concatenate(turned, axis=2), (1, 0, 2))


def unpack_heads(packed, at):
    part = packed[:, :, at * HEAD_DIM : (at + 1) * HEAD_DIM]
    return jnp.transpose(part, (1, 0, 2)).reshape(part.shape[1], HEADS * HEAD_DIM)


UNITS = 17
TAIL = 896
SHAPES = ((16, 4352), (16, 4352), (64, 1088))
PIECES = ((16, 2176), (16, 2176), (32, 1088))


def places():
    ctx = lax.axis_index("ctx")
    fsdp = lax.axis_index("fsdp")
    return ctx // 8, lax.rem(ctx // 2, 4), lax.rem(ctx, 2), fsdp // 2, lax.rem(fsdp, 2)


def device_at(z, x, y_low, y_high, core):
    return (z * 8 + x * 2 + y_low, y_high * 2 + core)


def z_peer(step):
    z, x, y_low, y_high, core = places()
    return device_at(lax.rem(z + step, 4), x, y_low, y_high, core)


def x_peer(step):
    z, x, y_low, y_high, core = places()
    return device_at(z, lax.rem(x + step, 4), y_low, y_high, core)


def near_peer():
    z, x, y_low, y_high, core = places()
    return device_at(z, x, 1 - y_low, y_high, core)


def cross_peer():
    z, x, y_low, y_high, core = places()
    return device_at(z, x, 1 - y_low, 1 - y_high, core)


def far_peer():
    z, x, y_low, y_high, core = places()
    return device_at(z, x, y_low, 1 - y_high, core)


def twin_peer():
    z, x, y_low, y_high, core = places()
    return device_at(z, x, y_low, y_high, 1 - core)


def far_twin():
    z, x, y_low, y_high, core = places()
    return device_at(z, x, y_low, 1 - y_high, 1 - core)


def ring_peers():
    return [z_peer(step) for step in (1, 2, 3)] + [x_peer(step) for step in (1, 2, 3)]


def greet(peers):
    barrier = pltpu.get_barrier_semaphore()
    for peer in peers:
        pl.semaphore_signal(barrier, inc=1, device_id=peer, device_id_type=MESH)
    pl.semaphore_wait(barrier, len(peers))


class Sender:
    def __init__(self, send_sem, recv_sem):
        self.send_sem = send_sem
        self.recv_sem = recv_sem
        self.used = 0
        self.started = []

    def push(self, source, target, peer):
        copy = pltpu.make_async_remote_copy(
            src_ref=source,
            dst_ref=target,
            send_sem=self.send_sem.at[self.used],
            recv_sem=self.recv_sem.at[self.used],
            device_id=peer,
            device_id_type=MESH,
        )
        self.used += 1
        copy.start()
        self.started.append(copy)
        return copy

    def finish(self):
        for copy in self.started:
            copy.wait_send()


class Mover:
    def __init__(self, sem):
        self.sem = sem
        self.used = 0

    def move(self, source, target):
        copy = pltpu.make_async_copy(source, target, self.sem.at[self.used])
        self.used += 1
        copy.start()
        return copy


GATHER_COPIES = 4 * 35 + 3


def gather_kernel(*refs):
    sources, small = refs[0:4], refs[4]
    targets, small_out = refs[5:9], refs[9]
    holds, small_hold = refs[10:14], refs[14]
    own_sem, send_sem, recv_sem = refs[15:18]
    z, x, y_low, y_high, core = places()
    mine = y_high * 2 + core
    cross = (1 - y_high) * 2 + core
    mover = Mover(own_sem)
    loads = [mover.move(sources[at], holds[at]) for at in range(4)]
    loads.append(mover.move(small, small_hold))
    greet(ring_peers() + [near_peer(), cross_peer(), far_peer(), twin_peer(), far_twin()])
    sender = Sender(send_sem, recv_sem)
    firsts = (2 * z + y_low, 8 + 2 * x + y_low, 16)
    others = (2 * z + 1 - y_low, 8 + 2 * x + 1 - y_low)
    arrivals = [
        sender.push(small, small_out.at[mine], twin_peer()),
        sender.push(small, small_out.at[mine], far_peer()),
        sender.push(small, small_out.at[mine], far_twin()),
    ]
    crossed = [
        [
            sender.push(sources[at].at[unit], targets[at].at[mine, unit], cross_peer())
            for unit in others + (16,)
        ]
        for at in range(4)
    ]
    for at in range(4):
        arrivals.append(sender.push(sources[at], targets[at].at[mine], twin_peer()))
    owns = []
    for at in range(4):
        loads[at].wait()
        owns.append(mover.move(holds[at], targets[at].at[mine]))
    loads[4].wait()
    owns.append(mover.move(small_hold, small_out.at[mine]))

    def ring(at, part, unit, kept):
        piece = targets[at].at[cross, unit]
        for step in (1, 3, 2):
            peer = z_peer(step) if part == 0 else x_peer(step)
            kept.append((at, part, step, sender.push(piece, piece, peer)))

    first_ring, second_ring = [], []

    def second(at, nears):
        for part in range(2):
            nears[part].wait_recv()
            ring(at, part, others[part], second_ring)
            piece = targets[at].at[cross, others[part]]
            arrivals.append(sender.push(piece, piece, twin_peer()))

    waiting = None
    for at in range(4):
        nears = []
        for part in range(3):
            crossed[at][part].wait_recv()
            piece = targets[at].at[cross, firsts[part]]
            if part < 2:
                nears.append(sender.push(piece, piece, near_peer()))
                ring(at, part, firsts[part], first_ring)
            arrivals.append(sender.push(piece, piece, twin_peer()))
        if waiting is not None:
            second(*waiting)
        waiting = (at, nears)
    second(*waiting)

    for at in range(4):
        for kept, base in ((first_ring, y_low), (second_ring, 1 - y_low)):
            for where, part, step, copy in kept:
                if where != at:
                    continue
                copy.wait_recv()
                if part == 0:
                    unit = 2 * lax.rem(z - step + 4, 4) + base
                else:
                    unit = 8 + 2 * lax.rem(x - step + 4, 4) + base
                piece = targets[at].at[cross, unit]
                arrivals.append(sender.push(piece, piece, twin_peer()))
    for copy in arrivals:
        copy.wait_recv()
    for own in owns:
        own.wait()
    sender.finish()


def gather_weights(parts, small, collective):
    whole = list(parts) + [small]
    shapes = [jax.ShapeDtypeStruct((4,) + part.shape, part.dtype) for part in whole]
    return pl.pallas_call(
        gather_kernel,
        out_shape=shapes,
        in_specs=[pl.BlockSpec(memory_space=pl.ANY)] * 5,
        out_specs=[pl.BlockSpec(memory_space=pl.ANY)] * 5,
        scratch_shapes=[pltpu.VMEM(part.shape, part.dtype) for part in whole]
        + [
            pltpu.SemaphoreType.DMA((10,)),
            pltpu.SemaphoreType.DMA((GATHER_COPIES,)),
            pltpu.SemaphoreType.DMA((GATHER_COPIES,)),
        ],
        compiler_params=pltpu.CompilerParams(
            collective_id=collective, has_side_effects=True, vmem_limit_bytes=24 << 20
        ),
        cost_estimate=pl.CostEstimate(flops=0, bytes_accessed=60 << 20, transcendentals=0),
    )(*whole)


def push_rings(sender, terms, by_z, by_x):
    z, x, y_low, y_high, core = places()
    copies = []
    for step in (2, 1, 3):
        to_z, to_x = lax.rem(z + step, 4), lax.rem(x + step, 4)
        copies.append(
            sender.push(terms.at[:, pl.ds(2 * to_z, 2)], by_z.at[step - 1], z_peer(step))
        )
        copies.append(
            sender.push(terms.at[:, pl.ds(8 + 2 * to_x, 2)], by_x.at[step - 1], x_peer(step))
        )
    return copies


def widen(values):
    return values.astype(jnp.float32)


def halves(values, group):
    if group == 2:
        return values[0:32], values[32:64]
    return values[:, 0:2176], values[:, 2176:4352]


LAST_COPIES = 6 + 3 * (6 + 3 + 6 + 6 + 18) + 3 + 3 + 3 + 3 + 3 + 9


def last_kernel(*refs):
    terms, tail = refs[0:3], refs[3]
    far_z, far_x = (None,) + refs[4:6], (None,) + refs[6:8]
    totals, small_out = refs[8:11], refs[11]
    scratch = refs[12:]
    own, by, parted, met, merged, landed, summed = [
        scratch[3 * at : 3 * at + 3] for at in range(7)
    ]
    own_t, by_t, parted_t, met_t, merged_t, landed_t, summed_t, whole_t = scratch[21:29]
    units, small_unit = scratch[29:32], scratch[32]
    own_sem, send_sem, recv_sem = scratch[33:36]
    z, x, y_low, y_high, core = places()
    mover = Mover(own_sem)
    order = (2, 1, 0)
    loads = {}
    for group in order:
        loads[group] = [
            mover.move(terms[group].at[:, pl.ds(2 * z, 2)], own[group].at[0]),
            mover.move(terms[group].at[:, pl.ds(8 + 2 * x, 2)], own[group].at[1]),
        ]
        if group > 0:
            loads[group].append(mover.move(far_z[group], by[group].at[0]))
            loads[group].append(mover.move(far_x[group], by[group].at[1]))
    load_tail = mover.move(tail.at[:, z], own_t)
    greet(ring_peers() + [near_peer(), cross_peer(), far_peer()])
    sender = Sender(send_sem, recv_sem)
    first = push_rings(sender, terms[0], by[0].at[0], by[0].at[1])
    first_t = [
        sender.push(tail.at[:, lax.rem(z + step, 4)], by_t.at[step - 1], z_peer(step))
        for step in (2, 1, 3)
    ]

    second = {}
    for group in order:
        for load in loads[group]:
            load.wait()
        if group == 0:
            for copy in first:
                copy.wait_recv()
        second[group] = []
        for ring in range(2):
            for unit in range(2):
                for side in range(2):
                    total = widen(own[group][ring, side, unit])
                    for step in range(3):
                        total = total + widen(by[group][ring, step, side, unit])
                    pair = halves(total.astype(jnp.bfloat16), group)
                    parted[group][ring, 2 * unit, side] = pair[0]
                    parted[group][ring, 2 * unit + 1, side] = pair[1]
            for step in (2, 1, 3):
                place = lax.rem(x + step, 4) if ring == 0 else lax.rem(z + step, 4)
                peer = x_peer(step) if ring == 0 else z_peer(step)
                second[group].append(
                    sender.push(
                        parted[group].at[ring, place], met[group].at[ring, step - 1], peer
                    )
                )
    load_tail.wait()
    for copy in first_t:
        copy.wait_recv()
    for place in range(4):
        total = widen(own_t[:, place])
        for step in range(3):
            total = total + widen(by_t[step, :, place])
        parted_t[place] = total.astype(jnp.bfloat16)
    second_t = [
        sender.push(parted_t.at[lax.rem(x + step, 4)], met_t.at[step - 1], x_peer(step))
        for step in (2, 1, 3)
    ]

    def across(source, target):
        return [
            sender.push(source.at[0], target.at[0], near_peer()),
            sender.push(source.at[1], target.at[1], cross_peer()),
            sender.push(source.at[1], target.at[2], far_peer()),
        ]

    third = {}
    for group in order:
        for copy in second[group]:
            copy.wait_recv()
        for ring in range(2):
            total = widen(parted[group][ring, x if ring == 0 else z])
            for step in range(3):
                total = total + widen(met[group][ring, step])
            merged[group][:, ring] = total.astype(jnp.bfloat16)
        third[group] = across(merged[group], landed[group])
    for copy in second_t:
        copy.wait_recv()
    total = widen(parted_t[x])
    for step in range(3):
        total = total + widen(met_t[step])
    merged_t[...] = total.astype(jnp.bfloat16)
    third_t = across(merged_t, landed_t)

    def spot(group, ring, at_z, at_x):
        unit = 2 * at_z + at_x // 2 if ring == 0 else 8 + 2 * at_x + at_z // 2
        half = lax.rem(at_x, 2) if ring == 0 else lax.rem(at_z, 2)
        if group == 2:
            return totals[group].at[unit, pl.ds(pl.multiple_of(half * 32, 32), 32)]
        return totals[group].at[unit, :, pl.ds(pl.multiple_of(half * 2176, 128), 2176)]

    passed, ends, owns = [], [], []
    for group in order:
        for copy in third[group]:
            copy.wait_recv()
        near = widen(merged[group][0]) + widen(landed[group][0])
        away = widen(landed[group][1]) + widen(landed[group][2])
        summed[group][...] = (near + away).astype(jnp.bfloat16)
        for ring in range(2):
            place = spot(group, ring, z, x)
            piece = summed[group].at[ring]
            owns.append(mover.move(piece, place))
            for step in (1, 3, 2):
                peer = x_peer(step) if ring == 0 else z_peer(step)
                passed.append((group, ring, step, sender.push(piece, place, peer)))
            for step in (1, 3, 2):
                peer = z_peer(step) if ring == 0 else x_peer(step)
                ends.append(sender.push(piece, place, peer))
    for copy in third_t:
        copy.wait_recv()
    near = widen(merged_t[0]) + widen(landed_t[0])
    away = widen(landed_t[1]) + widen(landed_t[2])
    summed_t[...] = (near + away).astype(jnp.bfloat16)
    owns.append(mover.move(summed_t, whole_t.at[z, x]))
    for step in (1, 3, 2):
        passed.append((3, 0, step, sender.push(summed_t, whole_t.at[z, x], x_peer(step))))
    for step in (1, 3, 2):
        ends.append(sender.push(summed_t, whole_t.at[z, x], z_peer(step)))

    for group, ring, step, copy in passed:
        copy.wait_recv()
        if group == 3:
            place = whole_t.at[z, lax.rem(x - step + 4, 4)]
        elif ring == 0:
            place = spot(group, ring, z, lax.rem(x - step + 4, 4))
        else:
            place = spot(group, ring, lax.rem(z - step + 4, 4), x)
        for other in (1, 3, 2):
            peer = z_peer(other) if ring == 0 else x_peer(other)
            ends.append(sender.push(place, place, peer))
    for copy in ends:
        copy.wait_recv()
    for copy in owns:
        copy.wait()

    def tile(at):
        return whole_t[at // 28, at // 7 % 4, :, 128 * (at % 7) : 128 * (at % 7 + 1)]

    for at in range(34):
        units[0][:, 128 * at : 128 * (at + 1)] = tile(at)
        units[1][:, 128 * at : 128 * (at + 1)] = tile(34 + at)
    for row in range(4):
        for at in range(9):
            width = min(128, 1088 - 128 * at)
            units[2][16 * row : 16 * row + 16, 128 * at : 128 * at + width] = tile(
                68 + 9 * row + at
            )[:, :width]
    for at in range(8):
        small_unit[:, 128 * at : 128 * (at + 1)] = tile(104 + at)
    lasts = [mover.move(units[group], totals[group].at[16]) for group in range(3)]
    lasts.append(mover.move(small_unit, small_out))
    for copy in lasts:
        copy.wait()
    sender.finish()


def last_exchange(terms, tail, far_z, far_x, collective):
    low = jnp.bfloat16

    def each(make):
        return [pltpu.VMEM(make(*pair), low) for pair in zip(SHAPES, PIECES)]

    scratch = (
        each(lambda unit, piece: (2, 2, 2) + unit)
        + each(lambda unit, piece: (2, 3, 2, 2) + unit)
        + each(lambda unit, piece: (2, 4, 2) + piece)
        + each(lambda unit, piece: (2, 3, 2) + piece)
        + each(lambda unit, piece: (2, 2) + piece)
        + each(lambda unit, piece: (3, 2) + piece)
        + each(lambda unit, piece: (2,) + piece)
        + [
            pltpu.VMEM((2, 4, 16, TAIL), low),
            pltpu.VMEM((3, 2, 4, 16, TAIL), low),
            pltpu.VMEM((4, 2, 16, TAIL), low),
            pltpu.VMEM((3, 2, 16, TAIL), low),
            pltpu.VMEM((2, 16, TAIL), low),
            pltpu.VMEM((3, 16, TAIL), low),
            pltpu.VMEM((16, TAIL), low),
            pltpu.VMEM((4, 4, 16, TAIL), low),
        ]
        + each(lambda unit, piece: unit)
        + [
            pltpu.VMEM((16, 1024), low),
            pltpu.SemaphoreType.DMA((24,)),
            pltpu.SemaphoreType.DMA((LAST_COPIES,)),
            pltpu.SemaphoreType.DMA((LAST_COPIES,)),
        ]
    )
    return pl.pallas_call(
        last_kernel,
        out_shape=[jax.ShapeDtypeStruct((UNITS,) + unit, low) for unit in SHAPES]
        + [jax.ShapeDtypeStruct((16, 1024), low)],
        in_specs=[pl.BlockSpec(memory_space=pl.ANY)] * 8,
        out_specs=[pl.BlockSpec(memory_space=pl.ANY)] * 4,
        scratch_shapes=scratch,
        compiler_params=pltpu.CompilerParams(
            collective_id=collective, has_side_effects=True, vmem_limit_bytes=48 << 20
        ),
        cost_estimate=pl.CostEstimate(flops=0, bytes_accessed=40 << 20, transcendentals=0),
    )(*terms, tail, *far_z, *far_x)


def reduce_grads(terms, small, far_z, far_x, collective):
    down = terms[2][:, 16].reshape(2, 4, 16, 1088)
    down = jnp.pad(down, ((0, 0), (0, 0), (0, 0), (0, 64)))
    down = jnp.transpose(down, (0, 2, 1, 3)).reshape(2, 16, 4608)
    extra = jnp.pad(small, ((0, 0), (0, 16 * 1024 - small.shape[1]))).reshape(2, 16, 1024)
    tail = jnp.concatenate(
        [terms[0][:, 16], terms[1][:, 16], down, extra.astype(jnp.bfloat16)], axis=-1
    )
    tail = jnp.transpose(tail.reshape(2, 16, 4, 4, TAIL), (0, 2, 3, 1, 4))
    joint, fc, down, small = last_exchange(terms, tail, far_z, far_x, collective)
    joint = joint.reshape(272, 4352)
    outs = (
        joint[:, :3264].astype(jnp.float32),
        joint[:, 3264:].astype(jnp.float32),
        fc.reshape(272, 4352).astype(jnp.float32),
        down.reshape(1088, 1088).astype(jnp.float32),
    )
    return outs, small.reshape(-1)[:3264].astype(jnp.float32)


def norm_rows(values, gain_vec, offset):
    centre = values - jnp.mean(values, axis=-1, keepdims=True)
    spread = jnp.mean(centre * centre, axis=-1, keepdims=True)
    return centre * lax.rsqrt(spread + 1e-05) * gain_vec + offset


def gelu_tanh(values):
    return (
        0.5
        * values
        * (1.0 + jnp.tanh(0.7978845608028654 * (values + 0.044715 * values * values * values)))
    )


def local(
    tokens,
    cotangent,
    ln1_scale,
    ln1_bias,
    w_qkv,
    bias_q,
    bias_v,
    w_out,
    bias_out,
    ln2_scale,
    ln2_bias,
    w_fc,
    bias_fc,
    w_down,
    bias_down,
):
    ctx_count = lax.axis_size("ctx")
    model_width = tokens.shape[2]
    vectors = (
        ln1_scale,
        ln1_bias,
        bias_q,
        bias_v,
        bias_out,
        ln2_scale,
        ln2_bias,
        bias_down,
        bias_fc,
    )
    small = jnp.pad(jnp.concatenate(vectors), (0, 4096 - 3264)).reshape(16, 256)
    own_parts = [
        part.reshape(UNITS, part.shape[0] // UNITS, part.shape[1])
        for part in (w_qkv, w_out, w_fc, w_down)
    ]
    full_qkv, full_out, full_fc, full_down, full_small = gather_weights(own_parts, small, 5)
    full_qkv = full_qkv.reshape(1088, 3264)
    full_out = full_out.reshape(1088, 1088)
    full_fc = full_fc.reshape(1088, 4352)
    full_down = full_down.reshape(4352, 1088)
    full_small = full_small.reshape(4, 4096)
    (g_scale1, g_shift1, full_bq, full_bv, full_bout, g_scale2, g_shift2, full_bdown) = [
        full_small[:, at * 272 : (at + 1) * 272].reshape(1088) for at in range(8)
    ]
    full_bfc = full_small[:, 2176:3264].reshape(4352)
    z, x, y_low, y_high, core = places()

    def swap(values):
        return lax.ppermute(values, "fsdp", [(0, 1), (1, 0), (2, 3), (3, 2)])

    def split(values):
        quarters = values.reshape(values.shape[0], 2, 2, -1)
        first, second = quarters[:, :, 0], quarters[:, :, 1]
        keep = jnp.where(core == 0, first, second)
        give = jnp.where(core == 0, second, first)
        keep = jnp.where(y_high == 0, keep, keep[:, ::-1])
        give = jnp.where(y_high == 0, give, give[:, ::-1])
        return keep.reshape(values.shape[0], -1), give.reshape(values.shape[0], -1)

    def left_rows(values):
        keep, give = split(values)
        return jnp.concatenate([keep, swap(give)], axis=0)

    def right_rows(values):
        return jnp.concatenate([values, swap(values)], axis=0)

    def weight_terms(left, right):
        terms = lax.dot_general(
            left_rows(left),
            right_rows(right),
            (((0,), (0,)), ((), ())),
            preferred_element_type=jnp.float32,
        ).astype(jnp.bfloat16)
        return terms.reshape(2, UNITS, terms.shape[0] // (2 * UNITS), terms.shape[1])

    scale_one = g_scale1.astype(jnp.float32)
    shift_one = g_shift1.astype(jnp.float32)
    scale_two = g_scale2.astype(jnp.float32)
    shift_two = g_shift2.astype(jnp.float32)
    inputs32 = tokens[0].astype(jnp.float32)
    norm_one, norm_one_pull = jax.vjp(norm_rows, inputs32, scale_one, shift_one)
    normed = norm_one.astype(jnp.bfloat16)
    joint_rows = jnp.dot(normed, full_qkv, preferred_element_type=jnp.float32)
    queries = (joint_rows[:, :model_width] + full_bq.astype(jnp.float32)).astype(jnp.bfloat16)
    key_rows = joint_rows[:, model_width : 2 * model_width].astype(jnp.bfloat16)
    value_rows = (joint_rows[:, 2 * model_width :] + full_bv.astype(jnp.float32)).astype(
        jnp.bfloat16
    )
    head_rows = spread_heads(pack_heads(queries, key_rows, value_rows), ctx_count, 1)
    out_rows, wide_out, lse_rows = run_forward(head_rows)
    attended = unpack_heads(collect_heads(out_rows, ctx_count, 2), 0)
    branch = jnp.dot(attended, full_out, preferred_element_type=jnp.float32) + full_bout.astype(
        jnp.float32
    )
    middle = inputs32 + branch
    norm_two, norm_two_pull = jax.vjp(norm_rows, middle, scale_two, shift_two)
    normed2 = norm_two.astype(jnp.bfloat16)
    hidden_pre = jnp.dot(normed2, full_fc, preferred_element_type=jnp.float32) + full_bfc.astype(
        jnp.float32
    )
    gelu_value, gelu_pull = jax.vjp(gelu_tanh, hidden_pre)
    active = gelu_value.astype(jnp.bfloat16)
    out_branch = jnp.dot(active, full_down, preferred_element_type=jnp.float32) + full_bdown.astype(
        jnp.float32
    )
    result = (middle + out_branch).astype(jnp.bfloat16)
    upstream = cotangent[0].astype(jnp.float32)
    grad_branch2 = cotangent[0]
    d_down = weight_terms(active, grad_branch2)
    d_bdown = jnp.sum(upstream, axis=0)
    grad_active = jnp.einsum(
        "td,fd->tf", grad_branch2, full_down, preferred_element_type=jnp.float32
    )
    grad_hidden = gelu_pull(grad_active)[0].astype(jnp.bfloat16)
    d_fc = weight_terms(normed2, grad_hidden)
    d_bfc = jnp.sum(grad_hidden.astype(jnp.float32), axis=0)
    grad_normed2 = jnp.einsum("tf,df->td", grad_hidden, full_fc, preferred_element_type=jnp.float32)
    grad_mid_part, d_scale2, d_shift2 = norm_two_pull(grad_normed2)
    grad_middle = upstream + grad_mid_part
    grad_branch = grad_middle.astype(jnp.bfloat16)
    d_out = weight_terms(attended, grad_branch)
    d_bout = jnp.sum(grad_branch.astype(jnp.float32), axis=0)
    grad_attended = jnp.einsum(
        "te,de->td", grad_branch, full_out, preferred_element_type=jnp.float32
    ).astype(jnp.bfloat16)
    grad_rows = spread_heads(pack_heads(grad_attended, jnp.zeros_like(grad_attended)), ctx_count, 3)
    joint_rows_grad, far_z, far_x = run_backward(
        head_rows, grad_rows, wide_out, lse_rows, d_fc, d_down, 7
    )
    packed_grads = collect_heads(joint_rows_grad, ctx_count, 4)
    grad_q16 = unpack_heads(packed_grads, 0)
    grad_k16 = unpack_heads(packed_grads, 1)
    grad_v16 = unpack_heads(packed_grads, 2)
    grad_joint = jnp.concatenate([grad_q16, grad_k16, grad_v16], axis=1)
    d_qkv = weight_terms(normed, grad_joint)
    d_bq = jnp.sum(grad_q16.astype(jnp.float32), axis=0)
    d_bv = jnp.sum(grad_v16.astype(jnp.float32), axis=0)
    grad_normed = jnp.einsum("te,de->td", grad_joint, full_qkv, preferred_element_type=jnp.float32)
    grad_in_part, d_scale1, d_shift1 = norm_one_pull(grad_normed)
    grad_inputs = grad_middle + grad_in_part
    narrow = (d_scale1, d_shift1, d_bq, d_bv, d_bout, d_scale2, d_shift2, d_bdown, d_bfc)
    sums = jnp.concatenate([vector.reshape(4, -1) for vector in narrow], axis=1)
    keep, give = split(sums.reshape(1, -1))
    sums = (keep + swap(give)).reshape(2, 3264)
    (t_qkv, t_out, t_fc, t_down), extras = reduce_grads(
        (jnp.concatenate([d_qkv, d_out], axis=-1), d_fc, d_down), sums, far_z, far_x, 6
    )
    (t_scale1, t_shift1, t_bq, t_bv, t_bout, t_scale2, t_shift2, t_bdown) = [
        extras[at * 272 : (at + 1) * 272] for at in range(8)
    ]
    t_bfc = extras[2176:]
    return (
        result[None],
        grad_inputs[None],
        t_scale1,
        t_shift1,
        t_qkv,
        t_bq,
        t_bv,
        t_out,
        t_bout,
        t_scale2,
        t_shift2,
        t_fc,
        t_bfc,
        t_down,
        t_bdown,
    )


def solution(mesh):
    placed = (
        P("fsdp", "ctx", None),
        P("fsdp", "ctx", None),
        P("fsdp"),
        P("fsdp"),
        P("fsdp", None),
        P("fsdp"),
        P("fsdp"),
        P("fsdp", None),
        P("fsdp"),
        P("fsdp"),
        P("fsdp"),
        P("fsdp", None),
        P("fsdp"),
        P("fsdp", None),
        P("fsdp"),
    )
    return jax.shard_map(
        local,
        mesh=mesh,
        in_specs=placed,
        out_specs=(
            P("fsdp", "ctx", None),
            P("fsdp", "ctx", None),
            P("fsdp"),
            P("fsdp"),
            P("fsdp", None),
            P("fsdp"),
            P("fsdp"),
            P("fsdp", None),
            P("fsdp"),
            P("fsdp"),
            P("fsdp"),
            P("fsdp", None),
            P("fsdp"),
            P("fsdp", None),
            P("fsdp"),
        ),
        check_vma=False,
    )
```

```python
import functools

import jax
import jax.numpy as jnp
from jax import lax
from jax.experimental import pallas as pl
from jax.experimental.pallas import tpu as pltpu
from jax.sharding import PartitionSpec as P

MESH = pl.DeviceIdType.MESH
HEAD_DIM = 64
HEADS = 17
BLOCK = 64
STEP = 512


def head_place(head, core):
    return jnp.where(head < 16, 2 * head + core, 1 - core)


def held_head(place, core):
    own = lax.rem(place, 2) == core
    head = jnp.where(own, place // 2, 16)
    return own | (place == 1 - core), head


def greet_ctx(me, count):
    barrier = pltpu.get_barrier_semaphore()

    def greet(step, carry):
        pl.semaphore_signal(
            barrier, inc=1, device_id={"ctx": lax.rem(me + step, count)}, device_id_type=MESH
        )
        return carry

    lax.fori_loop(1, count, greet, 0)
    pl.semaphore_wait(barrier, count - 1)


def rows_of(place, half, count):
    block = place if half == 0 else 2 * count - 1 - place
    return pl.ds(pl.multiple_of(block * BLOCK, BLOCK), BLOCK)


def spread_kernel(count, x_ref, out_ref, send_sem, recv_sem, own_sem):
    me = lax.axis_index("ctx")
    core = lax.rem(lax.axis_index("fsdp"), 2)
    has, _ = held_head(me, core)
    greet_ctx(me, count)

    def remote(head, source, half):
        return pltpu.make_async_remote_copy(
            src_ref=x_ref.at[head, pl.ds(half * BLOCK, BLOCK)],
            dst_ref=out_ref.at[rows_of(source, half, count)],
            send_sem=send_sem.at[head, half],
            recv_sem=recv_sem.at[source, half],
            device_id={"ctx": head_place(head, core)},
            device_id_type=MESH,
        )

    def own(head, half):
        return pltpu.make_async_copy(
            x_ref.at[head, pl.ds(half * BLOCK, BLOCK)],
            out_ref.at[rows_of(me, half, count)],
            own_sem.at[half],
        )

    def send(head, carry):
        target = head_place(head, core)
        for half in range(2):

            @pl.when(target != me)
            def _():
                remote(head, me, half).start()

            @pl.when(target == me)
            def _():
                own(head, half).start()

        return carry

    lax.fori_loop(0, HEADS, send, 0)

    def sent(head, carry):
        target = head_place(head, core)
        for half in range(2):

            @pl.when(target != me)
            def _():
                remote(head, me, half).wait_send()

            @pl.when(target == me)
            def _():
                own(head, half).wait()

        return carry

    lax.fori_loop(0, HEADS, sent, 0)

    @pl.when(has)
    def _():
        def arrived(source, carry):
            for half in range(2):

                @pl.when(source != me)
                def _():
                    remote(0, source, half).wait_recv()

            return carry

        lax.fori_loop(0, count, arrived, 0)


def collect_kernel(count, y_ref, out_ref, send_sem, recv_sem, own_sem):
    me = lax.axis_index("ctx")
    core = lax.rem(lax.axis_index("fsdp"), 2)
    has, mine = held_head(me, core)
    greet_ctx(me, count)

    def remote(head, target, half):
        return pltpu.make_async_remote_copy(
            src_ref=y_ref.at[rows_of(target, half, count)],
            dst_ref=out_ref.at[head, pl.ds(half * BLOCK, BLOCK)],
            send_sem=send_sem.at[target, half],
            recv_sem=recv_sem.at[head, half],
            device_id={"ctx": target},
            device_id_type=MESH,
        )

    def own(half):
        return pltpu.make_async_copy(
            y_ref.at[rows_of(me, half, count)],
            out_ref.at[mine, pl.ds(half * BLOCK, BLOCK)],
            own_sem.at[half],
        )

    @pl.when(has)
    def _():
        def send(step, carry):
            target = lax.rem(me + step, count)
            for half in range(2):
                remote(mine, target, half).start()
            return carry

        lax.fori_loop(1, count, send, 0)
        for half in range(2):
            own(half).start()

        def sent(step, carry):
            target = lax.rem(me + step, count)
            for half in range(2):
                remote(mine, target, half).wait_send()
            return carry

        lax.fori_loop(1, count, sent, 0)
        for half in range(2):
            own(half).wait()

    def arrived(head, carry):
        for half in range(2):

            @pl.when(head_place(head, core) != me)
            def _():
                remote(head, 0, half).wait_recv()

        return carry

    lax.fori_loop(0, HEADS, arrived, 0)


def spread_heads(packed, count, collective):
    width = packed.shape[2]
    return pl.pallas_call(
        functools.partial(spread_kernel, count),
        out_shape=jax.ShapeDtypeStruct((2 * BLOCK * count, width), packed.dtype),
        in_specs=[pl.BlockSpec(memory_space=pl.ANY)],
        out_specs=pl.BlockSpec(memory_space=pl.ANY),
        scratch_shapes=[
            pltpu.SemaphoreType.DMA((HEADS, 2)),
            pltpu.SemaphoreType.DMA((count, 2)),
            pltpu.SemaphoreType.DMA((2,)),
        ],
        compiler_params=pltpu.CompilerParams(collective_id=collective, has_side_effects=True),
        cost_estimate=pl.CostEstimate(flops=0, bytes_accessed=4 << 20, transcendentals=0),
    )(packed)


def collect_heads(rows, count, collective):
    width = rows.shape[1]
    return pl.pallas_call(
        functools.partial(collect_kernel, count),
        out_shape=jax.ShapeDtypeStruct((HEADS, 2 * BLOCK, width), rows.dtype),
        in_specs=[pl.BlockSpec(memory_space=pl.ANY)],
        out_specs=pl.BlockSpec(memory_space=pl.ANY),
        scratch_shapes=[
            pltpu.SemaphoreType.DMA((count, 2)),
            pltpu.SemaphoreType.DMA((HEADS, 2)),
            pltpu.SemaphoreType.DMA((2,)),
        ],
        compiler_params=pltpu.CompilerParams(collective_id=collective, has_side_effects=True),
        cost_estimate=pl.CostEstimate(flops=0, bytes_accessed=4 << 20, transcendentals=0),
    )(rows)


def dot_nt(left, right):
    return lax.dot_general(
        left, right, (((1,), (1,)), ((), ())), preferred_element_type=jnp.float32
    )


def dot_nn(left, right):
    return jnp.dot(left, right, preferred_element_type=jnp.float32)


def causal(scores):
    keys = lax.broadcasted_iota(jnp.int32, scores.shape, 0)
    asks = lax.broadcasted_iota(jnp.int32, scores.shape, 1)
    return keys <= asks


def attend_forward(*refs):
    x_ref, sources = refs[0], refs[1:4]
    out_ref, wide_ref, lse_ref = refs[4:7]
    targets = refs[7:10]
    q_ref, k_ref, vt_ref = refs[10:13]
    holds = refs[13:16]
    own_sem, send_sem, recv_sem = refs[16:19]
    has, _ = held_head(lax.axis_index("ctx"), lax.rem(lax.axis_index("fsdp"), 2))
    blocks = x_ref.shape[0] // STEP
    greet(gather_peers())
    sender = Sender(send_sem, recv_sem)
    steps = gather_steps(sources, targets, holds, Mover(own_sem), sender)
    next(steps)

    @pl.when(has)
    def _():
        def prepare(at, carry):
            rows = pl.ds(pl.multiple_of(at * STEP, STEP), STEP)
            q_ref[rows, :] = x_ref[rows, 0:64] * jnp.bfloat16(0.125)
            k_ref[rows, :] = x_ref[rows, 64:128]
            vt_ref[:, rows] = x_ref[rows, 128:256].T[0:64, :]
            return carry

        lax.fori_loop(0, blocks, prepare, 0)

    def one_block(at):
        asks = pl.ds(at * STEP, STEP)
        query = q_ref[asks, :]

        def update(state, place, masked):
            top, total, accum = state
            keys = pl.ds(pl.multiple_of(place * STEP, STEP), STEP)
            scores = dot_nt(k_ref[keys, :], query)
            if masked:
                scores = jnp.where(causal(scores), scores, -1e30)
            new_top = jnp.maximum(top, jnp.max(scores, axis=0, keepdims=True))
            factor = jnp.exp(top - new_top)
            weights = jnp.exp(scores - new_top)
            total = total * factor + jnp.sum(weights, axis=0, keepdims=True)
            accum = accum * factor + dot_nn(vt_ref[:, keys], weights.astype(jnp.bfloat16))
            return new_top, total, accum

        state = (
            jnp.full((1, STEP), -1e30, jnp.float32),
            jnp.zeros((1, STEP), jnp.float32),
            jnp.zeros((64, STEP), jnp.float32),
        )
        state = update(state, at, True)
        state = lax.fori_loop(0, at, lambda place, held: update(held, place, False), state)
        top, total, accum = state
        result = accum / total
        wide_ref[:, asks] = result
        lse_ref[:, asks] = top + jnp.log(total)
        full = jnp.concatenate([result, jnp.zeros_like(result)], axis=0)
        out_ref[asks, :] = full.T.astype(jnp.bfloat16)

    for at in range(blocks):
        pl.when(has)(functools.partial(one_block, at))
        if at >= 3:
            next(steps, None)
    for _ in steps:
        pass
    sender.finish()


def attend_backward(
    x_ref,
    g_ref,
    wide_ref,
    lse_ref,
    fc_ref,
    down_ref,
    out_ref,
    fc_z_ref,
    down_z_ref,
    fc_x_ref,
    down_x_ref,
    q_ref,
    k_ref,
    kt_ref,
    v_ref,
    go_ref,
    dq_ref,
    delta_ref,
    send_sem,
    recv_sem,
):
    has, _ = held_head(lax.axis_index("ctx"), lax.rem(lax.axis_index("fsdp"), 2))
    blocks = x_ref.shape[0] // STEP
    greet(ring_peers())
    sender = Sender(send_sem, recv_sem)
    push_rings(sender, down_ref, down_z_ref, down_x_ref)
    push_rings(sender, fc_ref, fc_z_ref, fc_x_ref)

    @pl.when(has)
    def _():
        def prepare(at, carry):
            rows = pl.ds(pl.multiple_of(at * STEP, STEP), STEP)
            q_ref[rows, :] = x_ref[rows, 0:64] * jnp.bfloat16(0.125)
            k_ref[rows, :] = x_ref[rows, 64:128]
            kt_ref[:, rows] = x_ref[rows, 0:128].T[64:128, :]
            v_ref[rows, :] = x_ref[rows, 128:192]
            go_ref[rows, :] = g_ref[rows, 0:64]
            turned = g_ref[rows, :].T[0:64, :].astype(jnp.float32)
            delta_ref[:, rows] = jnp.sum(turned * wide_ref[:, rows], axis=0, keepdims=True)
            dq_ref[:, rows] = jnp.zeros((64, STEP), jnp.float32)
            return carry

        lax.fori_loop(0, blocks, prepare, 0)

        def one_block(place, carry):
            keys = pl.ds(pl.multiple_of(place * STEP, STEP), STEP)
            key = k_ref[keys, :]
            turned_key = kt_ref[:, keys]
            value = v_ref[keys, :]

            def update(state, at, masked):
                grad_key, grad_value = state
                asks = pl.ds(pl.multiple_of(at * STEP, STEP), STEP)
                query = q_ref[asks, :]
                grad = go_ref[asks, :]
                probs = jnp.exp(dot_nt(key, query) - lse_ref[:, asks])
                if masked:
                    probs = jnp.where(causal(probs), probs, 0.0)
                grad_probs = dot_nt(value, grad)
                grad_scores = (probs * (grad_probs - delta_ref[:, asks])).astype(jnp.bfloat16)
                grad_value = grad_value + dot_nn(probs.astype(jnp.bfloat16), grad)
                grad_key = grad_key + dot_nn(grad_scores, query)
                dq_ref[:, asks] += dot_nn(turned_key, grad_scores)
                return grad_key, grad_value

            state = (jnp.zeros((STEP, 64), jnp.float32), jnp.zeros((STEP, 64), jnp.float32))
            state = update(state, place, True)
            grad_key, grad_value = lax.fori_loop(
                place + 1, blocks, lambda at, held: update(held, at, False), state
            )
            out_ref[keys, 64:128] = grad_key.astype(jnp.bfloat16)
            out_ref[keys, 128:192] = grad_value.astype(jnp.bfloat16)
            return carry

        lax.fori_loop(0, blocks, one_block, 0)

        def finish(at, carry):
            rows = pl.ds(pl.multiple_of(at * STEP, STEP), STEP)
            half = dq_ref[:, rows] * 0.125
            full = jnp.concatenate([half, jnp.zeros_like(half)], axis=0).T
            out_ref[rows, 0:64] = full[:, 0:64].astype(jnp.bfloat16)
            return carry

        lax.fori_loop(0, blocks, finish, 0)

    for copy in sender.started:
        copy.wait_recv()
    sender.finish()


def run_forward(rows, weights, collective):
    length = rows.shape[0]
    inside = pl.BlockSpec(memory_space=pltpu.VMEM)
    outside = pl.BlockSpec(memory_space=pl.ANY)
    results = pl.pallas_call(
        attend_forward,
        out_shape=[
            jax.ShapeDtypeStruct((length, 128), jnp.bfloat16),
            jax.ShapeDtypeStruct((64, length), jnp.float32),
            jax.ShapeDtypeStruct((1, length), jnp.float32),
        ]
        + [jax.ShapeDtypeStruct((4,) + weight.shape, weight.dtype) for weight in weights],
        in_specs=[inside] + [outside] * 3,
        out_specs=[inside] * 3 + [outside] * 3,
        scratch_shapes=[
            pltpu.VMEM((length, 64), jnp.bfloat16),
            pltpu.VMEM((length, 64), jnp.bfloat16),
            pltpu.VMEM((64, length), jnp.bfloat16),
        ]
        + [pltpu.VMEM(weight.shape, weight.dtype) for weight in weights]
        + [
            pltpu.SemaphoreType.DMA((6,)),
            pltpu.SemaphoreType.DMA((3 * GATHER_COPIES,)),
            pltpu.SemaphoreType.DMA((3 * GATHER_COPIES,)),
        ],
        compiler_params=pltpu.CompilerParams(
            collective_id=collective, has_side_effects=True, vmem_limit_bytes=56 << 20
        ),
        cost_estimate=pl.CostEstimate(
            flops=2 * length * length * 64,
            bytes_accessed=length * 512 * 2,
            transcendentals=length * length // 2,
        ),
    )(rows, *weights)
    return results[0:3], results[3:6]


def run_backward(rows, grads, wide, lse, fc, down, collective):
    length = rows.shape[0]
    inside = pl.BlockSpec(memory_space=pltpu.VMEM)
    outside = pl.BlockSpec(memory_space=pl.ANY)
    received = [
        jax.ShapeDtypeStruct((3, 2, 2) + part.shape[2:], part.dtype)
        for part in (fc, down, fc, down)
    ]
    results = pl.pallas_call(
        attend_backward,
        out_shape=[jax.ShapeDtypeStruct((length, 256), jnp.bfloat16)] + received,
        in_specs=[inside] * 4 + [outside] * 2,
        out_specs=[inside] + [outside] * 4,
        scratch_shapes=[
            pltpu.VMEM((length, 64), jnp.bfloat16),
            pltpu.VMEM((length, 64), jnp.bfloat16),
            pltpu.VMEM((64, length), jnp.bfloat16),
            pltpu.VMEM((length, 64), jnp.bfloat16),
            pltpu.VMEM((length, 64), jnp.bfloat16),
            pltpu.VMEM((64, length), jnp.float32),
            pltpu.VMEM((1, length), jnp.float32),
            pltpu.SemaphoreType.DMA((12,)),
            pltpu.SemaphoreType.DMA((12,)),
        ],
        compiler_params=pltpu.CompilerParams(
            collective_id=collective, has_side_effects=True, vmem_limit_bytes=40 << 20
        ),
        cost_estimate=pl.CostEstimate(
            flops=5 * length * length * 64,
            bytes_accessed=length * 512 * 3,
            transcendentals=length * length // 2,
        ),
    )(rows, grads, wide, lse, fc, down)
    return results[0], results[1:3], results[3:5]


UNITS = 17
TAIL = 896
SHAPES = ((16, 4352), (16, 4352), (64, 1088))
PIECES = ((16, 2176), (16, 2176), (32, 1088))


def places():
    ctx = lax.axis_index("ctx")
    fsdp = lax.axis_index("fsdp")
    return ctx // 8, lax.rem(ctx // 2, 4), lax.rem(ctx, 2), fsdp // 2, lax.rem(fsdp, 2)


def device_at(z, x, y_low, y_high, core):
    return (z * 8 + x * 2 + y_low, y_high * 2 + core)


def z_peer(step):
    z, x, y_low, y_high, core = places()
    return device_at(lax.rem(z + step, 4), x, y_low, y_high, core)


def x_peer(step):
    z, x, y_low, y_high, core = places()
    return device_at(z, lax.rem(x + step, 4), y_low, y_high, core)


def near_peer():
    z, x, y_low, y_high, core = places()
    return device_at(z, x, 1 - y_low, y_high, core)


def cross_peer():
    z, x, y_low, y_high, core = places()
    return device_at(z, x, 1 - y_low, 1 - y_high, core)


def far_peer():
    z, x, y_low, y_high, core = places()
    return device_at(z, x, y_low, 1 - y_high, core)


def twin_peer():
    z, x, y_low, y_high, core = places()
    return device_at(z, x, y_low, y_high, 1 - core)


def far_twin():
    z, x, y_low, y_high, core = places()
    return device_at(z, x, y_low, 1 - y_high, 1 - core)


def ring_peers():
    return [z_peer(step) for step in (1, 2, 3)] + [x_peer(step) for step in (1, 2, 3)]


def greet(peers):
    barrier = pltpu.get_barrier_semaphore()
    for peer in peers:
        pl.semaphore_signal(barrier, inc=1, device_id=peer, device_id_type=MESH)
    pl.semaphore_wait(barrier, len(peers))


class Sender:
    def __init__(self, send_sem, recv_sem):
        self.send_sem = send_sem
        self.recv_sem = recv_sem
        self.used = 0
        self.started = []

    def push(self, source, target, peer):
        copy = pltpu.make_async_remote_copy(
            src_ref=source,
            dst_ref=target,
            send_sem=self.send_sem.at[self.used],
            recv_sem=self.recv_sem.at[self.used],
            device_id=peer,
            device_id_type=MESH,
        )
        self.used += 1
        copy.start()
        self.started.append(copy)
        return copy

    def finish(self):
        for copy in self.started:
            copy.wait_send()


class Mover:
    def __init__(self, sem):
        self.sem = sem
        self.used = 0

    def move(self, source, target):
        copy = pltpu.make_async_copy(source, target, self.sem.at[self.used])
        self.used += 1
        copy.start()
        return copy


GATHER_COPIES = 35


def gather_peers():
    return ring_peers() + [near_peer(), cross_peer(), twin_peer()]


def gather_steps(sources, targets, holds, mover, sender):
    z, x, y_low, y_high, core = places()
    mine = y_high * 2 + core
    cross = (1 - y_high) * 2 + core
    count = len(sources)
    firsts = (2 * z + y_low, 8 + 2 * x + y_low, 16)
    others = (2 * z + 1 - y_low, 8 + 2 * x + 1 - y_low)
    crossed = [
        [
            sender.push(sources[at].at[unit], targets[at].at[mine, unit], cross_peer())
            for unit in others + (16,)
        ]
        for at in range(count)
    ]
    loads = [mover.move(sources[at], holds[at]) for at in range(count)]
    arrivals = [
        sender.push(sources[at], targets[at].at[mine], twin_peer()) for at in range(count)
    ]
    yield
    owns = []
    for at in range(count):
        loads[at].wait()
        owns.append(mover.move(holds[at], targets[at].at[mine]))

    def ring(at, part, unit, kept):
        piece = targets[at].at[cross, unit]
        for step in (1, 3, 2):
            peer = z_peer(step) if part == 0 else x_peer(step)
            kept.append((at, part, step, sender.push(piece, piece, peer)))

    first_ring, second_ring = [], []

    def second(at, nears):
        for part in range(2):
            nears[part].wait_recv()
            ring(at, part, others[part], second_ring)
            piece = targets[at].at[cross, others[part]]
            arrivals.append(sender.push(piece, piece, twin_peer()))

    waiting = None
    for at in range(count):
        nears = []
        for part in range(3):
            crossed[at][part].wait_recv()
            piece = targets[at].at[cross, firsts[part]]
            if part < 2:
                nears.append(sender.push(piece, piece, near_peer()))
                ring(at, part, firsts[part], first_ring)
            arrivals.append(sender.push(piece, piece, twin_peer()))
        yield
        if waiting is not None:
            second(*waiting)
        waiting = (at, nears)
    second(*waiting)
    yield
    for at in range(count):
        for kept, base in ((first_ring, y_low), (second_ring, 1 - y_low)):
            for where, part, step, copy in kept:
                if where != at:
                    continue
                copy.wait_recv()
                if part == 0:
                    unit = 2 * lax.rem(z - step + 4, 4) + base
                else:
                    unit = 8 + 2 * lax.rem(x - step + 4, 4) + base
                piece = targets[at].at[cross, unit]
                arrivals.append(sender.push(piece, piece, twin_peer()))
    for copy in arrivals:
        copy.wait_recv()
    for own in owns:
        own.wait()


def gather_kernel(source, small, target, small_out, hold, small_hold, own_sem, send_sem, recv_sem):
    z, x, y_low, y_high, core = places()
    mine = y_high * 2 + core
    mover = Mover(own_sem)
    load = mover.move(small, small_hold)
    greet(gather_peers() + [far_peer(), far_twin()])
    sender = Sender(send_sem, recv_sem)
    arrivals = [
        sender.push(small, small_out.at[mine], twin_peer()),
        sender.push(small, small_out.at[mine], far_peer()),
        sender.push(small, small_out.at[mine], far_twin()),
    ]
    load.wait()
    own = mover.move(small_hold, small_out.at[mine])
    for _ in gather_steps([source], [target], [hold], mover, sender):
        pass
    for copy in arrivals:
        copy.wait_recv()
    own.wait()
    sender.finish()


def gather_weights(part, small, collective):
    whole = [part, small]
    shapes = [jax.ShapeDtypeStruct((4,) + each.shape, each.dtype) for each in whole]
    return pl.pallas_call(
        gather_kernel,
        out_shape=shapes,
        in_specs=[pl.BlockSpec(memory_space=pl.ANY)] * 2,
        out_specs=[pl.BlockSpec(memory_space=pl.ANY)] * 2,
        scratch_shapes=[pltpu.VMEM(each.shape, each.dtype) for each in whole]
        + [
            pltpu.SemaphoreType.DMA((4,)),
            pltpu.SemaphoreType.DMA((GATHER_COPIES + 3,)),
            pltpu.SemaphoreType.DMA((GATHER_COPIES + 3,)),
        ],
        compiler_params=pltpu.CompilerParams(
            collective_id=collective, has_side_effects=True, vmem_limit_bytes=58 << 20
        ),
        cost_estimate=pl.CostEstimate(flops=0, bytes_accessed=20 << 20, transcendentals=0),
    )(*whole)


def product_kernel(cut, *refs):
    out = refs[-1]
    products = []
    for at in range(0, len(refs) - 1, 4):
        left = jnp.concatenate([refs[at][...], refs[at + 1][...]], axis=1)
        right = jnp.concatenate([refs[at + 2][...], refs[at + 3][...]], axis=0)
        products.append((left, right))
    if cut is None:
        out[...] = dot_nn(*products[0]).astype(jnp.bfloat16)
        return
    (left, right), (other_left, other_right) = products
    out[:, 0:cut] = dot_nn(left, right[:, 0:cut]).astype(jnp.bfloat16)
    shared = dot_nn(left, right[:, cut : cut + 128]) + dot_nn(other_left, other_right[:, 0:128])
    out[:, cut : cut + 128] = shared.astype(jnp.bfloat16)
    out[:, cut + 128 :] = dot_nn(other_left, other_right[:, 128:]).astype(jnp.bfloat16)


def weight_products(operands, width, cut=None):
    size = operands[0][0].shape[0]
    block = 272
    specs, flat = [], []
    for left, other_left, right, other_right in operands:
        specs += [pl.BlockSpec((block, left.shape[1]), lambda step: (step, 0))] * 2
        specs += [pl.BlockSpec(right.shape, lambda step: (0, 0))] * 2
        flat += [left, other_left, right, other_right]
    terms = pl.pallas_call(
        functools.partial(product_kernel, cut),
        grid=(size // block,),
        out_shape=jax.ShapeDtypeStruct((size, width), jnp.bfloat16),
        in_specs=specs,
        out_specs=pl.BlockSpec((block, width), lambda step: (step, 0)),
        compiler_params=pltpu.CompilerParams(vmem_limit_bytes=40 << 20),
        cost_estimate=pl.CostEstimate(
            flops=512 * size * width, bytes_accessed=2 * size * width, transcendentals=0
        ),
    )(*flat)
    return terms.reshape(2, UNITS, size // (2 * UNITS), width)


def push_rings(sender, terms, by_z, by_x):
    z, x, y_low, y_high, core = places()
    copies = []
    for step in (2, 1, 3):
        to_z, to_x = lax.rem(z + step, 4), lax.rem(x + step, 4)
        copies.append(
            sender.push(terms.at[:, pl.ds(2 * to_z, 2)], by_z.at[step - 1], z_peer(step))
        )
        copies.append(
            sender.push(terms.at[:, pl.ds(8 + 2 * to_x, 2)], by_x.at[step - 1], x_peer(step))
        )
    return copies


def widen(values):
    return values.astype(jnp.float32)


def halves(values, group):
    if group == 2:
        return values[0:32], values[32:64]
    return values[:, 0:2176], values[:, 2176:4352]


LAST_COPIES = 6 + 3 * (6 + 3 + 6 + 6 + 18) + 3 + 3 + 3 + 3 + 3 + 9


def last_kernel(*refs):
    terms, tail = refs[0:3], refs[3]
    far_z, far_x = (None,) + refs[4:6], (None,) + refs[6:8]
    totals, small_out = refs[8:11], refs[11]
    scratch = refs[12:]
    own, by, parted, met, merged, landed, summed = [
        scratch[3 * at : 3 * at + 3] for at in range(7)
    ]
    own_t, by_t, parted_t, met_t, merged_t, landed_t, summed_t, whole_t = scratch[21:29]
    units, small_unit = scratch[29:32], scratch[32]
    own_sem, send_sem, recv_sem = scratch[33:36]
    z, x, y_low, y_high, core = places()
    mover = Mover(own_sem)
    order = (2, 1, 0)
    loads = {}
    for group in order:
        loads[group] = [
            mover.move(terms[group].at[:, pl.ds(2 * z, 2)], own[group].at[0]),
            mover.move(terms[group].at[:, pl.ds(8 + 2 * x, 2)], own[group].at[1]),
        ]
        if group > 0:
            loads[group].append(mover.move(far_z[group], by[group].at[0]))
            loads[group].append(mover.move(far_x[group], by[group].at[1]))
    load_tail = mover.move(tail.at[:, z], own_t)
    greet(ring_peers() + [near_peer(), cross_peer(), far_peer()])
    sender = Sender(send_sem, recv_sem)
    first = push_rings(sender, terms[0], by[0].at[0], by[0].at[1])
    first_t = [
        sender.push(tail.at[:, lax.rem(z + step, 4)], by_t.at[step - 1], z_peer(step))
        for step in (2, 1, 3)
    ]

    second = {}
    for group in order:
        for load in loads[group]:
            load.wait()
        if group == 0:
            for copy in first:
                copy.wait_recv()
        second[group] = []
        for ring in range(2):
            for unit in range(2):
                for side in range(2):
                    total = widen(own[group][ring, side, unit])
                    for step in range(3):
                        total = total + widen(by[group][ring, step, side, unit])
                    pair = halves(total.astype(jnp.bfloat16), group)
                    parted[group][ring, 2 * unit, side] = pair[0]
                    parted[group][ring, 2 * unit + 1, side] = pair[1]
            for step in (2, 1, 3):
                place = lax.rem(x + step, 4) if ring == 0 else lax.rem(z + step, 4)
                peer = x_peer(step) if ring == 0 else z_peer(step)
                second[group].append(
                    sender.push(
                        parted[group].at[ring, place], met[group].at[ring, step - 1], peer
                    )
                )
    load_tail.wait()
    for copy in first_t:
        copy.wait_recv()
    for place in range(4):
        total = widen(own_t[:, place])
        for step in range(3):
            total = total + widen(by_t[step, :, place])
        parted_t[place] = total.astype(jnp.bfloat16)
    second_t = [
        sender.push(parted_t.at[lax.rem(x + step, 4)], met_t.at[step - 1], x_peer(step))
        for step in (2, 1, 3)
    ]

    def across(source, target):
        return [
            sender.push(source.at[0], target.at[0], near_peer()),
            sender.push(source.at[1], target.at[1], cross_peer()),
            sender.push(source.at[1], target.at[2], far_peer()),
        ]

    third = {}
    for group in order:
        for copy in second[group]:
            copy.wait_recv()
        for ring in range(2):
            total = widen(parted[group][ring, x if ring == 0 else z])
            for step in range(3):
                total = total + widen(met[group][ring, step])
            merged[group][:, ring] = total.astype(jnp.bfloat16)
        third[group] = across(merged[group], landed[group])
    for copy in second_t:
        copy.wait_recv()
    total = widen(parted_t[x])
    for step in range(3):
        total = total + widen(met_t[step])
    merged_t[...] = total.astype(jnp.bfloat16)
    third_t = across(merged_t, landed_t)

    def spot(group, ring, at_z, at_x):
        unit = 2 * at_z + at_x // 2 if ring == 0 else 8 + 2 * at_x + at_z // 2
        half = lax.rem(at_x, 2) if ring == 0 else lax.rem(at_z, 2)
        if group == 2:
            return totals[group].at[unit, pl.ds(pl.multiple_of(half * 32, 32), 32)]
        return totals[group].at[unit, :, pl.ds(pl.multiple_of(half * 2176, 128), 2176)]

    passed, ends, owns = [], [], []
    for group in order:
        for copy in third[group]:
            copy.wait_recv()
        near = widen(merged[group][0]) + widen(landed[group][0])
        away = widen(landed[group][1]) + widen(landed[group][2])
        summed[group][...] = (near + away).astype(jnp.bfloat16)
        for ring in range(2):
            place = spot(group, ring, z, x)
            piece = summed[group].at[ring]
            owns.append(mover.move(piece, place))
            for step in (1, 3, 2):
                peer = x_peer(step) if ring == 0 else z_peer(step)
                passed.append((group, ring, step, sender.push(piece, place, peer)))
            for step in (1, 3, 2):
                peer = z_peer(step) if ring == 0 else x_peer(step)
                ends.append(sender.push(piece, place, peer))
    for copy in third_t:
        copy.wait_recv()
    near = widen(merged_t[0]) + widen(landed_t[0])
    away = widen(landed_t[1]) + widen(landed_t[2])
    summed_t[...] = (near + away).astype(jnp.bfloat16)
    owns.append(mover.move(summed_t, whole_t.at[z, x]))
    for step in (1, 3, 2):
        passed.append((3, 0, step, sender.push(summed_t, whole_t.at[z, x], x_peer(step))))
    for step in (1, 3, 2):
        ends.append(sender.push(summed_t, whole_t.at[z, x], z_peer(step)))

    for group, ring, step, copy in passed:
        copy.wait_recv()
        if group == 3:
            place = whole_t.at[z, lax.rem(x - step + 4, 4)]
        elif ring == 0:
            place = spot(group, ring, z, lax.rem(x - step + 4, 4))
        else:
            place = spot(group, ring, lax.rem(z - step + 4, 4), x)
        for other in (1, 3, 2):
            peer = z_peer(other) if ring == 0 else x_peer(other)
            ends.append(sender.push(place, place, peer))
    for copy in ends:
        copy.wait_recv()
    for copy in owns:
        copy.wait()

    def tile(at):
        return whole_t[at // 28, at // 7 % 4, :, 128 * (at % 7) : 128 * (at % 7 + 1)]

    for at in range(34):
        units[0][:, 128 * at : 128 * (at + 1)] = tile(at)
        units[1][:, 128 * at : 128 * (at + 1)] = tile(34 + at)
    for row in range(4):
        for at in range(9):
            width = min(128, 1088 - 128 * at)
            units[2][16 * row : 16 * row + 16, 128 * at : 128 * at + width] = tile(
                68 + 9 * row + at
            )[:, :width]
    for at in range(8):
        small_unit[:, 128 * at : 128 * (at + 1)] = tile(104 + at)
    lasts = [mover.move(units[group], totals[group].at[16]) for group in range(3)]
    lasts.append(mover.move(small_unit, small_out))
    for copy in lasts:
        copy.wait()
    sender.finish()


def last_exchange(terms, tail, far_z, far_x, collective):
    low = jnp.bfloat16

    def each(make):
        return [pltpu.VMEM(make(*pair), low) for pair in zip(SHAPES, PIECES)]

    scratch = (
        each(lambda unit, piece: (2, 2, 2) + unit)
        + each(lambda unit, piece: (2, 3, 2, 2) + unit)
        + each(lambda unit, piece: (2, 4, 2) + piece)
        + each(lambda unit, piece: (2, 3, 2) + piece)
        + each(lambda unit, piece: (2, 2) + piece)
        + each(lambda unit, piece: (3, 2) + piece)
        + each(lambda unit, piece: (2,) + piece)
        + [
            pltpu.VMEM((2, 4, 16, TAIL), low),
            pltpu.VMEM((3, 2, 4, 16, TAIL), low),
            pltpu.VMEM((4, 2, 16, TAIL), low),
            pltpu.VMEM((3, 2, 16, TAIL), low),
            pltpu.VMEM((2, 16, TAIL), low),
            pltpu.VMEM((3, 16, TAIL), low),
            pltpu.VMEM((16, TAIL), low),
            pltpu.VMEM((4, 4, 16, TAIL), low),
        ]
        + each(lambda unit, piece: unit)
        + [
            pltpu.VMEM((16, 1024), low),
            pltpu.SemaphoreType.DMA((24,)),
            pltpu.SemaphoreType.DMA((LAST_COPIES,)),
            pltpu.SemaphoreType.DMA((LAST_COPIES,)),
        ]
    )
    return pl.pallas_call(
        last_kernel,
        out_shape=[jax.ShapeDtypeStruct((UNITS,) + unit, low) for unit in SHAPES]
        + [jax.ShapeDtypeStruct((16, 1024), low)],
        in_specs=[pl.BlockSpec(memory_space=pl.ANY)] * 8,
        out_specs=[pl.BlockSpec(memory_space=pl.ANY)] * 4,
        scratch_shapes=scratch,
        compiler_params=pltpu.CompilerParams(
            collective_id=collective, has_side_effects=True, vmem_limit_bytes=48 << 20
        ),
        cost_estimate=pl.CostEstimate(flops=0, bytes_accessed=40 << 20, transcendentals=0),
    )(*terms, tail, *far_z, *far_x)


def reduce_grads(terms, small, far_z, far_x, collective):
    down = terms[2][:, 16].reshape(2, 4, 16, 1088)
    down = jnp.pad(down, ((0, 0), (0, 0), (0, 0), (0, 64)))
    down = jnp.transpose(down, (0, 2, 1, 3)).reshape(2, 16, 4608)
    extra = jnp.pad(small, ((0, 0), (0, 16 * 1024 - small.shape[1]))).reshape(2, 16, 1024)
    tail = jnp.concatenate(
        [terms[0][:, 16], terms[1][:, 16], down, extra.astype(jnp.bfloat16)], axis=-1
    )
    tail = jnp.transpose(tail.reshape(2, 16, 4, 4, TAIL), (0, 2, 3, 1, 4))
    joint, fc, down, small = last_exchange(terms, tail, far_z, far_x, collective)
    joint = joint.reshape(272, 4352)
    outs = (
        joint[:, :3264].astype(jnp.float32),
        joint[:, 3264:].astype(jnp.float32),
        fc.reshape(272, 4352).astype(jnp.float32),
        down.reshape(1088, 1088).astype(jnp.float32),
    )
    return outs, small.reshape(-1)[:3264].astype(jnp.float32)


def mean_rows(values):
    return jnp.sum(values, axis=-1, keepdims=True) * (1.0 / values.shape[-1])


def normal_rows(values):
    centre = values - mean_rows(values)
    scale = lax.rsqrt(mean_rows(centre * centre) + 1e-05)
    return centre * scale, scale


def norm_back(grads, gain, unit, scale):
    scaled = grads * gain
    return scale * (scaled - mean_rows(scaled) - unit * mean_rows(scaled * unit))


def column_sums(values):
    return jnp.sum(values, axis=0, keepdims=True)


def turned(values):
    rows, width = values.shape
    full = jnp.concatenate([values, jnp.zeros((rows, 1152 - width), values.dtype)], axis=1)
    return full.T[0:width, :]


def before_kernel(tokens, gain, offset, weight, bias, packed, turned_ref, joint):
    unit, _ = normal_rows(widen(tokens[...]))
    normed = (unit * widen(gain[...]) + widen(offset[...])).astype(jnp.bfloat16)
    turned_ref[...] = turned(normed)
    joint[...] = (dot_nn(normed, weight[...]) + widen(bias[...])).astype(jnp.bfloat16)
    blank = jnp.zeros((joint.shape[0], HEAD_DIM), jnp.bfloat16)
    for head in range(HEADS):
        parts = [
            joint[:, 1088 * part + 64 * head : 1088 * part + 64 * head + 64] for part in range(3)
        ]
        packed[head] = jnp.concatenate(parts + [blank], axis=1)


def run_before(tokens, gain, offset, weight, bias):
    rows = tokens.shape[0]
    return pl.pallas_call(
        before_kernel,
        out_shape=(
            jax.ShapeDtypeStruct((HEADS, rows, 256), jnp.bfloat16),
            jax.ShapeDtypeStruct((1088, rows), jnp.bfloat16),
        ),
        scratch_shapes=[pltpu.VMEM((rows, 3264), jnp.bfloat16)],
        compiler_params=pltpu.CompilerParams(vmem_limit_bytes=40 << 20),
        cost_estimate=pl.CostEstimate(
            flops=2 * rows * 1088 * 3264, bytes_accessed=8 << 20, transcendentals=0
        ),
    )(tokens, gain, offset, weight, bias)


def middle_kernel(
    heads,
    tokens,
    cotangent,
    w_out,
    b_out,
    gain,
    offset,
    b_down,
    fc,
    b_fc,
    down,
    result,
    grad_middle,
    grad_heads,
    attended_t,
    normed_t,
    grad_branch,
    active_t,
    grad_hidden,
    d_fc,
    sums,
    attended,
    normed,
    unit,
    scale,
    total,
    grads,
):
    at = pl.program_id(0)

    @pl.when(at == 0)
    def _():
        for head in range(HEADS):
            attended[:, 64 * head : 64 * head + 64] = heads[head, :, 0:64]
        attended_t[...] = turned(attended[...])
        middle = widen(tokens[...]) + (dot_nn(attended[...], w_out[...]) + widen(b_out[...]))
        unit[...], scale[...] = normal_rows(middle)
        normed[...] = (unit[...] * widen(gain[...]) + widen(offset[...])).astype(jnp.bfloat16)
        normed_t[...] = turned(normed[...])
        total[...] = middle + widen(b_down[...])
        grads[...] = jnp.zeros_like(grads)

    hidden = dot_nn(normed[...], fc[...]) + widen(b_fc[...])
    square = hidden * hidden
    bend = jnp.tanh(0.7978845608028654 * (hidden + 0.044715 * square * hidden))
    active = (0.5 * hidden * (1.0 + bend)).astype(jnp.bfloat16)
    slope = 0.5 * (1.0 + bend) + 0.5 * hidden * (1.0 - bend * bend) * (
        0.7978845608028654 * (1.0 + 3.0 * 0.044715 * square)
    )
    back = (dot_nt(cotangent[...], down[...]) * slope).astype(jnp.bfloat16)
    active_t[...] = active.T
    grad_hidden[...] = back
    d_fc[...] = column_sums(widen(back))
    total[...] += dot_nn(active, down[...])
    grads[...] += dot_nt(back, fc[...])

    @pl.when(at == pl.num_programs(0) - 1)
    def _():
        result[...] = total[...].astype(jnp.bfloat16)
        arrived = widen(cotangent[...])
        whole = grads[...]
        grad = arrived + norm_back(whole, widen(gain[...]), unit[...], scale[...])
        grad_middle[...] = grad
        low = grad.astype(jnp.bfloat16)
        grad_branch[:, 0:64] = jnp.zeros((low.shape[0], 64), jnp.bfloat16)
        grad_branch[:, 64:1152] = low
        sums[0:1, :] = column_sums(widen(low))
        sums[1:2, :] = column_sums(whole * unit[...])
        sums[2:3, :] = column_sums(whole)
        sums[3:4, :] = column_sums(arrived)
        attended[...] = dot_nt(low, w_out[...]).astype(jnp.bfloat16)
        blank = jnp.zeros((low.shape[0], HEAD_DIM), jnp.bfloat16)
        for head in range(HEADS):
            piece = attended[:, 64 * head : 64 * head + 64]
            grad_heads[head] = jnp.concatenate([piece, blank], axis=1)


def run_middle(heads, tokens, cotangent, w_out, b_out, gain, offset, b_down, fc, b_fc, down):
    rows = tokens.shape[0]
    low, wide = jnp.bfloat16, jnp.float32
    block = 256

    def fixed(shape):
        return pl.BlockSpec(shape, lambda step: (0,) * len(shape))

    vector = fixed((1, 1088))
    square = fixed((rows, 1088))
    across = pl.BlockSpec((rows, block), lambda step: (0, step))
    line = pl.BlockSpec((1, block), lambda step: (0, step))
    return pl.pallas_call(
        middle_kernel,
        grid=(4352 // block,),
        in_specs=[
            fixed((HEADS, rows, 128)),
            square,
            square,
            fixed((1088, 1088)),
            vector,
            vector,
            vector,
            vector,
            pl.BlockSpec((1088, block), lambda step: (0, step)),
            line,
            pl.BlockSpec((block, 1088), lambda step: (step, 0)),
        ],
        out_specs=[
            square,
            square,
            fixed((HEADS, rows, 128)),
            fixed((1088, rows)),
            fixed((1088, rows)),
            fixed((rows, 1152)),
            pl.BlockSpec((block, rows), lambda step: (step, 0)),
            across,
            line,
            fixed((4, 1088)),
        ],
        out_shape=[
            jax.ShapeDtypeStruct((rows, 1088), low),
            jax.ShapeDtypeStruct((rows, 1088), wide),
            jax.ShapeDtypeStruct((HEADS, rows, 128), low),
            jax.ShapeDtypeStruct((1088, rows), low),
            jax.ShapeDtypeStruct((1088, rows), low),
            jax.ShapeDtypeStruct((rows, 1152), low),
            jax.ShapeDtypeStruct((4352, rows), low),
            jax.ShapeDtypeStruct((rows, 4352), low),
            jax.ShapeDtypeStruct((1, 4352), wide),
            jax.ShapeDtypeStruct((4, 1088), wide),
        ],
        scratch_shapes=[
            pltpu.VMEM((rows, 1088), low),
            pltpu.VMEM((rows, 1088), low),
            pltpu.VMEM((rows, 1088), wide),
            pltpu.VMEM((rows, 1), wide),
            pltpu.VMEM((rows, 1088), wide),
            pltpu.VMEM((rows, 1088), wide),
        ],
        compiler_params=pltpu.CompilerParams(vmem_limit_bytes=48 << 20),
        cost_estimate=pl.CostEstimate(
            flops=8 * rows * 1088 * 4352, bytes_accessed=24 << 20, transcendentals=rows * 4352
        ),
    )(heads, tokens, cotangent, w_out, b_out, gain, offset, b_down, fc, b_fc, down)


def after_kernel(packed, weight, tokens, gain, grad_middle, joint, grad_tokens, sums, line):
    for head in range(HEADS):
        for part in range(3):
            start = 1088 * part + 64 * head
            joint[:, start : start + 64] = packed[head, :, 64 * part : 64 * part + 64]
    joint[:, 3264:3328] = jnp.zeros((joint.shape[0], 64), jnp.bfloat16)
    unit, scale = normal_rows(widen(tokens[...]))
    grads = dot_nt(joint[:, 0:3264], weight[...])
    back = norm_back(grads, widen(gain[...]), unit, scale)
    grad_tokens[...] = grad_middle[...] + back
    sums[0:1, :] = column_sums(grads * unit)
    sums[1:2, :] = column_sums(grads)
    line[...] = column_sums(widen(joint[:, 0:3264]))


def run_after(packed, weight, tokens, gain, grad_middle):
    rows = tokens.shape[0]
    return pl.pallas_call(
        after_kernel,
        out_shape=(
            jax.ShapeDtypeStruct((rows, 3328), jnp.bfloat16),
            jax.ShapeDtypeStruct((rows, 1088), jnp.float32),
            jax.ShapeDtypeStruct((2, 1088), jnp.float32),
            jax.ShapeDtypeStruct((1, 3264), jnp.float32),
        ),
        compiler_params=pltpu.CompilerParams(vmem_limit_bytes=40 << 20),
        cost_estimate=pl.CostEstimate(
            flops=2 * rows * 1088 * 3264, bytes_accessed=10 << 20, transcendentals=0
        ),
    )(packed, weight, tokens, gain, grad_middle)


def local(
    tokens,
    cotangent,
    ln1_scale,
    ln1_bias,
    w_qkv,
    bias_q,
    bias_v,
    w_out,
    bias_out,
    ln2_scale,
    ln2_bias,
    w_fc,
    bias_fc,
    w_down,
    bias_down,
):
    ctx_count = lax.axis_size("ctx")
    vectors = (
        ln1_scale,
        ln1_bias,
        bias_q,
        bias_v,
        bias_out,
        ln2_scale,
        ln2_bias,
        bias_down,
        bias_fc,
    )
    small = jnp.concatenate(
        [jnp.stack(vectors[:8]), bias_fc.reshape(4, 272), jnp.zeros((4, 272), jnp.bfloat16)]
    )
    own_parts = [
        part.reshape(UNITS, part.shape[0] // UNITS, part.shape[1])
        for part in (w_qkv, w_out, w_fc, w_down)
    ]
    full_qkv, full_small = gather_weights(own_parts[0], small, 5)
    full_qkv = full_qkv.reshape(1088, 3264)
    lines = [full_small[:, at].reshape(1, 1088) for at in range(8)]
    (line_scale1, line_shift1, line_bq, line_bv, line_bout, line_scale2, line_shift2) = lines[:7]
    line_bdown = lines[7]
    line_bfc = full_small[:, 8:12].reshape(1, 4352)
    z, x, y_low, y_high, core = places()

    def swap(values):
        return lax.ppermute(values, "fsdp", [(0, 1), (1, 0), (2, 3), (3, 2)])

    def split(quarters):
        first, second = quarters[:, 0], quarters[:, 1]
        keep = jnp.where(core == 0, first, second)
        give = jnp.where(core == 0, second, first)
        keep = jnp.where(y_high == 0, keep, keep[::-1])
        give = jnp.where(y_high == 0, give, give[::-1])
        return keep, give

    def products(left, right):
        width, rows = left.shape
        keep, give = split(left.reshape(2, 2, width // 4, rows))
        keep, give = keep.reshape(width // 2, rows), give.reshape(width // 2, rows)
        return keep, swap(give), right, swap(right)

    bias_joint = jnp.concatenate([line_bq, jnp.zeros_like(line_bq), line_bv], axis=1)
    packed, normed_t = run_before(tokens[0], line_scale1, line_shift1, full_qkv, bias_joint)
    head_rows = spread_heads(packed, ctx_count, 1)
    (out_rows, wide_out, lse_rows), (full_out, full_fc, full_down) = run_forward(
        head_rows, own_parts[1:], 8
    )
    full_out = full_out.reshape(1088, 1088)
    full_fc = full_fc.reshape(1088, 4352)
    full_down = full_down.reshape(4352, 1088)
    (
        result,
        grad_middle,
        grad_heads,
        attended_t,
        normed2_t,
        grad_branch,
        active_t,
        grad_hidden,
        line_fc,
        sums_middle,
    ) = run_middle(
        collect_heads(out_rows, ctx_count, 2),
        tokens[0],
        cotangent[0],
        full_out,
        line_bout,
        line_scale2,
        line_shift2,
        line_bdown,
        full_fc,
        line_bfc,
        full_down,
    )
    d_down = weight_products([products(active_t, cotangent[0])], 1088)
    d_fc = weight_products([products(normed2_t, grad_hidden)], 4352)
    out_products = products(attended_t, grad_branch)
    grad_rows = spread_heads(grad_heads, ctx_count, 3)
    joint_rows_grad, far_z, far_x = run_backward(
        head_rows, grad_rows, wide_out, lse_rows, d_fc, d_down, 7
    )
    packed_grads = collect_heads(joint_rows_grad, ctx_count, 4)
    grad_joint, grad_inputs, sums_after, line_joint = run_after(
        packed_grads, full_qkv, tokens[0], line_scale1, grad_middle
    )
    d_joint = weight_products([products(normed_t, grad_joint), out_products], 4352, 3200)
    d_bout, d_scale2, d_shift2, d_bdown = [sums_middle[at] for at in range(4)]
    d_scale1, d_shift1 = sums_after[0], sums_after[1]
    d_bq, d_bv, d_bfc = line_joint[0, :1088], line_joint[0, 2176:], line_fc[0]
    narrow = (d_scale1, d_shift1, d_bq, d_bv, d_bout, d_scale2, d_shift2, d_bdown, d_bfc)
    sums = jnp.concatenate([vector.reshape(4, -1) for vector in narrow], axis=1)
    keep, give = split(sums.reshape(2, 2, 3264))
    sums = keep + swap(give)
    (t_qkv, t_out, t_fc, t_down), extras = reduce_grads(
        (d_joint, d_fc, d_down), sums, far_z, far_x, 6
    )
    (t_scale1, t_shift1, t_bq, t_bv, t_bout, t_scale2, t_shift2, t_bdown) = [
        extras[at * 272 : (at + 1) * 272] for at in range(8)
    ]
    t_bfc = extras[2176:]
    return (
        result[None],
        grad_inputs[None],
        t_scale1,
        t_shift1,
        t_qkv,
        t_bq,
        t_bv,
        t_out,
        t_bout,
        t_scale2,
        t_shift2,
        t_fc,
        t_bfc,
        t_down,
        t_bdown,
    )


def solution(mesh):
    placed = (
        P("fsdp", "ctx", None),
        P("fsdp", "ctx", None),
        P("fsdp"),
        P("fsdp"),
        P("fsdp", None),
        P("fsdp"),
        P("fsdp"),
        P("fsdp", None),
        P("fsdp"),
        P("fsdp"),
        P("fsdp"),
        P("fsdp", None),
        P("fsdp"),
        P("fsdp", None),
        P("fsdp"),
    )
    return jax.shard_map(
        local,
        mesh=mesh,
        in_specs=placed,
        out_specs=(
            P("fsdp", "ctx", None),
            P("fsdp", "ctx", None),
            P("fsdp"),
            P("fsdp"),
            P("fsdp", None),
            P("fsdp"),
            P("fsdp"),
            P("fsdp", None),
            P("fsdp"),
            P("fsdp"),
            P("fsdp"),
            P("fsdp", None),
            P("fsdp"),
            P("fsdp", None),
            P("fsdp"),
        ),
        check_vma=False,
    )
```

```python
import functools

import jax
import jax.numpy as jnp
from jax import lax
from jax.experimental import pallas as pl
from jax.experimental.pallas import tpu as pltpu
from jax.sharding import PartitionSpec as P

MESH = pl.DeviceIdType.MESH
HEAD_DIM = 64
HEADS = 17
BLOCK = 64
STEP = 512


def head_place(head, core):
    return jnp.where(head < 16, 2 * head + core, 1 - core)


def held_head(place, core):
    own = lax.rem(place, 2) == core
    head = jnp.where(own, place // 2, 16)
    return own | (place == 1 - core), head


def greet_ctx(me, count):
    barrier = pltpu.get_barrier_semaphore()

    def greet(step, carry):
        pl.semaphore_signal(
            barrier, inc=1, device_id={"ctx": lax.rem(me + step, count)}, device_id_type=MESH
        )
        return carry

    lax.fori_loop(1, count, greet, 0)
    pl.semaphore_wait(barrier, count - 1)


def spread_kernel(count, x_ref, out_ref, send_sem, recv_sem, own_sem):
    me = lax.axis_index("ctx")
    core = lax.rem(lax.axis_index("fsdp"), 2)
    has, _ = held_head(me, core)
    greet_ctx(me, count)

    def remote(head, source):
        return pltpu.make_async_remote_copy(
            src_ref=x_ref.at[head],
            dst_ref=out_ref.at[source],
            send_sem=send_sem.at[head],
            recv_sem=recv_sem.at[source],
            device_id={"ctx": head_place(head, core)},
            device_id_type=MESH,
        )

    def own(head):
        return pltpu.make_async_copy(x_ref.at[head], out_ref.at[me], own_sem.at[0])

    def send(head, carry):
        target = head_place(head, core)

        @pl.when(target != me)
        def _():
            remote(head, me).start()

        @pl.when(target == me)
        def _():
            own(head).start()

        return carry

    lax.fori_loop(0, HEADS, send, 0)

    def sent(head, carry):
        target = head_place(head, core)

        @pl.when(target != me)
        def _():
            remote(head, me).wait_send()

        @pl.when(target == me)
        def _():
            own(head).wait()

        return carry

    lax.fori_loop(0, HEADS, sent, 0)

    @pl.when(has)
    def _():
        def arrived(source, carry):
            @pl.when(source != me)
            def _():
                remote(0, source).wait_recv()

            return carry

        lax.fori_loop(0, count, arrived, 0)


def collect_kernel(count, y_ref, out_ref, send_sem, recv_sem, own_sem):
    me = lax.axis_index("ctx")
    core = lax.rem(lax.axis_index("fsdp"), 2)
    has, mine = held_head(me, core)
    greet_ctx(me, count)

    def remote(head, target):
        return pltpu.make_async_remote_copy(
            src_ref=y_ref.at[target],
            dst_ref=out_ref.at[head],
            send_sem=send_sem.at[target],
            recv_sem=recv_sem.at[head],
            device_id={"ctx": target},
            device_id_type=MESH,
        )

    @pl.when(has)
    def _():
        def send(step, carry):
            remote(mine, lax.rem(me + 11 * step, count)).start()
            return carry

        lax.fori_loop(1, count, send, 0)
        own = pltpu.make_async_copy(y_ref.at[me], out_ref.at[mine], own_sem.at[0])
        own.start()

        def sent(step, carry):
            remote(mine, lax.rem(me + 11 * step, count)).wait_send()
            return carry

        lax.fori_loop(1, count, sent, 0)
        own.wait()

    def arrived(head, carry):
        @pl.when(head_place(head, core) != me)
        def _():
            remote(head, 0).wait_recv()

        return carry

    lax.fori_loop(0, HEADS, arrived, 0)


def spread_heads(packed, count, collective):
    return pl.pallas_call(
        functools.partial(spread_kernel, count),
        out_shape=jax.ShapeDtypeStruct((count,) + packed.shape[1:], packed.dtype),
        in_specs=[pl.BlockSpec(memory_space=pltpu.VMEM)],
        out_specs=pl.BlockSpec(memory_space=pltpu.VMEM),
        scratch_shapes=[
            pltpu.SemaphoreType.DMA((HEADS,)),
            pltpu.SemaphoreType.DMA((count,)),
            pltpu.SemaphoreType.DMA((1,)),
        ],
        compiler_params=pltpu.CompilerParams(
            collective_id=collective, has_side_effects=True, vmem_limit_bytes=24 << 20
        ),
        cost_estimate=pl.CostEstimate(flops=0, bytes_accessed=4 << 20, transcendentals=0),
    )(packed)


def collect_heads(pieces, count, collective):
    return pl.pallas_call(
        functools.partial(collect_kernel, count),
        out_shape=jax.ShapeDtypeStruct((HEADS,) + pieces.shape[1:], pieces.dtype),
        in_specs=[pl.BlockSpec(memory_space=pltpu.VMEM)],
        out_specs=pl.BlockSpec(memory_space=pltpu.VMEM),
        scratch_shapes=[
            pltpu.SemaphoreType.DMA((count,)),
            pltpu.SemaphoreType.DMA((HEADS,)),
            pltpu.SemaphoreType.DMA((1,)),
        ],
        compiler_params=pltpu.CompilerParams(
            collective_id=collective, has_side_effects=True, vmem_limit_bytes=24 << 20
        ),
        cost_estimate=pl.CostEstimate(flops=0, bytes_accessed=4 << 20, transcendentals=0),
    )(pieces)


TILES = 32


def tile_span(at):
    return pl.ds(pl.multiple_of(at * 128, 128), 128)


def each_tile(visit):
    def low(at, carry):
        visit(at, 2 * at, 2 * at + 1, 0)
        return carry

    def high(at, carry):
        visit(TILES // 2 + at, TILES - 1 - 2 * at, TILES - 2 - 2 * at, 64)
        return carry

    lax.fori_loop(0, TILES // 2, low, 0)
    lax.fori_loop(0, TILES // 2, high, 0)


def take_tile(ref, first, second, lane):
    return jnp.concatenate(
        [ref[first, :, lane : lane + 64], ref[second, :, lane : lane + 64]], axis=1
    )


def put_tile(ref, first, second, lane, tile):
    ref[first, :, lane : lane + 64] = tile[:, 0:64]
    ref[second, :, lane : lane + 64] = tile[:, 64:128]


def dot_nt(left, right):
    return lax.dot_general(
        left, right, (((1,), (1,)), ((), ())), preferred_element_type=jnp.float32
    )


def dot_nn(left, right):
    return jnp.dot(left, right, preferred_element_type=jnp.float32)


def causal(scores):
    keys = lax.broadcasted_iota(jnp.int32, scores.shape, 0)
    asks = lax.broadcasted_iota(jnp.int32, scores.shape, 1)
    return keys <= asks


def attend_forward(*refs):
    x_ref, sources = refs[0], refs[1:4]
    out_ref, wide_ref, lse_ref = refs[4:7]
    targets = refs[7:10]
    q_ref, k_ref, vt_ref = refs[10:13]
    holds = refs[13:16]
    own_sem, send_sem, recv_sem = refs[16:19]
    has, _ = held_head(lax.axis_index("ctx"), lax.rem(lax.axis_index("fsdp"), 2))
    blocks = lse_ref.shape[1] // STEP
    greet(gather_peers())
    sender = Sender(send_sem, recv_sem)
    steps = gather_steps(sources, targets, holds, Mover(own_sem), sender)
    next(steps)

    @pl.when(has)
    def _():
        def prepare(at, first, second, lane):
            tile = take_tile(x_ref, first, second, lane)
            q_ref[:, tile_span(at)] = tile[0:64] * jnp.bfloat16(0.125)
            k_ref[tile_span(at), :] = tile[64:192].T[:, 0:64]
            vt_ref[:, tile_span(at)] = tile[128:192]

        each_tile(prepare)

    def one_block(at):
        asks = pl.ds(at * STEP, STEP)
        query = q_ref[:, asks]

        def update(state, place, masked):
            top, total, accum = state
            keys = pl.ds(pl.multiple_of(place * STEP, STEP), STEP)
            scores = dot_nn(k_ref[keys, :], query)
            if masked:
                scores = jnp.where(causal(scores), scores, -1e30)
            new_top = jnp.maximum(top, jnp.max(scores, axis=0, keepdims=True))
            factor = jnp.exp(top - new_top)
            weights = jnp.exp(scores - new_top)
            total = total * factor + jnp.sum(weights, axis=0, keepdims=True)
            accum = accum * factor + dot_nn(vt_ref[:, keys], weights.astype(jnp.bfloat16))
            return new_top, total, accum

        state = (
            jnp.full((1, STEP), -1e30, jnp.float32),
            jnp.zeros((1, STEP), jnp.float32),
            jnp.zeros((64, STEP), jnp.float32),
        )
        state = update(state, at, True)
        state = lax.fori_loop(0, at, lambda place, held: update(held, place, False), state)
        top, total, accum = state
        result = accum / total
        wide_ref[:, asks] = result
        lse_ref[:, asks] = top + jnp.log(total)
        low = result.astype(jnp.bfloat16)
        for part in range(4):
            tile = low[:, 128 * part : 128 * part + 128]
            index = 4 * at + part
            if index < TILES // 2:
                put_tile(out_ref, 2 * index, 2 * index + 1, 0, tile)
            else:
                rest = 2 * (index - TILES // 2)
                put_tile(out_ref, TILES - 1 - rest, TILES - 2 - rest, 64, tile)

    for at in range(blocks):
        pl.when(has)(functools.partial(one_block, at))
        if at >= 3:
            next(steps, None)
    for _ in steps:
        pass
    sender.finish()


def attend_backward(
    x_ref,
    g_ref,
    wide_ref,
    lse_ref,
    fc_ref,
    down_ref,
    out_ref,
    fc_z_ref,
    down_z_ref,
    fc_x_ref,
    down_x_ref,
    q_ref,
    k_ref,
    kt_ref,
    v_ref,
    go_ref,
    dq_ref,
    delta_ref,
    grad_ref,
    send_sem,
    recv_sem,
):
    has, _ = held_head(lax.axis_index("ctx"), lax.rem(lax.axis_index("fsdp"), 2))
    blocks = lse_ref.shape[1] // STEP
    greet(ring_peers())
    sender = Sender(send_sem, recv_sem)
    push_rings(sender, down_ref, down_z_ref, down_x_ref)
    push_rings(sender, fc_ref, fc_z_ref, fc_x_ref)

    @pl.when(has)
    def _():
        blank = jnp.zeros((64, 128), jnp.bfloat16)

        def prepare(at, first, second, lane):
            span = tile_span(at)
            tile = take_tile(x_ref, first, second, lane)
            rows = jnp.concatenate([tile, blank], axis=0).T
            q_ref[span, :] = rows[:, 0:64] * jnp.bfloat16(0.125)
            k_ref[span, :] = rows[:, 64:128]
            kt_ref[:, span] = tile[64:128]
            v_ref[span, :] = rows[:, 128:192]
            grad = take_tile(g_ref, first, second, lane)
            go_ref[span, :] = jnp.concatenate([grad, blank], axis=0).T[:, 0:64]
            delta_ref[:, span] = jnp.sum(
                grad.astype(jnp.float32) * wide_ref[:, span], axis=0, keepdims=True
            )
            dq_ref[:, span] = jnp.zeros((64, 128), jnp.float32)

        each_tile(prepare)

        def one_block(place, carry):
            keys = pl.ds(pl.multiple_of(place * STEP, STEP), STEP)
            key = k_ref[keys, :]
            turned_key = kt_ref[:, keys]
            value = v_ref[keys, :]

            def update(state, at, masked):
                grad_key, grad_value = state
                asks = pl.ds(pl.multiple_of(at * STEP, STEP), STEP)
                query = q_ref[asks, :]
                grad = go_ref[asks, :]
                probs = jnp.exp(dot_nt(key, query) - lse_ref[:, asks])
                if masked:
                    probs = jnp.where(causal(probs), probs, 0.0)
                grad_probs = dot_nt(value, grad)
                grad_scores = (probs * (grad_probs - delta_ref[:, asks])).astype(jnp.bfloat16)
                grad_value = grad_value + dot_nn(probs.astype(jnp.bfloat16), grad)
                grad_key = grad_key + dot_nn(grad_scores, query)
                dq_ref[:, asks] += dot_nn(turned_key, grad_scores)
                return grad_key, grad_value

            state = (jnp.zeros((STEP, 64), jnp.float32), jnp.zeros((STEP, 64), jnp.float32))
            state = update(state, place, True)
            grad_key, grad_value = lax.fori_loop(
                place + 1, blocks, lambda at, held: update(held, at, False), state
            )
            grad_ref[64:192, keys] = (
                jnp.concatenate([grad_key, grad_value], axis=1).T.astype(jnp.bfloat16)
            )
            return carry

        lax.fori_loop(0, blocks, one_block, 0)

        def finish(at, first, second, lane):
            span = tile_span(at)
            query_part = (dq_ref[:, span] * 0.125).astype(jnp.bfloat16)
            tile = jnp.concatenate([query_part, grad_ref[64:192, span]], axis=0)
            put_tile(out_ref, first, second, lane, tile)

        each_tile(finish)

    for copy in sender.started:
        copy.wait_recv()
    sender.finish()


def run_forward(rows, weights, collective):
    length = rows.shape[0] * rows.shape[2]
    inside = pl.BlockSpec(memory_space=pltpu.VMEM)
    outside = pl.BlockSpec(memory_space=pl.ANY)
    results = pl.pallas_call(
        attend_forward,
        out_shape=[
            jax.ShapeDtypeStruct((TILES, 64, 128), jnp.bfloat16),
            jax.ShapeDtypeStruct((64, length), jnp.float32),
            jax.ShapeDtypeStruct((1, length), jnp.float32),
        ]
        + [jax.ShapeDtypeStruct((4,) + weight.shape, weight.dtype) for weight in weights],
        in_specs=[inside] + [outside] * 3,
        out_specs=[inside] * 3 + [outside] * 3,
        scratch_shapes=[
            pltpu.VMEM((64, length), jnp.bfloat16),
            pltpu.VMEM((length, 64), jnp.bfloat16),
            pltpu.VMEM((64, length), jnp.bfloat16),
        ]
        + [pltpu.VMEM(weight.shape, weight.dtype) for weight in weights]
        + [
            pltpu.SemaphoreType.DMA((6,)),
            pltpu.SemaphoreType.DMA((3 * GATHER_COPIES,)),
            pltpu.SemaphoreType.DMA((3 * GATHER_COPIES,)),
        ],
        compiler_params=pltpu.CompilerParams(
            collective_id=collective, has_side_effects=True, vmem_limit_bytes=56 << 20
        ),
        cost_estimate=pl.CostEstimate(
            flops=2 * length * length * 64,
            bytes_accessed=length * 512 * 2,
            transcendentals=length * length // 2,
        ),
    )(rows, *weights)
    return results[0:3], results[3:6]


def run_backward(rows, grads, wide, lse, fc, down, collective):
    length = rows.shape[0] * rows.shape[2]
    inside = pl.BlockSpec(memory_space=pltpu.VMEM)
    outside = pl.BlockSpec(memory_space=pl.ANY)
    received = [
        jax.ShapeDtypeStruct((3, 2, 2) + part.shape[2:], part.dtype)
        for part in (fc, down, fc, down)
    ]
    results = pl.pallas_call(
        attend_backward,
        out_shape=[jax.ShapeDtypeStruct(rows.shape, jnp.bfloat16)] + received,
        in_specs=[inside] * 4 + [outside] * 2,
        out_specs=[inside] + [outside] * 4,
        scratch_shapes=[
            pltpu.VMEM((length, 64), jnp.bfloat16),
            pltpu.VMEM((length, 64), jnp.bfloat16),
            pltpu.VMEM((64, length), jnp.bfloat16),
            pltpu.VMEM((length, 64), jnp.bfloat16),
            pltpu.VMEM((length, 64), jnp.bfloat16),
            pltpu.VMEM((64, length), jnp.float32),
            pltpu.VMEM((1, length), jnp.float32),
            pltpu.VMEM((192, length), jnp.bfloat16),
            pltpu.SemaphoreType.DMA((12,)),
            pltpu.SemaphoreType.DMA((12,)),
        ],
        compiler_params=pltpu.CompilerParams(
            collective_id=collective, has_side_effects=True, vmem_limit_bytes=58 << 20
        ),
        cost_estimate=pl.CostEstimate(
            flops=5 * length * length * 64,
            bytes_accessed=length * 512 * 3,
            transcendentals=length * length // 2,
        ),
    )(rows, grads, wide, lse, fc, down)
    return results[0], results[1:3], results[3:5]


UNITS = 17
TAIL = 896
SHAPES = ((16, 4352), (16, 4352), (64, 1088))
PIECES = ((16, 2176), (16, 2176), (32, 1088))


def places():
    ctx = lax.axis_index("ctx")
    fsdp = lax.axis_index("fsdp")
    return ctx // 8, lax.rem(ctx // 2, 4), lax.rem(ctx, 2), fsdp // 2, lax.rem(fsdp, 2)


def device_at(z, x, y_low, y_high, core):
    return (z * 8 + x * 2 + y_low, y_high * 2 + core)


def z_peer(step):
    z, x, y_low, y_high, core = places()
    return device_at(lax.rem(z + step, 4), x, y_low, y_high, core)


def x_peer(step):
    z, x, y_low, y_high, core = places()
    return device_at(z, lax.rem(x + step, 4), y_low, y_high, core)


def near_peer():
    z, x, y_low, y_high, core = places()
    return device_at(z, x, 1 - y_low, y_high, core)


def cross_peer():
    z, x, y_low, y_high, core = places()
    return device_at(z, x, 1 - y_low, 1 - y_high, core)


def far_peer():
    z, x, y_low, y_high, core = places()
    return device_at(z, x, y_low, 1 - y_high, core)


def twin_peer():
    z, x, y_low, y_high, core = places()
    return device_at(z, x, y_low, y_high, 1 - core)


def far_twin():
    z, x, y_low, y_high, core = places()
    return device_at(z, x, y_low, 1 - y_high, 1 - core)


def ring_peers():
    return [z_peer(step) for step in (1, 2, 3)] + [x_peer(step) for step in (1, 2, 3)]


def greet(peers):
    barrier = pltpu.get_barrier_semaphore()
    for peer in peers:
        pl.semaphore_signal(barrier, inc=1, device_id=peer, device_id_type=MESH)
    pl.semaphore_wait(barrier, len(peers))


class Sender:
    def __init__(self, send_sem, recv_sem):
        self.send_sem = send_sem
        self.recv_sem = recv_sem
        self.used = 0
        self.started = []

    def push(self, source, target, peer):
        copy = pltpu.make_async_remote_copy(
            src_ref=source,
            dst_ref=target,
            send_sem=self.send_sem.at[self.used],
            recv_sem=self.recv_sem.at[self.used],
            device_id=peer,
            device_id_type=MESH,
        )
        self.used += 1
        copy.start()
        self.started.append(copy)
        return copy

    def finish(self):
        for copy in self.started:
            copy.wait_send()


class Mover:
    def __init__(self, sem):
        self.sem = sem
        self.used = 0

    def move(self, source, target):
        copy = pltpu.make_async_copy(source, target, self.sem.at[self.used])
        self.used += 1
        copy.start()
        return copy


GATHER_COPIES = 35


def gather_peers():
    return ring_peers() + [near_peer(), cross_peer(), twin_peer()]


def gather_steps(sources, targets, holds, mover, sender):
    z, x, y_low, y_high, core = places()
    mine = y_high * 2 + core
    cross = (1 - y_high) * 2 + core
    count = len(sources)
    firsts = (2 * z + y_low, 8 + 2 * x + y_low, 16)
    others = (2 * z + 1 - y_low, 8 + 2 * x + 1 - y_low)
    crossed = [
        [
            sender.push(sources[at].at[unit], targets[at].at[mine, unit], cross_peer())
            for unit in others + (16,)
        ]
        for at in range(count)
    ]
    loads = [mover.move(sources[at], holds[at]) for at in range(count)]
    arrivals = [
        sender.push(sources[at], targets[at].at[mine], twin_peer()) for at in range(count)
    ]
    yield
    owns = []
    for at in range(count):
        loads[at].wait()
        owns.append(mover.move(holds[at], targets[at].at[mine]))

    def ring(at, part, unit, kept):
        piece = targets[at].at[cross, unit]
        for step in (1, 3, 2):
            peer = z_peer(step) if part == 0 else x_peer(step)
            kept.append((at, part, step, sender.push(piece, piece, peer)))

    first_ring, second_ring = [], []

    def second(at, nears):
        for part in range(2):
            nears[part].wait_recv()
            ring(at, part, others[part], second_ring)
            piece = targets[at].at[cross, others[part]]
            arrivals.append(sender.push(piece, piece, twin_peer()))

    waiting = None
    for at in range(count):
        nears = []
        for part in range(3):
            crossed[at][part].wait_recv()
            piece = targets[at].at[cross, firsts[part]]
            if part < 2:
                nears.append(sender.push(piece, piece, near_peer()))
                ring(at, part, firsts[part], first_ring)
            arrivals.append(sender.push(piece, piece, twin_peer()))
        yield
        if waiting is not None:
            second(*waiting)
        waiting = (at, nears)
    second(*waiting)
    yield
    for at in range(count):
        for kept, base in ((first_ring, y_low), (second_ring, 1 - y_low)):
            for where, part, step, copy in kept:
                if where != at:
                    continue
                copy.wait_recv()
                if part == 0:
                    unit = 2 * lax.rem(z - step + 4, 4) + base
                else:
                    unit = 8 + 2 * lax.rem(x - step + 4, 4) + base
                piece = targets[at].at[cross, unit]
                arrivals.append(sender.push(piece, piece, twin_peer()))
    for copy in arrivals:
        copy.wait_recv()
    for own in owns:
        own.wait()


def gather_kernel(source, small, target, small_out, hold, small_hold, own_sem, send_sem, recv_sem):
    z, x, y_low, y_high, core = places()
    mine = y_high * 2 + core
    mover = Mover(own_sem)
    load = mover.move(small, small_hold)
    greet(gather_peers() + [far_peer(), far_twin()])
    sender = Sender(send_sem, recv_sem)
    arrivals = [
        sender.push(small, small_out.at[mine], twin_peer()),
        sender.push(small, small_out.at[mine], far_peer()),
        sender.push(small, small_out.at[mine], far_twin()),
    ]
    load.wait()
    own = mover.move(small_hold, small_out.at[mine])
    for _ in gather_steps([source], [target], [hold], mover, sender):
        pass
    for copy in arrivals:
        copy.wait_recv()
    own.wait()
    sender.finish()


def gather_weights(part, small, collective):
    whole = [part, small]
    shapes = [jax.ShapeDtypeStruct((4,) + each.shape, each.dtype) for each in whole]
    return pl.pallas_call(
        gather_kernel,
        out_shape=shapes,
        in_specs=[pl.BlockSpec(memory_space=pl.ANY)] * 2,
        out_specs=[pl.BlockSpec(memory_space=pl.ANY)] * 2,
        scratch_shapes=[pltpu.VMEM(each.shape, each.dtype) for each in whole]
        + [
            pltpu.SemaphoreType.DMA((4,)),
            pltpu.SemaphoreType.DMA((GATHER_COPIES + 3,)),
            pltpu.SemaphoreType.DMA((GATHER_COPIES + 3,)),
        ],
        compiler_params=pltpu.CompilerParams(
            collective_id=collective, has_side_effects=True, vmem_limit_bytes=58 << 20
        ),
        cost_estimate=pl.CostEstimate(flops=0, bytes_accessed=20 << 20, transcendentals=0),
    )(*whole)


def product_kernel(cut, *refs):
    out = refs[-1]
    products = []
    for at in range(0, len(refs) - 1, 4):
        left = jnp.concatenate([refs[at][...], refs[at + 1][...]], axis=1)
        right = jnp.concatenate([refs[at + 2][...], refs[at + 3][...]], axis=0)
        products.append((left, right))
    if cut is None:
        out[...] = dot_nn(*products[0]).astype(jnp.bfloat16)
        return
    (left, right), (other_left, other_right) = products
    out[:, 0:cut] = dot_nn(left, right[:, 0:cut]).astype(jnp.bfloat16)
    shared = dot_nn(left, right[:, cut : cut + 128]) + dot_nn(other_left, other_right[:, 0:128])
    out[:, cut : cut + 128] = shared.astype(jnp.bfloat16)
    out[:, cut + 128 :] = dot_nn(other_left, other_right[:, 128:]).astype(jnp.bfloat16)


def weight_products(operands, width, cut=None):
    size = operands[0][0].shape[0]
    block = 272
    specs, flat = [], []
    for left, other_left, right, other_right in operands:
        specs += [pl.BlockSpec((block, left.shape[1]), lambda step: (step, 0))] * 2
        specs += [pl.BlockSpec(right.shape, lambda step: (0, 0))] * 2
        flat += [left, other_left, right, other_right]
    terms = pl.pallas_call(
        functools.partial(product_kernel, cut),
        grid=(size // block,),
        out_shape=jax.ShapeDtypeStruct((size, width), jnp.bfloat16),
        in_specs=specs,
        out_specs=pl.BlockSpec((block, width), lambda step: (step, 0)),
        compiler_params=pltpu.CompilerParams(vmem_limit_bytes=58 << 20),
        cost_estimate=pl.CostEstimate(
            flops=512 * size * width, bytes_accessed=2 * size * width, transcendentals=0
        ),
    )(*flat)
    return terms.reshape(2, UNITS, size // (2 * UNITS), width)


def push_rings(sender, terms, by_z, by_x):
    z, x, y_low, y_high, core = places()
    copies = []
    for step in (2, 1, 3):
        to_z, to_x = lax.rem(z + step, 4), lax.rem(x + step, 4)
        copies.append(
            sender.push(terms.at[:, pl.ds(2 * to_z, 2)], by_z.at[step - 1], z_peer(step))
        )
        copies.append(
            sender.push(terms.at[:, pl.ds(8 + 2 * to_x, 2)], by_x.at[step - 1], x_peer(step))
        )
    return copies


def widen(values):
    return values.astype(jnp.float32)


def halves(values, group):
    if group == 2:
        return values[0:32], values[32:64]
    return values[:, 0:2176], values[:, 2176:4352]


LAST_COPIES = 6 + 3 * (6 + 3 + 6 + 6 + 18) + 3 + 3 + 3 + 3 + 3 + 9


def last_kernel(*refs):
    terms, tail = refs[0:3], refs[3]
    far_z, far_x = (None,) + refs[4:6], (None,) + refs[6:8]
    totals, small_out = refs[8:11], refs[11]
    scratch = refs[12:]
    own, by, parted, met, merged, landed, summed = [
        scratch[3 * at : 3 * at + 3] for at in range(7)
    ]
    own_t, by_t, parted_t, met_t, merged_t, landed_t, summed_t, whole_t = scratch[21:29]
    units, small_unit = scratch[29:32], scratch[32]
    own_sem, send_sem, recv_sem = scratch[33:36]
    z, x, y_low, y_high, core = places()
    mover = Mover(own_sem)
    order = (2, 1, 0)
    loads = {}
    for group in order:
        loads[group] = [
            mover.move(terms[group].at[:, pl.ds(2 * z, 2)], own[group].at[0]),
            mover.move(terms[group].at[:, pl.ds(8 + 2 * x, 2)], own[group].at[1]),
        ]
        if group > 0:
            loads[group].append(mover.move(far_z[group], by[group].at[0]))
            loads[group].append(mover.move(far_x[group], by[group].at[1]))
    load_tail = mover.move(tail.at[:, z], own_t)
    greet(ring_peers() + [near_peer(), cross_peer(), far_peer()])
    sender = Sender(send_sem, recv_sem)
    first = push_rings(sender, terms[0], by[0].at[0], by[0].at[1])
    first_t = [
        sender.push(tail.at[:, lax.rem(z + step, 4)], by_t.at[step - 1], z_peer(step))
        for step in (2, 1, 3)
    ]

    second = {}
    for group in order:
        for load in loads[group]:
            load.wait()
        if group == 0:
            for copy in first:
                copy.wait_recv()
        second[group] = []
        for ring in range(2):
            for unit in range(2):
                for side in range(2):
                    total = widen(own[group][ring, side, unit])
                    for step in range(3):
                        total = total + widen(by[group][ring, step, side, unit])
                    pair = halves(total.astype(jnp.bfloat16), group)
                    parted[group][ring, 2 * unit, side] = pair[0]
                    parted[group][ring, 2 * unit + 1, side] = pair[1]
            for step in (2, 1, 3):
                place = lax.rem(x + step, 4) if ring == 0 else lax.rem(z + step, 4)
                peer = x_peer(step) if ring == 0 else z_peer(step)
                second[group].append(
                    sender.push(
                        parted[group].at[ring, place], met[group].at[ring, step - 1], peer
                    )
                )
    load_tail.wait()
    for copy in first_t:
        copy.wait_recv()
    for place in range(4):
        total = widen(own_t[:, place])
        for step in range(3):
            total = total + widen(by_t[step, :, place])
        parted_t[place] = total.astype(jnp.bfloat16)
    second_t = [
        sender.push(parted_t.at[lax.rem(x + step, 4)], met_t.at[step - 1], x_peer(step))
        for step in (2, 1, 3)
    ]

    def across(source, target):
        return [
            sender.push(source.at[0], target.at[0], near_peer()),
            sender.push(source.at[1], target.at[1], cross_peer()),
            sender.push(source.at[1], target.at[2], far_peer()),
        ]

    third = {}
    for group in order:
        for copy in second[group]:
            copy.wait_recv()
        for ring in range(2):
            total = widen(parted[group][ring, x if ring == 0 else z])
            for step in range(3):
                total = total + widen(met[group][ring, step])
            merged[group][:, ring] = total.astype(jnp.bfloat16)
        third[group] = across(merged[group], landed[group])
    for copy in second_t:
        copy.wait_recv()
    total = widen(parted_t[x])
    for step in range(3):
        total = total + widen(met_t[step])
    merged_t[...] = total.astype(jnp.bfloat16)
    third_t = across(merged_t, landed_t)

    def spot(group, ring, at_z, at_x):
        unit = 2 * at_z + at_x // 2 if ring == 0 else 8 + 2 * at_x + at_z // 2
        half = lax.rem(at_x, 2) if ring == 0 else lax.rem(at_z, 2)
        if group == 2:
            return totals[group].at[unit, pl.ds(pl.multiple_of(half * 32, 32), 32)]
        return totals[group].at[unit, :, pl.ds(pl.multiple_of(half * 2176, 128), 2176)]

    passed, ends, owns = [], [], []
    for group in order:
        for copy in third[group]:
            copy.wait_recv()
        near = widen(merged[group][0]) + widen(landed[group][0])
        away = widen(landed[group][1]) + widen(landed[group][2])
        summed[group][...] = (near + away).astype(jnp.bfloat16)
        for ring in range(2):
            place = spot(group, ring, z, x)
            piece = summed[group].at[ring]
            owns.append(mover.move(piece, place))
            for step in (1, 3, 2):
                peer = x_peer(step) if ring == 0 else z_peer(step)
                passed.append((group, ring, step, sender.push(piece, place, peer)))
            for step in (1, 3, 2):
                peer = z_peer(step) if ring == 0 else x_peer(step)
                ends.append(sender.push(piece, place, peer))
    for copy in third_t:
        copy.wait_recv()
    near = widen(merged_t[0]) + widen(landed_t[0])
    away = widen(landed_t[1]) + widen(landed_t[2])
    summed_t[...] = (near + away).astype(jnp.bfloat16)
    owns.append(mover.move(summed_t, whole_t.at[z, x]))
    for step in (1, 3, 2):
        passed.append((3, 0, step, sender.push(summed_t, whole_t.at[z, x], x_peer(step))))
    for step in (1, 3, 2):
        ends.append(sender.push(summed_t, whole_t.at[z, x], z_peer(step)))

    for group, ring, step, copy in passed:
        copy.wait_recv()
        if group == 3:
            place = whole_t.at[z, lax.rem(x - step + 4, 4)]
        elif ring == 0:
            place = spot(group, ring, z, lax.rem(x - step + 4, 4))
        else:
            place = spot(group, ring, lax.rem(z - step + 4, 4), x)
        for other in (1, 3, 2):
            peer = z_peer(other) if ring == 0 else x_peer(other)
            ends.append(sender.push(place, place, peer))
    for copy in ends:
        copy.wait_recv()
    for copy in owns:
        copy.wait()

    def tile(at):
        return whole_t[at // 28, at // 7 % 4, :, 128 * (at % 7) : 128 * (at % 7 + 1)]

    for at in range(34):
        units[0][:, 128 * at : 128 * (at + 1)] = tile(at)
        units[1][:, 128 * at : 128 * (at + 1)] = tile(34 + at)
    for row in range(4):
        for at in range(9):
            width = min(128, 1088 - 128 * at)
            units[2][16 * row : 16 * row + 16, 128 * at : 128 * at + width] = tile(
                68 + 9 * row + at
            )[:, :width]
    for at in range(8):
        small_unit[:, 128 * at : 128 * (at + 1)] = tile(104 + at)
    lasts = [mover.move(units[group], totals[group].at[16]) for group in range(3)]
    lasts.append(mover.move(small_unit, small_out))
    for copy in lasts:
        copy.wait()
    sender.finish()


def last_exchange(terms, tail, far_z, far_x, collective):
    low = jnp.bfloat16

    def each(make):
        return [pltpu.VMEM(make(*pair), low) for pair in zip(SHAPES, PIECES)]

    scratch = (
        each(lambda unit, piece: (2, 2, 2) + unit)
        + each(lambda unit, piece: (2, 3, 2, 2) + unit)
        + each(lambda unit, piece: (2, 4, 2) + piece)
        + each(lambda unit, piece: (2, 3, 2) + piece)
        + each(lambda unit, piece: (2, 2) + piece)
        + each(lambda unit, piece: (3, 2) + piece)
        + each(lambda unit, piece: (2,) + piece)
        + [
            pltpu.VMEM((2, 4, 16, TAIL), low),
            pltpu.VMEM((3, 2, 4, 16, TAIL), low),
            pltpu.VMEM((4, 2, 16, TAIL), low),
            pltpu.VMEM((3, 2, 16, TAIL), low),
            pltpu.VMEM((2, 16, TAIL), low),
            pltpu.VMEM((3, 16, TAIL), low),
            pltpu.VMEM((16, TAIL), low),
            pltpu.VMEM((4, 4, 16, TAIL), low),
        ]
        + each(lambda unit, piece: unit)
        + [
            pltpu.VMEM((16, 1024), low),
            pltpu.SemaphoreType.DMA((24,)),
            pltpu.SemaphoreType.DMA((LAST_COPIES,)),
            pltpu.SemaphoreType.DMA((LAST_COPIES,)),
        ]
    )
    return pl.pallas_call(
        last_kernel,
        out_shape=[jax.ShapeDtypeStruct((UNITS,) + unit, low) for unit in SHAPES]
        + [jax.ShapeDtypeStruct((16, 1024), low)],
        in_specs=[pl.BlockSpec(memory_space=pl.ANY)] * 8,
        out_specs=[pl.BlockSpec(memory_space=pl.ANY)] * 4,
        scratch_shapes=scratch,
        compiler_params=pltpu.CompilerParams(
            collective_id=collective, has_side_effects=True, vmem_limit_bytes=48 << 20
        ),
        cost_estimate=pl.CostEstimate(flops=0, bytes_accessed=40 << 20, transcendentals=0),
    )(*terms, tail, *far_z, *far_x)


def reduce_grads(terms, small, far_z, far_x, collective):
    down = terms[2][:, 16].reshape(2, 4, 16, 1088)
    down = jnp.pad(down, ((0, 0), (0, 0), (0, 0), (0, 64)))
    down = jnp.transpose(down, (0, 2, 1, 3)).reshape(2, 16, 4608)
    extra = jnp.pad(small, ((0, 0), (0, 16 * 1024 - small.shape[1]))).reshape(2, 16, 1024)
    tail = jnp.concatenate(
        [terms[0][:, 16], terms[1][:, 16], down, extra.astype(jnp.bfloat16)], axis=-1
    )
    tail = jnp.transpose(tail.reshape(2, 16, 4, 4, TAIL), (0, 2, 3, 1, 4))
    joint, fc, down, small = last_exchange(terms, tail, far_z, far_x, collective)
    joint = joint.reshape(272, 4352)
    outs = (
        joint[:, :3264].astype(jnp.float32),
        joint[:, 3264:].astype(jnp.float32),
        fc.reshape(272, 4352).astype(jnp.float32),
        down.reshape(1088, 1088).astype(jnp.float32),
    )
    return outs, small.reshape(-1)[:3264].astype(jnp.float32)


def mean_rows(values):
    return jnp.sum(values, axis=-1, keepdims=True) * (1.0 / values.shape[-1])


def normal_rows(values):
    centre = values - mean_rows(values)
    scale = lax.rsqrt(mean_rows(centre * centre) + 1e-05)
    return centre * scale, scale


def norm_back(grads, gain, unit, scale):
    scaled = grads * gain
    return scale * (scaled - mean_rows(scaled) - unit * mean_rows(scaled * unit))


def column_sums(values):
    return jnp.sum(values, axis=0, keepdims=True)


def turned(values):
    rows, width = values.shape
    full = jnp.concatenate([values, jnp.zeros((rows, 1152 - width), values.dtype)], axis=1)
    return full.T[0:width, :]


def before_kernel(tokens, gain, offset, weight, bias, packed, turned_ref, joint, joint_t):
    unit, _ = normal_rows(widen(tokens[...]))
    normed = (unit * widen(gain[...]) + widen(offset[...])).astype(jnp.bfloat16)
    turned_ref[...] = turned(normed)
    joint[...] = (dot_nn(normed, weight[...]) + widen(bias[...])).astype(jnp.bfloat16)
    blank = jnp.zeros((joint.shape[0], 64), jnp.bfloat16)
    joint_t[...] = jnp.concatenate([joint[...], blank], axis=1).T
    for head in range(HEADS):
        for part in range(3):
            start = 1088 * part + 64 * head
            packed[head, 64 * part : 64 * part + 64] = joint_t[start : start + 64]


def run_before(tokens, gain, offset, weight, bias):
    rows = tokens.shape[0]
    return pl.pallas_call(
        before_kernel,
        out_shape=(
            jax.ShapeDtypeStruct((HEADS, 192, rows), jnp.bfloat16),
            jax.ShapeDtypeStruct((1088, rows), jnp.bfloat16),
        ),
        scratch_shapes=[
            pltpu.VMEM((rows, 3264), jnp.bfloat16),
            pltpu.VMEM((3328, rows), jnp.bfloat16),
        ],
        compiler_params=pltpu.CompilerParams(vmem_limit_bytes=40 << 20),
        cost_estimate=pl.CostEstimate(
            flops=2 * rows * 1088 * 3264, bytes_accessed=8 << 20, transcendentals=0
        ),
    )(tokens, gain, offset, weight, bias)


def middle_kernel(
    heads,
    tokens,
    cotangent,
    w_out,
    b_out,
    gain,
    offset,
    b_down,
    fc,
    b_fc,
    down,
    result,
    grad_middle,
    grad_heads,
    normed_t,
    grad_branch,
    active_t,
    grad_hidden,
    d_fc,
    sums,
    attended,
    normed,
    unit,
    scale,
    total,
    grads,
):
    at = pl.program_id(0)

    @pl.when(at == 0)
    def _():
        filler = jnp.zeros((64, heads.shape[1]), jnp.bfloat16)
        attended[...] = jnp.concatenate([heads[...], filler], axis=0).T[:, 0:1088]
        middle = widen(tokens[...]) + (dot_nn(attended[...], w_out[...]) + widen(b_out[...]))
        unit[...], scale[...] = normal_rows(middle)
        normed[...] = (unit[...] * widen(gain[...]) + widen(offset[...])).astype(jnp.bfloat16)
        normed_t[...] = turned(normed[...])
        total[...] = middle + widen(b_down[...])
        grads[...] = jnp.zeros_like(grads)

    hidden = dot_nn(normed[...], fc[...]) + widen(b_fc[...])
    square = hidden * hidden
    bend = jnp.tanh(0.7978845608028654 * (hidden + 0.044715 * square * hidden))
    active = (0.5 * hidden * (1.0 + bend)).astype(jnp.bfloat16)
    slope = 0.5 * (1.0 + bend) + 0.5 * hidden * (1.0 - bend * bend) * (
        0.7978845608028654 * (1.0 + 3.0 * 0.044715 * square)
    )
    back = (dot_nt(cotangent[...], down[...]) * slope).astype(jnp.bfloat16)
    active_t[...] = active.T
    grad_hidden[...] = back
    d_fc[...] = column_sums(widen(back))
    total[...] += dot_nn(active, down[...])
    grads[...] += dot_nt(back, fc[...])

    @pl.when(at == pl.num_programs(0) - 1)
    def _():
        result[...] = total[...].astype(jnp.bfloat16)
        arrived = widen(cotangent[...])
        whole = grads[...]
        grad = arrived + norm_back(whole, widen(gain[...]), unit[...], scale[...])
        grad_middle[...] = grad
        low = grad.astype(jnp.bfloat16)
        grad_branch[:, 0:64] = jnp.zeros((low.shape[0], 64), jnp.bfloat16)
        grad_branch[:, 64:1152] = low
        sums[0:1, :] = column_sums(widen(low))
        sums[1:2, :] = column_sums(whole * unit[...])
        sums[2:3, :] = column_sums(whole)
        sums[3:4, :] = column_sums(arrived)
        attended[...] = dot_nt(low, w_out[...]).astype(jnp.bfloat16)
        grad_heads[...] = turned(attended[...])


def run_middle(heads, tokens, cotangent, w_out, b_out, gain, offset, b_down, fc, b_fc, down):
    rows = tokens.shape[0]
    low, wide = jnp.bfloat16, jnp.float32
    block = 256

    def fixed(shape):
        return pl.BlockSpec(shape, lambda step: (0,) * len(shape))

    vector = fixed((1, 1088))
    square = fixed((rows, 1088))
    across = pl.BlockSpec((rows, block), lambda step: (0, step))
    line = pl.BlockSpec((1, block), lambda step: (0, step))
    return pl.pallas_call(
        middle_kernel,
        grid=(4352 // block,),
        in_specs=[
            fixed((1088, rows)),
            square,
            square,
            fixed((1088, 1088)),
            vector,
            vector,
            vector,
            vector,
            pl.BlockSpec((1088, block), lambda step: (0, step)),
            line,
            pl.BlockSpec((block, 1088), lambda step: (step, 0)),
        ],
        out_specs=[
            square,
            square,
            fixed((1088, rows)),
            fixed((1088, rows)),
            fixed((rows, 1152)),
            pl.BlockSpec((block, rows), lambda step: (step, 0)),
            across,
            line,
            fixed((4, 1088)),
        ],
        out_shape=[
            jax.ShapeDtypeStruct((rows, 1088), low),
            jax.ShapeDtypeStruct((rows, 1088), wide),
            jax.ShapeDtypeStruct((1088, rows), low),
            jax.ShapeDtypeStruct((1088, rows), low),
            jax.ShapeDtypeStruct((rows, 1152), low),
            jax.ShapeDtypeStruct((4352, rows), low),
            jax.ShapeDtypeStruct((rows, 4352), low),
            jax.ShapeDtypeStruct((1, 4352), wide),
            jax.ShapeDtypeStruct((4, 1088), wide),
        ],
        scratch_shapes=[
            pltpu.VMEM((rows, 1088), low),
            pltpu.VMEM((rows, 1088), low),
            pltpu.VMEM((rows, 1088), wide),
            pltpu.VMEM((rows, 1), wide),
            pltpu.VMEM((rows, 1088), wide),
            pltpu.VMEM((rows, 1088), wide),
        ],
        compiler_params=pltpu.CompilerParams(vmem_limit_bytes=48 << 20),
        cost_estimate=pl.CostEstimate(
            flops=8 * rows * 1088 * 4352, bytes_accessed=24 << 20, transcendentals=rows * 4352
        ),
    )(heads, tokens, cotangent, w_out, b_out, gain, offset, b_down, fc, b_fc, down)


def after_kernel(packed, weight, tokens, gain, grad_middle, joint, grad_tokens, sums, line, joint_t):
    for head in range(HEADS):
        for part in range(3):
            start = 1088 * part + 64 * head
            joint_t[start : start + 64] = packed[head, 64 * part : 64 * part + 64]
    joint_t[3264:3328] = jnp.zeros((64, joint.shape[0]), jnp.bfloat16)
    joint[...] = joint_t[...].T
    unit, scale = normal_rows(widen(tokens[...]))
    grads = dot_nt(joint[:, 0:3264], weight[...])
    back = norm_back(grads, widen(gain[...]), unit, scale)
    grad_tokens[...] = grad_middle[...] + back
    sums[0:1, :] = column_sums(grads * unit)
    sums[1:2, :] = column_sums(grads)
    line[...] = column_sums(widen(joint[:, 0:3264]))


def run_after(packed, weight, tokens, gain, grad_middle):
    rows = tokens.shape[0]
    return pl.pallas_call(
        after_kernel,
        out_shape=(
            jax.ShapeDtypeStruct((rows, 3328), jnp.bfloat16),
            jax.ShapeDtypeStruct((rows, 1088), jnp.float32),
            jax.ShapeDtypeStruct((2, 1088), jnp.float32),
            jax.ShapeDtypeStruct((1, 3264), jnp.float32),
        ),
        scratch_shapes=[pltpu.VMEM((3328, rows), jnp.bfloat16)],
        compiler_params=pltpu.CompilerParams(vmem_limit_bytes=40 << 20),
        cost_estimate=pl.CostEstimate(
            flops=2 * rows * 1088 * 3264, bytes_accessed=10 << 20, transcendentals=0
        ),
    )(packed, weight, tokens, gain, grad_middle)


def local(
    tokens,
    cotangent,
    ln1_scale,
    ln1_bias,
    w_qkv,
    bias_q,
    bias_v,
    w_out,
    bias_out,
    ln2_scale,
    ln2_bias,
    w_fc,
    bias_fc,
    w_down,
    bias_down,
):
    ctx_count = lax.axis_size("ctx")
    vectors = (
        ln1_scale,
        ln1_bias,
        bias_q,
        bias_v,
        bias_out,
        ln2_scale,
        ln2_bias,
        bias_down,
        bias_fc,
    )
    small = jnp.concatenate(
        [jnp.stack(vectors[:8]), bias_fc.reshape(4, 272), jnp.zeros((4, 272), jnp.bfloat16)]
    )
    own_parts = [
        part.reshape(UNITS, part.shape[0] // UNITS, part.shape[1])
        for part in (w_qkv, w_out, w_fc, w_down)
    ]
    full_qkv, full_small = gather_weights(own_parts[0], small, 5)
    full_qkv = full_qkv.reshape(1088, 3264)
    lines = [full_small[:, at].reshape(1, 1088) for at in range(8)]
    (line_scale1, line_shift1, line_bq, line_bv, line_bout, line_scale2, line_shift2) = lines[:7]
    line_bdown = lines[7]
    line_bfc = full_small[:, 8:12].reshape(1, 4352)
    z, x, y_low, y_high, core = places()

    def swap(values):
        return lax.ppermute(values, "fsdp", [(0, 1), (1, 0), (2, 3), (3, 2)])

    def split(quarters):
        first, second = quarters[:, 0], quarters[:, 1]
        keep = jnp.where(core == 0, first, second)
        give = jnp.where(core == 0, second, first)
        keep = jnp.where(y_high == 0, keep, keep[::-1])
        give = jnp.where(y_high == 0, give, give[::-1])
        return keep, give

    def products(left, right):
        width, rows = left.shape
        keep, give = split(left.reshape(2, 2, width // 4, rows))
        keep, give = keep.reshape(width // 2, rows), give.reshape(width // 2, rows)
        return keep, swap(give), right, swap(right)

    bias_joint = jnp.concatenate([line_bq, jnp.zeros_like(line_bq), line_bv], axis=1)
    packed, normed_t = run_before(tokens[0], line_scale1, line_shift1, full_qkv, bias_joint)
    head_rows = spread_heads(packed, ctx_count, 1)
    (out_rows, wide_out, lse_rows), (full_out, full_fc, full_down) = run_forward(
        head_rows, own_parts[1:], 8
    )
    full_out = full_out.reshape(1088, 1088)
    full_fc = full_fc.reshape(1088, 4352)
    full_down = full_down.reshape(4352, 1088)
    attended_t = collect_heads(out_rows, ctx_count, 2).reshape(1088, -1)
    (
        result,
        grad_middle,
        grad_heads,
        normed2_t,
        grad_branch,
        active_t,
        grad_hidden,
        line_fc,
        sums_middle,
    ) = run_middle(
        attended_t,
        tokens[0],
        cotangent[0],
        full_out,
        line_bout,
        line_scale2,
        line_shift2,
        line_bdown,
        full_fc,
        line_bfc,
        full_down,
    )
    d_down = weight_products([products(active_t, cotangent[0])], 1088)
    d_fc = weight_products([products(normed2_t, grad_hidden)], 4352)
    out_products = products(attended_t, grad_branch)
    grad_rows = spread_heads(
        grad_heads.reshape(HEADS, HEAD_DIM, -1), ctx_count, 3
    )
    joint_rows_grad, far_z, far_x = run_backward(
        head_rows, grad_rows, wide_out, lse_rows, d_fc, d_down, 7
    )
    packed_grads = collect_heads(joint_rows_grad, ctx_count, 4)
    grad_joint, grad_inputs, sums_after, line_joint = run_after(
        packed_grads, full_qkv, tokens[0], line_scale1, grad_middle
    )
    d_joint = weight_products([products(normed_t, grad_joint), out_products], 4352, 3200)
    d_bout, d_scale2, d_shift2, d_bdown = [sums_middle[at] for at in range(4)]
    d_scale1, d_shift1 = sums_after[0], sums_after[1]
    d_bq, d_bv, d_bfc = line_joint[0, :1088], line_joint[0, 2176:], line_fc[0]
    narrow = (d_scale1, d_shift1, d_bq, d_bv, d_bout, d_scale2, d_shift2, d_bdown, d_bfc)
    sums = jnp.concatenate([vector.reshape(4, -1) for vector in narrow], axis=1)
    keep, give = split(sums.reshape(2, 2, 3264))
    sums = keep + swap(give)
    (t_qkv, t_out, t_fc, t_down), extras = reduce_grads(
        (d_joint, d_fc, d_down), sums, far_z, far_x, 6
    )
    (t_scale1, t_shift1, t_bq, t_bv, t_bout, t_scale2, t_shift2, t_bdown) = [
        extras[at * 272 : (at + 1) * 272] for at in range(8)
    ]
    t_bfc = extras[2176:]
    return (
        result[None],
        grad_inputs[None],
        t_scale1,
        t_shift1,
        t_qkv,
        t_bq,
        t_bv,
        t_out,
        t_bout,
        t_scale2,
        t_shift2,
        t_fc,
        t_bfc,
        t_down,
        t_bdown,
    )


def solution(mesh):
    placed = (
        P("fsdp", "ctx", None),
        P("fsdp", "ctx", None),
        P("fsdp"),
        P("fsdp"),
        P("fsdp", None),
        P("fsdp"),
        P("fsdp"),
        P("fsdp", None),
        P("fsdp"),
        P("fsdp"),
        P("fsdp"),
        P("fsdp", None),
        P("fsdp"),
        P("fsdp", None),
        P("fsdp"),
    )
    return jax.shard_map(
        local,
        mesh=mesh,
        in_specs=placed,
        out_specs=(
            P("fsdp", "ctx", None),
            P("fsdp", "ctx", None),
            P("fsdp"),
            P("fsdp"),
            P("fsdp", None),
            P("fsdp"),
            P("fsdp"),
            P("fsdp", None),
            P("fsdp"),
            P("fsdp"),
            P("fsdp"),
            P("fsdp", None),
            P("fsdp"),
            P("fsdp", None),
            P("fsdp"),
        ),
        check_vma=False,
    )
```

```python
import functools

import jax
import jax.numpy as jnp
from jax import lax
from jax.experimental import pallas as pl
from jax.experimental.pallas import tpu as pltpu
from jax.sharding import PartitionSpec as P

MESH = pl.DeviceIdType.MESH
HEAD_DIM = 64
HEADS = 17
BLOCK = 64
STEP = 512


def head_place(head, core):
    return jnp.where(head < 16, 2 * head + core, 1 - core)


def held_head(place, core):
    own = lax.rem(place, 2) == core
    head = jnp.where(own, place // 2, 16)
    return own | (place == 1 - core), head


def greet_ctx(me, count):
    barrier = pltpu.get_barrier_semaphore()

    def greet(step, carry):
        pl.semaphore_signal(
            barrier, inc=1, device_id={"ctx": lax.rem(me + step, count)}, device_id_type=MESH
        )
        return carry

    lax.fori_loop(1, count, greet, 0)
    pl.semaphore_wait(barrier, count - 1)


def spread_kernel(count, x_ref, out_ref, send_sem, recv_sem, own_sem):
    me = lax.axis_index("ctx")
    core = lax.rem(lax.axis_index("fsdp"), 2)
    has, _ = held_head(me, core)
    greet_ctx(me, count)

    def remote(head, source):
        return pltpu.make_async_remote_copy(
            src_ref=x_ref.at[head],
            dst_ref=out_ref.at[source],
            send_sem=send_sem.at[head],
            recv_sem=recv_sem.at[source],
            device_id={"ctx": head_place(head, core)},
            device_id_type=MESH,
        )

    def own(head):
        return pltpu.make_async_copy(x_ref.at[head], out_ref.at[me], own_sem.at[0])

    def send(head, carry):
        target = head_place(head, core)

        @pl.when(target != me)
        def _():
            remote(head, me).start()

        @pl.when(target == me)
        def _():
            own(head).start()

        return carry

    lax.fori_loop(0, HEADS, send, 0)

    def sent(head, carry):
        target = head_place(head, core)

        @pl.when(target != me)
        def _():
            remote(head, me).wait_send()

        @pl.when(target == me)
        def _():
            own(head).wait()

        return carry

    lax.fori_loop(0, HEADS, sent, 0)

    @pl.when(has)
    def _():
        def arrived(source, carry):
            @pl.when(source != me)
            def _():
                remote(0, source).wait_recv()

            return carry

        lax.fori_loop(0, count, arrived, 0)


def collect_kernel(count, y_ref, out_ref, send_sem, recv_sem, own_sem):
    me = lax.axis_index("ctx")
    core = lax.rem(lax.axis_index("fsdp"), 2)
    has, mine = held_head(me, core)
    greet_ctx(me, count)

    def remote(head, target):
        return pltpu.make_async_remote_copy(
            src_ref=y_ref.at[target],
            dst_ref=out_ref.at[head],
            send_sem=send_sem.at[target],
            recv_sem=recv_sem.at[head],
            device_id={"ctx": target},
            device_id_type=MESH,
        )

    @pl.when(has)
    def _():
        def send(step, carry):
            remote(mine, lax.rem(me + 11 * step, count)).start()
            return carry

        lax.fori_loop(1, count, send, 0)
        own = pltpu.make_async_copy(y_ref.at[me], out_ref.at[mine], own_sem.at[0])
        own.start()

        def sent(step, carry):
            remote(mine, lax.rem(me + 11 * step, count)).wait_send()
            return carry

        lax.fori_loop(1, count, sent, 0)
        own.wait()

    def arrived(head, carry):
        @pl.when(head_place(head, core) != me)
        def _():
            remote(head, 0).wait_recv()

        return carry

    lax.fori_loop(0, HEADS, arrived, 0)


def spread_heads(packed, count, collective):
    return pl.pallas_call(
        functools.partial(spread_kernel, count),
        out_shape=jax.ShapeDtypeStruct((count,) + packed.shape[1:], packed.dtype),
        in_specs=[pl.BlockSpec(memory_space=pltpu.VMEM)],
        out_specs=pl.BlockSpec(memory_space=pltpu.VMEM),
        scratch_shapes=[
            pltpu.SemaphoreType.DMA((HEADS,)),
            pltpu.SemaphoreType.DMA((count,)),
            pltpu.SemaphoreType.DMA((1,)),
        ],
        compiler_params=pltpu.CompilerParams(
            collective_id=collective, has_side_effects=True, vmem_limit_bytes=24 << 20
        ),
        cost_estimate=pl.CostEstimate(flops=0, bytes_accessed=4 << 20, transcendentals=0),
    )(packed)


def collect_heads(pieces, count, collective):
    return pl.pallas_call(
        functools.partial(collect_kernel, count),
        out_shape=jax.ShapeDtypeStruct((HEADS,) + pieces.shape[1:], pieces.dtype),
        in_specs=[pl.BlockSpec(memory_space=pltpu.VMEM)],
        out_specs=pl.BlockSpec(memory_space=pltpu.VMEM),
        scratch_shapes=[
            pltpu.SemaphoreType.DMA((count,)),
            pltpu.SemaphoreType.DMA((HEADS,)),
            pltpu.SemaphoreType.DMA((1,)),
        ],
        compiler_params=pltpu.CompilerParams(
            collective_id=collective, has_side_effects=True, vmem_limit_bytes=24 << 20
        ),
        cost_estimate=pl.CostEstimate(flops=0, bytes_accessed=4 << 20, transcendentals=0),
    )(pieces)


TILES = 32


def tile_span(at):
    return pl.ds(pl.multiple_of(at * 128, 128), 128)


def each_tile(visit):
    def low(at, carry):
        visit(at, 2 * at, 2 * at + 1, 0)
        return carry

    def high(at, carry):
        visit(TILES // 2 + at, TILES - 1 - 2 * at, TILES - 2 - 2 * at, 64)
        return carry

    lax.fori_loop(0, TILES // 2, low, 0)
    lax.fori_loop(0, TILES // 2, high, 0)


def take_tile(ref, first, second, lane):
    return jnp.concatenate(
        [ref[first, :, lane : lane + 64], ref[second, :, lane : lane + 64]], axis=1
    )


def put_tile(ref, first, second, lane, tile):
    ref[first, :, lane : lane + 64] = tile[:, 0:64]
    ref[second, :, lane : lane + 64] = tile[:, 64:128]


def dot_nt(left, right):
    return lax.dot_general(
        left, right, (((1,), (1,)), ((), ())), preferred_element_type=jnp.float32
    )


def dot_nn(left, right):
    return jnp.dot(left, right, preferred_element_type=jnp.float32)


def causal(scores):
    keys = lax.broadcasted_iota(jnp.int32, scores.shape, 0)
    asks = lax.broadcasted_iota(jnp.int32, scores.shape, 1)
    return keys <= asks


def attend_forward(*refs):
    x_ref, sources = refs[0], refs[1:4]
    out_ref, wide_ref, lse_ref = refs[4:7]
    targets = refs[7:10]
    q_ref, k_ref, vt_ref = refs[10:13]
    holds = refs[13:16]
    own_sem, send_sem, recv_sem = refs[16:19]
    has, _ = held_head(lax.axis_index("ctx"), lax.rem(lax.axis_index("fsdp"), 2))
    blocks = lse_ref.shape[1] // STEP
    greet(gather_peers())
    sender = Sender(send_sem, recv_sem)
    steps = gather_steps(sources, targets, holds, Mover(own_sem), sender)
    next(steps)

    @pl.when(has)
    def _():
        def prepare(at, first, second, lane):
            tile = take_tile(x_ref, first, second, lane)
            q_ref[:, tile_span(at)] = tile[0:64] * jnp.bfloat16(0.125)
            k_ref[tile_span(at), :] = tile[64:192].T[:, 0:64]
            vt_ref[:, tile_span(at)] = tile[128:192]

        each_tile(prepare)

    def one_block(at):
        asks = pl.ds(at * STEP, STEP)
        query = q_ref[:, asks]

        def update(state, place, masked):
            top, total, accum = state
            keys = pl.ds(pl.multiple_of(place * STEP, STEP), STEP)
            scores = dot_nn(k_ref[keys, :], query)
            if masked:
                scores = jnp.where(causal(scores), scores, -1e30)
            new_top = jnp.maximum(top, jnp.max(scores, axis=0, keepdims=True))
            factor = jnp.exp(top - new_top)
            weights = jnp.exp(scores - new_top)
            total = total * factor + jnp.sum(weights, axis=0, keepdims=True)
            accum = accum * factor + dot_nn(vt_ref[:, keys], weights.astype(jnp.bfloat16))
            return new_top, total, accum

        state = (
            jnp.full((1, STEP), -1e30, jnp.float32),
            jnp.zeros((1, STEP), jnp.float32),
            jnp.zeros((64, STEP), jnp.float32),
        )
        state = update(state, at, True)
        state = lax.fori_loop(0, at, lambda place, held: update(held, place, False), state)
        top, total, accum = state
        result = accum / total
        wide_ref[:, asks] = result
        lse_ref[:, asks] = top + jnp.log(total)
        low = result.astype(jnp.bfloat16)
        for part in range(4):
            tile = low[:, 128 * part : 128 * part + 128]
            index = 4 * at + part
            if index < TILES // 2:
                put_tile(out_ref, 2 * index, 2 * index + 1, 0, tile)
            else:
                rest = 2 * (index - TILES // 2)
                put_tile(out_ref, TILES - 1 - rest, TILES - 2 - rest, 64, tile)

    for at in range(blocks):
        pl.when(has)(functools.partial(one_block, at))
        if at >= 3:
            next(steps, None)
    for _ in steps:
        pass
    sender.finish()


def attend_backward(
    x_ref,
    g_ref,
    wide_ref,
    lse_ref,
    fc_ref,
    down_ref,
    out_ref,
    fc_z_ref,
    down_z_ref,
    fc_x_ref,
    down_x_ref,
    q_ref,
    k_ref,
    kt_ref,
    v_ref,
    go_ref,
    dq_ref,
    delta_ref,
    grad_ref,
    send_sem,
    recv_sem,
):
    has, _ = held_head(lax.axis_index("ctx"), lax.rem(lax.axis_index("fsdp"), 2))
    blocks = lse_ref.shape[1] // STEP
    greet(ring_peers())
    sender = Sender(send_sem, recv_sem)
    push_rings(sender, down_ref, down_z_ref, down_x_ref)
    push_rings(sender, fc_ref, fc_z_ref, fc_x_ref)

    @pl.when(has)
    def _():
        blank = jnp.zeros((64, 128), jnp.bfloat16)

        def prepare(at, first, second, lane):
            span = tile_span(at)
            tile = take_tile(x_ref, first, second, lane)
            rows = jnp.concatenate([tile, blank], axis=0).T
            q_ref[span, :] = rows[:, 0:64] * jnp.bfloat16(0.125)
            k_ref[span, :] = rows[:, 64:128]
            kt_ref[:, span] = tile[64:128]
            v_ref[span, :] = rows[:, 128:192]
            grad = take_tile(g_ref, first, second, lane)
            go_ref[span, :] = jnp.concatenate([grad, blank], axis=0).T[:, 0:64]
            delta_ref[:, span] = jnp.sum(
                grad.astype(jnp.float32) * wide_ref[:, span], axis=0, keepdims=True
            )
            dq_ref[:, span] = jnp.zeros((64, 128), jnp.float32)

        each_tile(prepare)

        def one_block(place, carry):
            keys = pl.ds(pl.multiple_of(place * STEP, STEP), STEP)
            key = k_ref[keys, :]
            turned_key = kt_ref[:, keys]
            value = v_ref[keys, :]

            def update(state, at, masked):
                grad_key, grad_value = state
                asks = pl.ds(pl.multiple_of(at * STEP, STEP), STEP)
                query = q_ref[asks, :]
                grad = go_ref[asks, :]
                probs = jnp.exp(dot_nt(key, query) - lse_ref[:, asks])
                if masked:
                    probs = jnp.where(causal(probs), probs, 0.0)
                grad_probs = dot_nt(value, grad)
                grad_scores = (probs * (grad_probs - delta_ref[:, asks])).astype(jnp.bfloat16)
                grad_value = grad_value + dot_nn(probs.astype(jnp.bfloat16), grad)
                grad_key = grad_key + dot_nn(grad_scores, query)
                dq_ref[:, asks] += dot_nn(turned_key, grad_scores)
                return grad_key, grad_value

            state = (jnp.zeros((STEP, 64), jnp.float32), jnp.zeros((STEP, 64), jnp.float32))
            state = update(state, place, True)
            grad_key, grad_value = lax.fori_loop(
                place + 1, blocks, lambda at, held: update(held, at, False), state
            )
            grad_ref[64:192, keys] = (
                jnp.concatenate([grad_key, grad_value], axis=1).T.astype(jnp.bfloat16)
            )
            return carry

        lax.fori_loop(0, blocks, one_block, 0)

        def finish(at, first, second, lane):
            span = tile_span(at)
            query_part = (dq_ref[:, span] * 0.125).astype(jnp.bfloat16)
            tile = jnp.concatenate([query_part, grad_ref[64:192, span]], axis=0)
            put_tile(out_ref, first, second, lane, tile)

        each_tile(finish)

    for copy in sender.started:
        copy.wait_recv()
    sender.finish()


def run_forward(rows, weights, collective):
    length = rows.shape[0] * rows.shape[2]
    inside = pl.BlockSpec(memory_space=pltpu.VMEM)
    outside = pl.BlockSpec(memory_space=pl.ANY)
    results = pl.pallas_call(
        attend_forward,
        out_shape=[
            jax.ShapeDtypeStruct((TILES, 64, 128), jnp.bfloat16),
            jax.ShapeDtypeStruct((64, length), jnp.float32),
            jax.ShapeDtypeStruct((1, length), jnp.float32),
        ]
        + [jax.ShapeDtypeStruct((4,) + weight.shape, weight.dtype) for weight in weights],
        in_specs=[inside] + [outside] * 3,
        out_specs=[inside] * 3 + [outside] * 3,
        scratch_shapes=[
            pltpu.VMEM((64, length), jnp.bfloat16),
            pltpu.VMEM((length, 64), jnp.bfloat16),
            pltpu.VMEM((64, length), jnp.bfloat16),
        ]
        + [pltpu.VMEM(weight.shape, weight.dtype) for weight in weights]
        + [
            pltpu.SemaphoreType.DMA((6,)),
            pltpu.SemaphoreType.DMA((3 * GATHER_COPIES,)),
            pltpu.SemaphoreType.DMA((3 * GATHER_COPIES,)),
        ],
        compiler_params=pltpu.CompilerParams(
            collective_id=collective, has_side_effects=True, vmem_limit_bytes=56 << 20
        ),
        cost_estimate=pl.CostEstimate(
            flops=2 * length * length * 64,
            bytes_accessed=length * 512 * 2,
            transcendentals=length * length // 2,
        ),
    )(rows, *weights)
    return results[0:3], results[3:6]


def run_backward(rows, grads, wide, lse, fc, down, collective):
    length = rows.shape[0] * rows.shape[2]
    inside = pl.BlockSpec(memory_space=pltpu.VMEM)
    outside = pl.BlockSpec(memory_space=pl.ANY)
    received = [
        jax.ShapeDtypeStruct((3, 2, 2) + part.shape[2:], part.dtype)
        for part in (fc, down, fc, down)
    ]
    results = pl.pallas_call(
        attend_backward,
        out_shape=[jax.ShapeDtypeStruct(rows.shape, jnp.bfloat16)] + received,
        in_specs=[inside] * 4 + [outside] * 2,
        out_specs=[inside] + [outside] * 4,
        scratch_shapes=[
            pltpu.VMEM((length, 64), jnp.bfloat16),
            pltpu.VMEM((length, 64), jnp.bfloat16),
            pltpu.VMEM((64, length), jnp.bfloat16),
            pltpu.VMEM((length, 64), jnp.bfloat16),
            pltpu.VMEM((length, 64), jnp.bfloat16),
            pltpu.VMEM((64, length), jnp.float32),
            pltpu.VMEM((1, length), jnp.float32),
            pltpu.VMEM((192, length), jnp.bfloat16),
            pltpu.SemaphoreType.DMA((12,)),
            pltpu.SemaphoreType.DMA((12,)),
        ],
        compiler_params=pltpu.CompilerParams(
            collective_id=collective, has_side_effects=True, vmem_limit_bytes=58 << 20
        ),
        cost_estimate=pl.CostEstimate(
            flops=5 * length * length * 64,
            bytes_accessed=length * 512 * 3,
            transcendentals=length * length // 2,
        ),
    )(rows, grads, wide, lse, fc, down)
    return results[0], results[1:3], results[3:5]


UNITS = 17
TAIL = 896
SHAPES = ((16, 4352), (16, 4352), (64, 1088))
PIECES = ((16, 2176), (16, 2176), (32, 1088))


def places():
    ctx = lax.axis_index("ctx")
    fsdp = lax.axis_index("fsdp")
    return ctx // 8, lax.rem(ctx // 2, 4), lax.rem(ctx, 2), fsdp // 2, lax.rem(fsdp, 2)


def device_at(z, x, y_low, y_high, core):
    return (z * 8 + x * 2 + y_low, y_high * 2 + core)


def z_peer(step):
    z, x, y_low, y_high, core = places()
    return device_at(lax.rem(z + step, 4), x, y_low, y_high, core)


def x_peer(step):
    z, x, y_low, y_high, core = places()
    return device_at(z, lax.rem(x + step, 4), y_low, y_high, core)


def near_peer():
    z, x, y_low, y_high, core = places()
    return device_at(z, x, 1 - y_low, y_high, core)


def cross_peer():
    z, x, y_low, y_high, core = places()
    return device_at(z, x, 1 - y_low, 1 - y_high, core)


def far_peer():
    z, x, y_low, y_high, core = places()
    return device_at(z, x, y_low, 1 - y_high, core)


def twin_peer():
    z, x, y_low, y_high, core = places()
    return device_at(z, x, y_low, y_high, 1 - core)


def far_twin():
    z, x, y_low, y_high, core = places()
    return device_at(z, x, y_low, 1 - y_high, 1 - core)


def ring_peers():
    return [z_peer(step) for step in (1, 2, 3)] + [x_peer(step) for step in (1, 2, 3)]


def greet(peers):
    barrier = pltpu.get_barrier_semaphore()
    for peer in peers:
        pl.semaphore_signal(barrier, inc=1, device_id=peer, device_id_type=MESH)
    pl.semaphore_wait(barrier, len(peers))


class Sender:
    def __init__(self, send_sem, recv_sem):
        self.send_sem = send_sem
        self.recv_sem = recv_sem
        self.used = 0
        self.started = []

    def push(self, source, target, peer):
        copy = pltpu.make_async_remote_copy(
            src_ref=source,
            dst_ref=target,
            send_sem=self.send_sem.at[self.used],
            recv_sem=self.recv_sem.at[self.used],
            device_id=peer,
            device_id_type=MESH,
        )
        self.used += 1
        copy.start()
        self.started.append(copy)
        return copy

    def finish(self):
        for copy in self.started:
            copy.wait_send()


class Mover:
    def __init__(self, sem):
        self.sem = sem
        self.used = 0

    def move(self, source, target):
        copy = pltpu.make_async_copy(source, target, self.sem.at[self.used])
        self.used += 1
        copy.start()
        return copy


GATHER_COPIES = 35


def gather_peers():
    return ring_peers() + [near_peer(), cross_peer(), twin_peer()]


def gather_steps(sources, targets, holds, mover, sender):
    z, x, y_low, y_high, core = places()
    mine = y_high * 2 + core
    cross = (1 - y_high) * 2 + core
    count = len(sources)
    firsts = (2 * z + y_low, 8 + 2 * x + y_low, 16)
    others = (2 * z + 1 - y_low, 8 + 2 * x + 1 - y_low)
    crossed = [
        [
            sender.push(sources[at].at[unit], targets[at].at[mine, unit], cross_peer())
            for unit in others + (16,)
        ]
        for at in range(count)
    ]
    loads = [mover.move(sources[at], holds[at]) for at in range(count)]
    arrivals = [
        sender.push(sources[at], targets[at].at[mine], twin_peer()) for at in range(count)
    ]
    yield
    owns = []
    for at in range(count):
        loads[at].wait()
        owns.append(mover.move(holds[at], targets[at].at[mine]))

    def ring(at, part, unit, kept):
        piece = targets[at].at[cross, unit]
        for step in (1, 3, 2):
            peer = z_peer(step) if part == 0 else x_peer(step)
            kept.append((at, part, step, sender.push(piece, piece, peer)))

    first_ring, second_ring = [], []

    def second(at, nears):
        for part in range(2):
            nears[part].wait_recv()
            ring(at, part, others[part], second_ring)
            piece = targets[at].at[cross, others[part]]
            arrivals.append(sender.push(piece, piece, twin_peer()))

    waiting = None
    for at in range(count):
        nears = []
        for part in range(3):
            crossed[at][part].wait_recv()
            piece = targets[at].at[cross, firsts[part]]
            if part < 2:
                nears.append(sender.push(piece, piece, near_peer()))
                ring(at, part, firsts[part], first_ring)
            arrivals.append(sender.push(piece, piece, twin_peer()))
        yield
        if waiting is not None:
            second(*waiting)
        waiting = (at, nears)
    second(*waiting)
    yield
    for at in range(count):
        for kept, base in ((first_ring, y_low), (second_ring, 1 - y_low)):
            for where, part, step, copy in kept:
                if where != at:
                    continue
                copy.wait_recv()
                if part == 0:
                    unit = 2 * lax.rem(z - step + 4, 4) + base
                else:
                    unit = 8 + 2 * lax.rem(x - step + 4, 4) + base
                piece = targets[at].at[cross, unit]
                arrivals.append(sender.push(piece, piece, twin_peer()))
    for copy in arrivals:
        copy.wait_recv()
    for own in owns:
        own.wait()


def gather_kernel(source, small, target, small_out, hold, small_hold, own_sem, send_sem, recv_sem):
    z, x, y_low, y_high, core = places()
    mine = y_high * 2 + core
    mover = Mover(own_sem)
    load = mover.move(small, small_hold)
    greet(gather_peers() + [far_peer(), far_twin()])
    sender = Sender(send_sem, recv_sem)
    arrivals = [
        sender.push(small, small_out.at[mine], twin_peer()),
        sender.push(small, small_out.at[mine], far_peer()),
        sender.push(small, small_out.at[mine], far_twin()),
    ]
    load.wait()
    own = mover.move(small_hold, small_out.at[mine])
    for _ in gather_steps([source], [target], [hold], mover, sender):
        pass
    for copy in arrivals:
        copy.wait_recv()
    own.wait()
    sender.finish()


def gather_weights(part, small, collective):
    whole = [part, small]
    shapes = [jax.ShapeDtypeStruct((4,) + each.shape, each.dtype) for each in whole]
    return pl.pallas_call(
        gather_kernel,
        out_shape=shapes,
        in_specs=[pl.BlockSpec(memory_space=pl.ANY)] * 2,
        out_specs=[pl.BlockSpec(memory_space=pl.ANY)] * 2,
        scratch_shapes=[pltpu.VMEM(each.shape, each.dtype) for each in whole]
        + [
            pltpu.SemaphoreType.DMA((4,)),
            pltpu.SemaphoreType.DMA((GATHER_COPIES + 3,)),
            pltpu.SemaphoreType.DMA((GATHER_COPIES + 3,)),
        ],
        compiler_params=pltpu.CompilerParams(
            collective_id=collective, has_side_effects=True, vmem_limit_bytes=58 << 20
        ),
        cost_estimate=pl.CostEstimate(flops=0, bytes_accessed=20 << 20, transcendentals=0),
    )(*whole)


def product_kernel(cut, *refs):
    out = refs[-1]
    products = []
    for at in range(0, len(refs) - 1, 4):
        left = jnp.concatenate([refs[at][...], refs[at + 1][...]], axis=1)
        right = jnp.concatenate([refs[at + 2][...], refs[at + 3][...]], axis=0)
        products.append((left, right))
    if cut is None:
        out[...] = dot_nn(*products[0]).astype(jnp.bfloat16)
        return
    (left, right), (other_left, other_right) = products
    out[:, 0:cut] = dot_nn(left, right[:, 0:cut]).astype(jnp.bfloat16)
    shared = dot_nn(left, right[:, cut : cut + 128]) + dot_nn(other_left, other_right[:, 0:128])
    out[:, cut : cut + 128] = shared.astype(jnp.bfloat16)
    out[:, cut + 128 :] = dot_nn(other_left, other_right[:, 128:]).astype(jnp.bfloat16)


def weight_products(operands, width, cut=None):
    size = operands[0][0].shape[0]
    block = 272
    specs, flat = [], []
    for left, other_left, right, other_right in operands:
        specs += [pl.BlockSpec((block, left.shape[1]), lambda step: (step, 0))] * 2
        specs += [pl.BlockSpec(right.shape, lambda step: (0, 0))] * 2
        flat += [left, other_left, right, other_right]
    terms = pl.pallas_call(
        functools.partial(product_kernel, cut),
        grid=(size // block,),
        out_shape=jax.ShapeDtypeStruct((size, width), jnp.bfloat16),
        in_specs=specs,
        out_specs=pl.BlockSpec((block, width), lambda step: (step, 0)),
        compiler_params=pltpu.CompilerParams(vmem_limit_bytes=58 << 20),
        cost_estimate=pl.CostEstimate(
            flops=512 * size * width, bytes_accessed=2 * size * width, transcendentals=0
        ),
    )(*flat)
    return terms.reshape(2, UNITS, size // (2 * UNITS), width)


def push_rings(sender, terms, by_z, by_x):
    z, x, y_low, y_high, core = places()
    copies = []
    for step in (2, 1, 3):
        to_z, to_x = lax.rem(z + step, 4), lax.rem(x + step, 4)
        copies.append(
            sender.push(terms.at[:, pl.ds(2 * to_z, 2)], by_z.at[step - 1], z_peer(step))
        )
        copies.append(
            sender.push(terms.at[:, pl.ds(8 + 2 * to_x, 2)], by_x.at[step - 1], x_peer(step))
        )
    return copies


def widen(values):
    return values.astype(jnp.float32)


def halves(values, group):
    if group == 2:
        return values[0:32], values[32:64]
    return values[:, 0:2176], values[:, 2176:4352]


LAST_COPIES = 6 + 3 * (6 + 3 + 6 + 16 + 16) + 3 + 3 + 3 + 3 + 3 + 9


def last_kernel(*refs):
    terms, tail = refs[0:3], refs[3]
    far_z, far_x = (None,) + refs[4:6], (None,) + refs[6:8]
    totals, small_out = refs[8:11], refs[11]
    scratch = refs[12:]
    own, by, parted, met, merged, landed, summed = [
        scratch[3 * at : 3 * at + 3] for at in range(7)
    ]
    own_t, by_t, parted_t, met_t, merged_t, landed_t, summed_t, whole_t = scratch[21:29]
    units, small_unit = scratch[29:32], scratch[32]
    own_sem, send_sem, recv_sem = scratch[33:36]
    z, x, y_low, y_high, core = places()
    mover = Mover(own_sem)
    order = (2, 1, 0)
    loads = {}
    for group in order:
        loads[group] = [
            mover.move(terms[group].at[:, pl.ds(2 * z, 2)], own[group].at[0]),
            mover.move(terms[group].at[:, pl.ds(8 + 2 * x, 2)], own[group].at[1]),
        ]
        if group > 0:
            loads[group].append(mover.move(far_z[group], by[group].at[0]))
            loads[group].append(mover.move(far_x[group], by[group].at[1]))

    def tail_part(place):
        return tail.at[:, :, pl.ds(pl.multiple_of(place * 4 * TAIL, 128), 4 * TAIL)]

    load_tail = mover.move(tail_part(z), own_t)
    greet(ring_peers() + [near_peer(), cross_peer(), far_peer()])
    sender = Sender(send_sem, recv_sem)
    first = push_rings(sender, terms[0], by[0].at[0], by[0].at[1])
    first_t = [
        sender.push(tail_part(lax.rem(z + step, 4)), by_t.at[step - 1], z_peer(step))
        for step in (2, 1, 3)
    ]

    second = {}
    for group in order:
        for load in loads[group]:
            load.wait()
        if group == 0:
            for copy in first:
                copy.wait_recv()
        second[group] = []
        for ring in range(2):
            for unit in range(2):
                for side in range(2):
                    total = widen(own[group][ring, side, unit])
                    for step in range(3):
                        total = total + widen(by[group][ring, step, side, unit])
                    pair = halves(total.astype(jnp.bfloat16), group)
                    parted[group][ring, 2 * unit, side] = pair[0]
                    parted[group][ring, 2 * unit + 1, side] = pair[1]
            for step in (2, 1, 3):
                place = lax.rem(x + step, 4) if ring == 0 else lax.rem(z + step, 4)
                peer = x_peer(step) if ring == 0 else z_peer(step)
                second[group].append(
                    sender.push(
                        parted[group].at[ring, place], met[group].at[ring, step - 1], peer
                    )
                )
    load_tail.wait()
    for copy in first_t:
        copy.wait_recv()
    for place in range(4):
        columns = slice(TAIL * place, TAIL * (place + 1))
        total = widen(own_t[:, :, columns])
        for step in range(3):
            total = total + widen(by_t[step, :, :, columns])
        parted_t[place] = total.astype(jnp.bfloat16)
    second_t = [
        sender.push(parted_t.at[lax.rem(x + step, 4)], met_t.at[step - 1], x_peer(step))
        for step in (2, 1, 3)
    ]

    def across(source, target):
        return [
            sender.push(source.at[0], target.at[0], near_peer()),
            sender.push(source.at[1], target.at[1], cross_peer()),
            sender.push(source.at[1], target.at[2], far_peer()),
        ]

    third = {}
    for group in order:
        for copy in second[group]:
            copy.wait_recv()
        for ring in range(2):
            total = widen(parted[group][ring, x if ring == 0 else z])
            for step in range(3):
                total = total + widen(met[group][ring, step])
            merged[group][:, ring] = total.astype(jnp.bfloat16)
        third[group] = across(merged[group], landed[group])
    for copy in second_t:
        copy.wait_recv()
    total = widen(parted_t[x])
    for step in range(3):
        total = total + widen(met_t[step])
    merged_t[...] = total.astype(jnp.bfloat16)
    third_t = across(merged_t, landed_t)

    def spot(group, ring, at_z, at_x, side=None):
        unit = 2 * at_z + at_x // 2 if ring == 0 else 8 + 2 * at_x + at_z // 2
        half = lax.rem(at_x, 2) if ring == 0 else lax.rem(at_z, 2)
        if group == 2:
            start, size = ((0, 32), (0, 16), (16, 16))[0 if side is None else side + 1]
            rows = pl.ds(pl.multiple_of(half * 32 + start, 16), size)
            return totals[group].at[unit, rows]
        start, size = ((0, 2176), (0, 1152), (1152, 1024))[0 if side is None else side + 1]
        columns = pl.ds(pl.multiple_of(half * 2176 + start, 128), size)
        return totals[group].at[unit, :, columns]

    def step_on(ring, at_z, at_x, step):
        if ring == 0:
            return lax.rem(at_z + step, 4), at_x
        return at_z, lax.rem(at_x + step, 4)

    passed, ends, owns, nexts = [], [], [], []

    def spread_on(group, ring, source, at_z, at_x):
        place = spot(group, ring, at_z, at_x)
        for step in (1, 3):
            peer = z_peer(step) if ring == 0 else x_peer(step)
            copy = sender.push(source, place, peer)
            nexts.append((group, ring, step, at_z, at_x, copy))

    for group in order:
        for copy in third[group]:
            copy.wait_recv()
        near = widen(merged[group][0]) + widen(landed[group][0])
        away = widen(landed[group][1]) + widen(landed[group][2])
        summed[group][...] = (near + away).astype(jnp.bfloat16)
        for ring in range(2):
            place = spot(group, ring, z, x)
            piece = summed[group].at[ring]
            owns.append(mover.move(piece, place))
            for step in (1, 3, 2):
                peer = x_peer(step) if ring == 0 else z_peer(step)
                passed.append((group, ring, step, sender.push(piece, place, peer)))
            spread_on(group, ring, piece, z, x)
    for copy in third_t:
        copy.wait_recv()
    near = widen(merged_t[0]) + widen(landed_t[0])
    away = widen(landed_t[1]) + widen(landed_t[2])
    summed_t[...] = (near + away).astype(jnp.bfloat16)
    owns.append(mover.move(summed_t, whole_t.at[z, x]))
    for step in (1, 3, 2):
        passed.append((3, 0, step, sender.push(summed_t, whole_t.at[z, x], x_peer(step))))
    for step in (1, 3, 2):
        ends.append(sender.push(summed_t, whole_t.at[z, x], z_peer(step)))

    for group, ring, step, copy in passed:
        copy.wait_recv()
        if group == 3:
            place = whole_t.at[z, lax.rem(x - step + 4, 4)]
            for other in (1, 3, 2):
                ends.append(sender.push(place, place, z_peer(other)))
            continue
        at_z, at_x = step_on(1 - ring, z, x, 4 - step)
        spread_on(group, ring, spot(group, ring, at_z, at_x), at_z, at_x)
    for group, ring, step, at_z, at_x, copy in nexts:
        copy.wait_recv()
        from_z, from_x = step_on(ring, at_z, at_x, 4 - step)
        piece = spot(group, ring, from_z, from_x, 0 if step == 1 else 1)
        peer = z_peer(step) if ring == 0 else x_peer(step)
        ends.append(sender.push(piece, piece, peer))
    for copy in ends:
        copy.wait_recv()
    for copy in owns:
        copy.wait()

    def tile(at):
        return whole_t[at // 28, at // 7 % 4, :, 128 * (at % 7) : 128 * (at % 7 + 1)]

    for at in range(34):
        units[0][:, 128 * at : 128 * (at + 1)] = tile(at)
        units[1][:, 128 * at : 128 * (at + 1)] = tile(34 + at)
    for row in range(4):
        for at in range(9):
            width = min(128, 1088 - 128 * at)
            units[2][16 * row : 16 * row + 16, 128 * at : 128 * at + width] = tile(
                68 + 9 * row + at
            )[:, :width]
    for at in range(8):
        small_unit[:, 128 * at : 128 * (at + 1)] = tile(104 + at)
    lasts = [mover.move(units[group], totals[group].at[16]) for group in range(3)]
    lasts.append(mover.move(small_unit, small_out))
    for copy in lasts:
        copy.wait()
    sender.finish()


def last_exchange(terms, tail, far_z, far_x, collective):
    low = jnp.bfloat16

    def each(make):
        return [pltpu.VMEM(make(*pair), low) for pair in zip(SHAPES, PIECES)]

    scratch = (
        each(lambda unit, piece: (2, 2, 2) + unit)
        + each(lambda unit, piece: (2, 3, 2, 2) + unit)
        + each(lambda unit, piece: (2, 4, 2) + piece)
        + each(lambda unit, piece: (2, 3, 2) + piece)
        + each(lambda unit, piece: (2, 2) + piece)
        + each(lambda unit, piece: (3, 2) + piece)
        + each(lambda unit, piece: (2,) + piece)
        + [
            pltpu.VMEM((2, 16, 4 * TAIL), low),
            pltpu.VMEM((3, 2, 16, 4 * TAIL), low),
            pltpu.VMEM((4, 2, 16, TAIL), low),
            pltpu.VMEM((3, 2, 16, TAIL), low),
            pltpu.VMEM((2, 16, TAIL), low),
            pltpu.VMEM((3, 16, TAIL), low),
            pltpu.VMEM((16, TAIL), low),
            pltpu.VMEM((4, 4, 16, TAIL), low),
        ]
        + each(lambda unit, piece: unit)
        + [
            pltpu.VMEM((16, 1024), low),
            pltpu.SemaphoreType.DMA((24,)),
            pltpu.SemaphoreType.DMA((LAST_COPIES,)),
            pltpu.SemaphoreType.DMA((LAST_COPIES,)),
        ]
    )
    return pl.pallas_call(
        last_kernel,
        out_shape=[jax.ShapeDtypeStruct((UNITS,) + unit, low) for unit in SHAPES]
        + [jax.ShapeDtypeStruct((16, 1024), low)],
        in_specs=[pl.BlockSpec(memory_space=pl.ANY)] * 8,
        out_specs=[pl.BlockSpec(memory_space=pl.ANY)] * 4,
        scratch_shapes=scratch,
        compiler_params=pltpu.CompilerParams(
            collective_id=collective, has_side_effects=True, vmem_limit_bytes=48 << 20
        ),
        cost_estimate=pl.CostEstimate(flops=0, bytes_accessed=40 << 20, transcendentals=0),
    )(*terms, tail, *far_z, *far_x)


def reduce_grads(terms, small, far_z, far_x, collective):
    down = terms[2][:, 16].reshape(2, 4, 16, 1088)
    down = jnp.pad(down, ((0, 0), (0, 0), (0, 0), (0, 64)))
    down = jnp.transpose(down, (0, 2, 1, 3)).reshape(2, 16, 4608)
    extra = jnp.pad(small, ((0, 0), (0, 16 * 1024 - small.shape[1]))).reshape(2, 16, 1024)
    tail = jnp.concatenate(
        [terms[0][:, 16], terms[1][:, 16], down, extra.astype(jnp.bfloat16)], axis=-1
    )
    joint, fc, down, small = last_exchange(terms, tail, far_z, far_x, collective)
    joint = joint.reshape(272, 4352)
    outs = (
        joint[:, :3264].astype(jnp.float32),
        joint[:, 3264:].astype(jnp.float32),
        fc.reshape(272, 4352).astype(jnp.float32),
        down.reshape(1088, 1088).astype(jnp.float32),
    )
    return outs, small.reshape(-1)[:3264].astype(jnp.float32)


def mean_rows(values):
    return jnp.sum(values, axis=-1, keepdims=True) * (1.0 / values.shape[-1])


def normal_rows(values):
    centre = values - mean_rows(values)
    scale = lax.rsqrt(mean_rows(centre * centre) + 1e-05)
    return centre * scale, scale


def norm_back(grads, gain, unit, scale):
    scaled = grads * gain
    return scale * (scaled - mean_rows(scaled) - unit * mean_rows(scaled * unit))


def column_sums(values):
    return jnp.sum(values, axis=0, keepdims=True)


def turned(values):
    rows, width = values.shape
    full = jnp.concatenate([values, jnp.zeros((rows, 1152 - width), values.dtype)], axis=1)
    return full.T[0:width, :]


def before_kernel(tokens, gain, offset, weight, bias, packed, turned_ref, joint, joint_t):
    unit, _ = normal_rows(widen(tokens[...]))
    normed = (unit * widen(gain[...]) + widen(offset[...])).astype(jnp.bfloat16)
    turned_ref[...] = turned(normed)
    joint[...] = (dot_nn(normed, weight[...]) + widen(bias[...])).astype(jnp.bfloat16)
    blank = jnp.zeros((joint.shape[0], 64), jnp.bfloat16)
    joint_t[...] = jnp.concatenate([joint[...], blank], axis=1).T
    for head in range(HEADS):
        for part in range(3):
            start = 1088 * part + 64 * head
            packed[head, 64 * part : 64 * part + 64] = joint_t[start : start + 64]


def run_before(tokens, gain, offset, weight, bias):
    rows = tokens.shape[0]
    return pl.pallas_call(
        before_kernel,
        out_shape=(
            jax.ShapeDtypeStruct((HEADS, 192, rows), jnp.bfloat16),
            jax.ShapeDtypeStruct((1088, rows), jnp.bfloat16),
        ),
        scratch_shapes=[
            pltpu.VMEM((rows, 3264), jnp.bfloat16),
            pltpu.VMEM((3328, rows), jnp.bfloat16),
        ],
        compiler_params=pltpu.CompilerParams(vmem_limit_bytes=40 << 20),
        cost_estimate=pl.CostEstimate(
            flops=2 * rows * 1088 * 3264, bytes_accessed=8 << 20, transcendentals=0
        ),
    )(tokens, gain, offset, weight, bias)


def middle_kernel(
    heads,
    tokens,
    cotangent,
    w_out,
    b_out,
    gain,
    offset,
    b_down,
    fc,
    b_fc,
    down,
    result,
    grad_middle,
    grad_heads,
    normed_t,
    grad_branch,
    active_t,
    grad_hidden,
    d_fc,
    sums,
    attended,
    normed,
    unit,
    scale,
    total,
    grads,
):
    at = pl.program_id(0)

    @pl.when(at == 0)
    def _():
        filler = jnp.zeros((64, heads.shape[1]), jnp.bfloat16)
        attended[...] = jnp.concatenate([heads[...], filler], axis=0).T[:, 0:1088]
        middle = widen(tokens[...]) + (dot_nn(attended[...], w_out[...]) + widen(b_out[...]))
        unit[...], scale[...] = normal_rows(middle)
        normed[...] = (unit[...] * widen(gain[...]) + widen(offset[...])).astype(jnp.bfloat16)
        normed_t[...] = turned(normed[...])
        total[...] = middle + widen(b_down[...])
        grads[...] = jnp.zeros_like(grads)

    hidden = dot_nn(normed[...], fc[...]) + widen(b_fc[...])
    square = hidden * hidden
    bend = jnp.tanh(0.7978845608028654 * (hidden + 0.044715 * square * hidden))
    active = (0.5 * hidden * (1.0 + bend)).astype(jnp.bfloat16)
    slope = 0.5 * (1.0 + bend) + 0.5 * hidden * (1.0 - bend * bend) * (
        0.7978845608028654 * (1.0 + 3.0 * 0.044715 * square)
    )
    back = (dot_nt(cotangent[...], down[...]) * slope).astype(jnp.bfloat16)
    active_t[...] = active.T
    grad_hidden[...] = back
    d_fc[...] = column_sums(widen(back))
    total[...] += dot_nn(active, down[...])
    grads[...] += dot_nt(back, fc[...])

    @pl.when(at == pl.num_programs(0) - 1)
    def _():
        result[...] = total[...].astype(jnp.bfloat16)
        arrived = widen(cotangent[...])
        whole = grads[...]
        grad = arrived + norm_back(whole, widen(gain[...]), unit[...], scale[...])
        grad_middle[...] = grad
        low = grad.astype(jnp.bfloat16)
        grad_branch[:, 0:64] = jnp.zeros((low.shape[0], 64), jnp.bfloat16)
        grad_branch[:, 64:1152] = low
        sums[0:1, :] = column_sums(widen(low))
        sums[1:2, :] = column_sums(whole * unit[...])
        sums[2:3, :] = column_sums(whole)
        sums[3:4, :] = column_sums(arrived)
        attended[...] = dot_nt(low, w_out[...]).astype(jnp.bfloat16)
        grad_heads[...] = turned(attended[...])


def run_middle(heads, tokens, cotangent, w_out, b_out, gain, offset, b_down, fc, b_fc, down):
    rows = tokens.shape[0]
    low, wide = jnp.bfloat16, jnp.float32
    block = 256

    def fixed(shape):
        return pl.BlockSpec(shape, lambda step: (0,) * len(shape))

    vector = fixed((1, 1088))
    square = fixed((rows, 1088))
    across = pl.BlockSpec((rows, block), lambda step: (0, step))
    line = pl.BlockSpec((1, block), lambda step: (0, step))
    return pl.pallas_call(
        middle_kernel,
        grid=(4352 // block,),
        in_specs=[
            fixed((1088, rows)),
            square,
            square,
            fixed((1088, 1088)),
            vector,
            vector,
            vector,
            vector,
            pl.BlockSpec((1088, block), lambda step: (0, step)),
            line,
            pl.BlockSpec((block, 1088), lambda step: (step, 0)),
        ],
        out_specs=[
            square,
            square,
            fixed((1088, rows)),
            fixed((1088, rows)),
            fixed((rows, 1152)),
            pl.BlockSpec((block, rows), lambda step: (step, 0)),
            across,
            line,
            fixed((4, 1088)),
        ],
        out_shape=[
            jax.ShapeDtypeStruct((rows, 1088), low),
            jax.ShapeDtypeStruct((rows, 1088), wide),
            jax.ShapeDtypeStruct((1088, rows), low),
            jax.ShapeDtypeStruct((1088, rows), low),
            jax.ShapeDtypeStruct((rows, 1152), low),
            jax.ShapeDtypeStruct((4352, rows), low),
            jax.ShapeDtypeStruct((rows, 4352), low),
            jax.ShapeDtypeStruct((1, 4352), wide),
            jax.ShapeDtypeStruct((4, 1088), wide),
        ],
        scratch_shapes=[
            pltpu.VMEM((rows, 1088), low),
            pltpu.VMEM((rows, 1088), low),
            pltpu.VMEM((rows, 1088), wide),
            pltpu.VMEM((rows, 1), wide),
            pltpu.VMEM((rows, 1088), wide),
            pltpu.VMEM((rows, 1088), wide),
        ],
        compiler_params=pltpu.CompilerParams(vmem_limit_bytes=48 << 20),
        cost_estimate=pl.CostEstimate(
            flops=8 * rows * 1088 * 4352, bytes_accessed=24 << 20, transcendentals=rows * 4352
        ),
    )(heads, tokens, cotangent, w_out, b_out, gain, offset, b_down, fc, b_fc, down)


def after_kernel(packed, weight, tokens, gain, grad_middle, joint, grad_tokens, sums, line, joint_t):
    for head in range(HEADS):
        for part in range(3):
            start = 1088 * part + 64 * head
            joint_t[start : start + 64] = packed[head, 64 * part : 64 * part + 64]
    joint_t[3264:3328] = jnp.zeros((64, joint.shape[0]), jnp.bfloat16)
    joint[...] = joint_t[...].T
    unit, scale = normal_rows(widen(tokens[...]))
    grads = dot_nt(joint[:, 0:3264], weight[...])
    back = norm_back(grads, widen(gain[...]), unit, scale)
    grad_tokens[...] = grad_middle[...] + back
    sums[0:1, :] = column_sums(grads * unit)
    sums[1:2, :] = column_sums(grads)
    line[...] = column_sums(widen(joint[:, 0:3264]))


def run_after(packed, weight, tokens, gain, grad_middle):
    rows = tokens.shape[0]
    return pl.pallas_call(
        after_kernel,
        out_shape=(
            jax.ShapeDtypeStruct((rows, 3328), jnp.bfloat16),
            jax.ShapeDtypeStruct((rows, 1088), jnp.float32),
            jax.ShapeDtypeStruct((2, 1088), jnp.float32),
            jax.ShapeDtypeStruct((1, 3264), jnp.float32),
        ),
        scratch_shapes=[pltpu.VMEM((3328, rows), jnp.bfloat16)],
        compiler_params=pltpu.CompilerParams(vmem_limit_bytes=40 << 20),
        cost_estimate=pl.CostEstimate(
            flops=2 * rows * 1088 * 3264, bytes_accessed=10 << 20, transcendentals=0
        ),
    )(packed, weight, tokens, gain, grad_middle)


def local(
    tokens,
    cotangent,
    ln1_scale,
    ln1_bias,
    w_qkv,
    bias_q,
    bias_v,
    w_out,
    bias_out,
    ln2_scale,
    ln2_bias,
    w_fc,
    bias_fc,
    w_down,
    bias_down,
):
    ctx_count = lax.axis_size("ctx")
    vectors = (
        ln1_scale,
        ln1_bias,
        bias_q,
        bias_v,
        bias_out,
        ln2_scale,
        ln2_bias,
        bias_down,
        bias_fc,
    )
    small = jnp.concatenate(
        [jnp.stack(vectors[:8]), bias_fc.reshape(4, 272), jnp.zeros((4, 272), jnp.bfloat16)]
    )
    own_parts = [
        part.reshape(UNITS, part.shape[0] // UNITS, part.shape[1])
        for part in (w_qkv, w_out, w_fc, w_down)
    ]
    full_qkv, full_small = gather_weights(own_parts[0], small, 5)
    full_qkv = full_qkv.reshape(1088, 3264)
    lines = [full_small[:, at].reshape(1, 1088) for at in range(8)]
    (line_scale1, line_shift1, line_bq, line_bv, line_bout, line_scale2, line_shift2) = lines[:7]
    line_bdown = lines[7]
    line_bfc = full_small[:, 8:12].reshape(1, 4352)
    z, x, y_low, y_high, core = places()

    def swap(values):
        return lax.ppermute(values, "fsdp", [(0, 1), (1, 0), (2, 3), (3, 2)])

    def split(quarters):
        first, second = quarters[:, 0], quarters[:, 1]
        keep = jnp.where(core == 0, first, second)
        give = jnp.where(core == 0, second, first)
        keep = jnp.where(y_high == 0, keep, keep[::-1])
        give = jnp.where(y_high == 0, give, give[::-1])
        return keep, give

    def products(left, right):
        width, rows = left.shape
        keep, give = split(left.reshape(2, 2, width // 4, rows))
        keep, give = keep.reshape(width // 2, rows), give.reshape(width // 2, rows)
        return keep, swap(give), right, swap(right)

    bias_joint = jnp.concatenate([line_bq, jnp.zeros_like(line_bq), line_bv], axis=1)
    packed, normed_t = run_before(tokens[0], line_scale1, line_shift1, full_qkv, bias_joint)
    head_rows = spread_heads(packed, ctx_count, 1)
    (out_rows, wide_out, lse_rows), (full_out, full_fc, full_down) = run_forward(
        head_rows, own_parts[1:], 8
    )
    full_out = full_out.reshape(1088, 1088)
    full_fc = full_fc.reshape(1088, 4352)
    full_down = full_down.reshape(4352, 1088)
    attended_t = collect_heads(out_rows, ctx_count, 2).reshape(1088, -1)
    (
        result,
        grad_middle,
        grad_heads,
        normed2_t,
        grad_branch,
        active_t,
        grad_hidden,
        line_fc,
        sums_middle,
    ) = run_middle(
        attended_t,
        tokens[0],
        cotangent[0],
        full_out,
        line_bout,
        line_scale2,
        line_shift2,
        line_bdown,
        full_fc,
        line_bfc,
        full_down,
    )
    d_down = weight_products([products(active_t, cotangent[0])], 1088)
    d_fc = weight_products([products(normed2_t, grad_hidden)], 4352)
    out_products = products(attended_t, grad_branch)
    grad_rows = spread_heads(
        grad_heads.reshape(HEADS, HEAD_DIM, -1), ctx_count, 3
    )
    joint_rows_grad, far_z, far_x = run_backward(
        head_rows, grad_rows, wide_out, lse_rows, d_fc, d_down, 7
    )
    packed_grads = collect_heads(joint_rows_grad, ctx_count, 4)
    grad_joint, grad_inputs, sums_after, line_joint = run_after(
        packed_grads, full_qkv, tokens[0], line_scale1, grad_middle
    )
    d_joint = weight_products([products(normed_t, grad_joint), out_products], 4352, 3200)
    d_bout, d_scale2, d_shift2, d_bdown = [sums_middle[at] for at in range(4)]
    d_scale1, d_shift1 = sums_after[0], sums_after[1]
    d_bq, d_bv, d_bfc = line_joint[0, :1088], line_joint[0, 2176:], line_fc[0]
    narrow = (d_scale1, d_shift1, d_bq, d_bv, d_bout, d_scale2, d_shift2, d_bdown, d_bfc)
    sums = jnp.concatenate([vector.reshape(4, -1) for vector in narrow], axis=1)
    keep, give = split(sums.reshape(2, 2, 3264))
    sums = keep + swap(give)
    (t_qkv, t_out, t_fc, t_down), extras = reduce_grads(
        (d_joint, d_fc, d_down), sums, far_z, far_x, 6
    )
    (t_scale1, t_shift1, t_bq, t_bv, t_bout, t_scale2, t_shift2, t_bdown) = [
        extras[at * 272 : (at + 1) * 272] for at in range(8)
    ]
    t_bfc = extras[2176:]
    return (
        result[None],
        grad_inputs[None],
        t_scale1,
        t_shift1,
        t_qkv,
        t_bq,
        t_bv,
        t_out,
        t_bout,
        t_scale2,
        t_shift2,
        t_fc,
        t_bfc,
        t_down,
        t_bdown,
    )


def solution(mesh):
    placed = (
        P("fsdp", "ctx", None),
        P("fsdp", "ctx", None),
        P("fsdp"),
        P("fsdp"),
        P("fsdp", None),
        P("fsdp"),
        P("fsdp"),
        P("fsdp", None),
        P("fsdp"),
        P("fsdp"),
        P("fsdp"),
        P("fsdp", None),
        P("fsdp"),
        P("fsdp", None),
        P("fsdp"),
    )
    return jax.shard_map(
        local,
        mesh=mesh,
        in_specs=placed,
        out_specs=(
            P("fsdp", "ctx", None),
            P("fsdp", "ctx", None),
            P("fsdp"),
            P("fsdp"),
            P("fsdp", None),
            P("fsdp"),
            P("fsdp"),
            P("fsdp", None),
            P("fsdp"),
            P("fsdp"),
            P("fsdp"),
            P("fsdp", None),
            P("fsdp"),
            P("fsdp", None),
            P("fsdp"),
        ),
        check_vma=False,
    )
```

```python
import functools

import jax
import jax.numpy as jnp
from jax import lax
from jax.experimental import pallas as pl
from jax.experimental.pallas import tpu as pltpu
from jax.sharding import PartitionSpec as P

MESH = pl.DeviceIdType.MESH
HEAD_DIM = 64
HEADS = 17
BLOCK = 64
STEP = 512


def head_place(head, core):
    return jnp.where(head < 16, 2 * head + core, 1 - core)


def held_head(place, core):
    own = lax.rem(place, 2) == core
    head = jnp.where(own, place // 2, 16)
    return own | (place == 1 - core), head


def greet_ctx(me, count):
    barrier = pltpu.get_barrier_semaphore()

    def greet(step, carry):
        pl.semaphore_signal(
            barrier, inc=1, device_id={"ctx": lax.rem(me + step, count)}, device_id_type=MESH
        )
        return carry

    lax.fori_loop(1, count, greet, 0)
    pl.semaphore_wait(barrier, count - 1)


def spread_kernel(count, x_ref, out_ref, send_sem, recv_sem, own_sem):
    me = lax.axis_index("ctx")
    core = lax.rem(lax.axis_index("fsdp"), 2)
    has, _ = held_head(me, core)
    greet_ctx(me, count)

    def remote(head, source):
        return pltpu.make_async_remote_copy(
            src_ref=x_ref.at[head],
            dst_ref=out_ref.at[source],
            send_sem=send_sem.at[head],
            recv_sem=recv_sem.at[source],
            device_id={"ctx": head_place(head, core)},
            device_id_type=MESH,
        )

    def own(head):
        return pltpu.make_async_copy(x_ref.at[head], out_ref.at[me], own_sem.at[0])

    def send(head, carry):
        target = head_place(head, core)

        @pl.when(target != me)
        def _():
            remote(head, me).start()

        @pl.when(target == me)
        def _():
            own(head).start()

        return carry

    lax.fori_loop(0, HEADS, send, 0)

    def sent(head, carry):
        target = head_place(head, core)

        @pl.when(target != me)
        def _():
            remote(head, me).wait_send()

        @pl.when(target == me)
        def _():
            own(head).wait()

        return carry

    lax.fori_loop(0, HEADS, sent, 0)

    @pl.when(has)
    def _():
        def arrived(source, carry):
            @pl.when(source != me)
            def _():
                remote(0, source).wait_recv()

            return carry

        lax.fori_loop(0, count, arrived, 0)


def collect_kernel(count, y_ref, out_ref, send_sem, recv_sem, own_sem):
    me = lax.axis_index("ctx")
    core = lax.rem(lax.axis_index("fsdp"), 2)
    has, mine = held_head(me, core)
    greet_ctx(me, count)

    def remote(head, target):
        return pltpu.make_async_remote_copy(
            src_ref=y_ref.at[target],
            dst_ref=out_ref.at[head],
            send_sem=send_sem.at[target],
            recv_sem=recv_sem.at[head],
            device_id={"ctx": target},
            device_id_type=MESH,
        )

    @pl.when(has)
    def _():
        def send(step, carry):
            remote(mine, lax.rem(me + 11 * step, count)).start()
            return carry

        lax.fori_loop(1, count, send, 0)
        own = pltpu.make_async_copy(y_ref.at[me], out_ref.at[mine], own_sem.at[0])
        own.start()

        def sent(step, carry):
            remote(mine, lax.rem(me + 11 * step, count)).wait_send()
            return carry

        lax.fori_loop(1, count, sent, 0)
        own.wait()

    def arrived(head, carry):
        @pl.when(head_place(head, core) != me)
        def _():
            remote(head, 0).wait_recv()

        return carry

    lax.fori_loop(0, HEADS, arrived, 0)


def spread_heads(packed, count, collective):
    return pl.pallas_call(
        functools.partial(spread_kernel, count),
        out_shape=jax.ShapeDtypeStruct((count,) + packed.shape[1:], packed.dtype),
        in_specs=[pl.BlockSpec(memory_space=pltpu.VMEM)],
        out_specs=pl.BlockSpec(memory_space=pltpu.VMEM),
        scratch_shapes=[
            pltpu.SemaphoreType.DMA((HEADS,)),
            pltpu.SemaphoreType.DMA((count,)),
            pltpu.SemaphoreType.DMA((1,)),
        ],
        compiler_params=pltpu.CompilerParams(
            collective_id=collective, has_side_effects=True, vmem_limit_bytes=24 << 20
        ),
        cost_estimate=pl.CostEstimate(flops=0, bytes_accessed=4 << 20, transcendentals=0),
    )(packed)


def collect_heads(pieces, count, collective):
    return pl.pallas_call(
        functools.partial(collect_kernel, count),
        out_shape=jax.ShapeDtypeStruct((HEADS,) + pieces.shape[1:], pieces.dtype),
        in_specs=[pl.BlockSpec(memory_space=pltpu.VMEM)],
        out_specs=pl.BlockSpec(memory_space=pltpu.VMEM),
        scratch_shapes=[
            pltpu.SemaphoreType.DMA((count,)),
            pltpu.SemaphoreType.DMA((HEADS,)),
            pltpu.SemaphoreType.DMA((1,)),
        ],
        compiler_params=pltpu.CompilerParams(
            collective_id=collective, has_side_effects=True, vmem_limit_bytes=24 << 20
        ),
        cost_estimate=pl.CostEstimate(flops=0, bytes_accessed=4 << 20, transcendentals=0),
    )(pieces)


TILES = 32


def tile_span(at):
    return pl.ds(pl.multiple_of(at * 128, 128), 128)


def each_tile(visit):
    def low(at, carry):
        visit(at, 2 * at, 2 * at + 1, 0)
        return carry

    def high(at, carry):
        visit(TILES // 2 + at, TILES - 1 - 2 * at, TILES - 2 - 2 * at, 64)
        return carry

    lax.fori_loop(0, TILES // 2, low, 0)
    lax.fori_loop(0, TILES // 2, high, 0)


def take_tile(ref, first, second, lane):
    return jnp.concatenate(
        [ref[first, :, lane : lane + 64], ref[second, :, lane : lane + 64]], axis=1
    )


def put_tile(ref, first, second, lane, tile):
    ref[first, :, lane : lane + 64] = tile[:, 0:64]
    ref[second, :, lane : lane + 64] = tile[:, 64:128]


def dot_nt(left, right):
    return lax.dot_general(
        left, right, (((1,), (1,)), ((), ())), preferred_element_type=jnp.float32
    )


def dot_nn(left, right):
    return jnp.dot(left, right, preferred_element_type=jnp.float32)


def causal(scores):
    keys = lax.broadcasted_iota(jnp.int32, scores.shape, 0)
    asks = lax.broadcasted_iota(jnp.int32, scores.shape, 1)
    return keys <= asks


def attend_forward(*refs):
    x_ref, sources = refs[0], refs[1:4]
    out_ref, wide_ref, lse_ref = refs[4:7]
    targets = refs[7:10]
    q_ref, k_ref, vt_ref = refs[10:13]
    holds = refs[13:16]
    own_sem, send_sem, recv_sem = refs[16:19]
    has, _ = held_head(lax.axis_index("ctx"), lax.rem(lax.axis_index("fsdp"), 2))
    blocks = lse_ref.shape[1] // STEP
    greet(gather_peers())
    sender = Sender(send_sem, recv_sem)
    steps = gather_steps(sources, targets, holds, Mover(own_sem), sender)
    next(steps)

    @pl.when(has)
    def _():
        def prepare(at, first, second, lane):
            tile = take_tile(x_ref, first, second, lane)
            q_ref[:, tile_span(at)] = tile[0:64] * jnp.bfloat16(0.125)
            k_ref[tile_span(at), :] = tile[64:192].T[:, 0:64]
            vt_ref[:, tile_span(at)] = tile[128:192]

        each_tile(prepare)

    def one_block(at):
        asks = pl.ds(at * STEP, STEP)
        query = q_ref[:, asks]

        def update(state, place, masked):
            top, total, accum = state
            keys = pl.ds(pl.multiple_of(place * STEP, STEP), STEP)
            scores = dot_nn(k_ref[keys, :], query)
            if masked:
                scores = jnp.where(causal(scores), scores, -1e30)
            new_top = jnp.maximum(top, jnp.max(scores, axis=0, keepdims=True))
            factor = jnp.exp(top - new_top)
            weights = jnp.exp(scores - new_top)
            total = total * factor + jnp.sum(weights, axis=0, keepdims=True)
            accum = accum * factor + dot_nn(vt_ref[:, keys], weights.astype(jnp.bfloat16))
            return new_top, total, accum

        state = (
            jnp.full((1, STEP), -1e30, jnp.float32),
            jnp.zeros((1, STEP), jnp.float32),
            jnp.zeros((64, STEP), jnp.float32),
        )
        state = update(state, at, True)
        state = lax.fori_loop(0, at, lambda place, held: update(held, place, False), state)
        top, total, accum = state
        result = accum / total
        wide_ref[:, asks] = result
        lse_ref[:, asks] = top + jnp.log(total)
        low = result.astype(jnp.bfloat16)
        for part in range(4):
            tile = low[:, 128 * part : 128 * part + 128]
            index = 4 * at + part
            if index < TILES // 2:
                put_tile(out_ref, 2 * index, 2 * index + 1, 0, tile)
            else:
                rest = 2 * (index - TILES // 2)
                put_tile(out_ref, TILES - 1 - rest, TILES - 2 - rest, 64, tile)

    for at in range(blocks):
        pl.when(has)(functools.partial(one_block, at))
        if at in (1, 4, 6, 7):
            next(steps, None)
    for _ in steps:
        pass
    sender.finish()


def attend_backward(
    x_ref,
    g_ref,
    wide_ref,
    lse_ref,
    fc_ref,
    down_ref,
    out_ref,
    fc_z_ref,
    down_z_ref,
    fc_x_ref,
    down_x_ref,
    q_ref,
    k_ref,
    kt_ref,
    v_ref,
    go_ref,
    dq_ref,
    delta_ref,
    grad_ref,
    send_sem,
    recv_sem,
):
    has, _ = held_head(lax.axis_index("ctx"), lax.rem(lax.axis_index("fsdp"), 2))
    blocks = lse_ref.shape[1] // STEP
    greet(ring_peers())
    sender = Sender(send_sem, recv_sem)
    push_rings(sender, down_ref, down_z_ref, down_x_ref)
    push_rings(sender, fc_ref, fc_z_ref, fc_x_ref)

    @pl.when(has)
    def _():
        blank = jnp.zeros((64, 128), jnp.bfloat16)

        def prepare(at, first, second, lane):
            span = tile_span(at)
            tile = take_tile(x_ref, first, second, lane)
            rows = jnp.concatenate([tile, blank], axis=0).T
            q_ref[span, :] = rows[:, 0:64] * jnp.bfloat16(0.125)
            k_ref[span, :] = rows[:, 64:128]
            kt_ref[:, span] = tile[64:128]
            v_ref[span, :] = rows[:, 128:192]
            grad = take_tile(g_ref, first, second, lane)
            go_ref[span, :] = jnp.concatenate([grad, blank], axis=0).T[:, 0:64]
            delta_ref[:, span] = jnp.sum(
                grad.astype(jnp.float32) * wide_ref[:, span], axis=0, keepdims=True
            )
            dq_ref[:, span] = jnp.zeros((64, 128), jnp.float32)

        each_tile(prepare)

        def one_block(place, carry):
            keys = pl.ds(pl.multiple_of(place * STEP, STEP), STEP)
            key = k_ref[keys, :]
            turned_key = kt_ref[:, keys]
            value = v_ref[keys, :]

            def update(state, at, masked):
                grad_key, grad_value = state
                asks = pl.ds(pl.multiple_of(at * STEP, STEP), STEP)
                query = q_ref[asks, :]
                grad = go_ref[asks, :]
                probs = jnp.exp(dot_nt(key, query) - lse_ref[:, asks])
                if masked:
                    probs = jnp.where(causal(probs), probs, 0.0)
                grad_probs = dot_nt(value, grad)
                grad_scores = (probs * (grad_probs - delta_ref[:, asks])).astype(jnp.bfloat16)
                grad_value = grad_value + dot_nn(probs.astype(jnp.bfloat16), grad)
                grad_key = grad_key + dot_nn(grad_scores, query)
                dq_ref[:, asks] += dot_nn(turned_key, grad_scores)
                return grad_key, grad_value

            state = (jnp.zeros((STEP, 64), jnp.float32), jnp.zeros((STEP, 64), jnp.float32))
            state = update(state, place, True)
            grad_key, grad_value = lax.fori_loop(
                place + 1, blocks, lambda at, held: update(held, at, False), state
            )
            grad_ref[64:192, keys] = (
                jnp.concatenate([grad_key, grad_value], axis=1).T.astype(jnp.bfloat16)
            )
            return carry

        lax.fori_loop(0, blocks, one_block, 0)

        def finish(at, first, second, lane):
            span = tile_span(at)
            query_part = (dq_ref[:, span] * 0.125).astype(jnp.bfloat16)
            tile = jnp.concatenate([query_part, grad_ref[64:192, span]], axis=0)
            put_tile(out_ref, first, second, lane, tile)

        each_tile(finish)

    for copy in sender.started:
        copy.wait_recv()
    sender.finish()


def run_forward(rows, weights, collective):
    length = rows.shape[0] * rows.shape[2]
    inside = pl.BlockSpec(memory_space=pltpu.VMEM)
    outside = pl.BlockSpec(memory_space=pl.ANY)
    results = pl.pallas_call(
        attend_forward,
        out_shape=[
            jax.ShapeDtypeStruct((TILES, 64, 128), jnp.bfloat16),
            jax.ShapeDtypeStruct((64, length), jnp.float32),
            jax.ShapeDtypeStruct((1, length), jnp.float32),
        ]
        + [jax.ShapeDtypeStruct((4,) + weight.shape, weight.dtype) for weight in weights],
        in_specs=[inside] + [outside] * 3,
        out_specs=[inside] * 3 + [outside] * 3,
        scratch_shapes=[
            pltpu.VMEM((64, length), jnp.bfloat16),
            pltpu.VMEM((length, 64), jnp.bfloat16),
            pltpu.VMEM((64, length), jnp.bfloat16),
        ]
        + [pltpu.VMEM(weight.shape, weight.dtype) for weight in weights]
        + [
            pltpu.SemaphoreType.DMA((6,)),
            pltpu.SemaphoreType.DMA((3 * GATHER_COPIES,)),
            pltpu.SemaphoreType.DMA((3 * GATHER_COPIES,)),
        ],
        compiler_params=pltpu.CompilerParams(
            collective_id=collective, has_side_effects=True, vmem_limit_bytes=56 << 20
        ),
        cost_estimate=pl.CostEstimate(
            flops=2 * length * length * 64,
            bytes_accessed=length * 512 * 2,
            transcendentals=length * length // 2,
        ),
    )(rows, *weights)
    return results[0:3], results[3:6]


def run_backward(rows, grads, wide, lse, fc, down, collective):
    length = rows.shape[0] * rows.shape[2]
    inside = pl.BlockSpec(memory_space=pltpu.VMEM)
    outside = pl.BlockSpec(memory_space=pl.ANY)
    received = [
        jax.ShapeDtypeStruct((3, 2, 2) + part.shape[2:], part.dtype)
        for part in (fc, down, fc, down)
    ]
    results = pl.pallas_call(
        attend_backward,
        out_shape=[jax.ShapeDtypeStruct(rows.shape, jnp.bfloat16)] + received,
        in_specs=[inside] * 4 + [outside] * 2,
        out_specs=[inside] + [outside] * 4,
        scratch_shapes=[
            pltpu.VMEM((length, 64), jnp.bfloat16),
            pltpu.VMEM((length, 64), jnp.bfloat16),
            pltpu.VMEM((64, length), jnp.bfloat16),
            pltpu.VMEM((length, 64), jnp.bfloat16),
            pltpu.VMEM((length, 64), jnp.bfloat16),
            pltpu.VMEM((64, length), jnp.float32),
            pltpu.VMEM((1, length), jnp.float32),
            pltpu.VMEM((192, length), jnp.bfloat16),
            pltpu.SemaphoreType.DMA((12,)),
            pltpu.SemaphoreType.DMA((12,)),
        ],
        compiler_params=pltpu.CompilerParams(
            collective_id=collective, has_side_effects=True, vmem_limit_bytes=58 << 20
        ),
        cost_estimate=pl.CostEstimate(
            flops=5 * length * length * 64,
            bytes_accessed=length * 512 * 3,
            transcendentals=length * length // 2,
        ),
    )(rows, grads, wide, lse, fc, down)
    return results[0], results[1:3], results[3:5]


UNITS = 17
TAIL = 896
SHAPES = ((16, 4352), (16, 4352), (64, 1088))
PIECES = ((16, 2176), (16, 2176), (32, 1088))


def places():
    ctx = lax.axis_index("ctx")
    fsdp = lax.axis_index("fsdp")
    return ctx // 8, lax.rem(ctx // 2, 4), lax.rem(ctx, 2), fsdp // 2, lax.rem(fsdp, 2)


def device_at(z, x, y_low, y_high, core):
    return (z * 8 + x * 2 + y_low, y_high * 2 + core)


def z_peer(step):
    z, x, y_low, y_high, core = places()
    return device_at(lax.rem(z + step, 4), x, y_low, y_high, core)


def x_peer(step):
    z, x, y_low, y_high, core = places()
    return device_at(z, lax.rem(x + step, 4), y_low, y_high, core)


def near_peer():
    z, x, y_low, y_high, core = places()
    return device_at(z, x, 1 - y_low, y_high, core)


def cross_peer():
    z, x, y_low, y_high, core = places()
    return device_at(z, x, 1 - y_low, 1 - y_high, core)


def far_peer():
    z, x, y_low, y_high, core = places()
    return device_at(z, x, y_low, 1 - y_high, core)


def twin_peer():
    z, x, y_low, y_high, core = places()
    return device_at(z, x, y_low, y_high, 1 - core)


def far_twin():
    z, x, y_low, y_high, core = places()
    return device_at(z, x, y_low, 1 - y_high, 1 - core)


def ring_peers():
    return [z_peer(step) for step in (1, 2, 3)] + [x_peer(step) for step in (1, 2, 3)]


def greet(peers):
    barrier = pltpu.get_barrier_semaphore()
    for peer in peers:
        pl.semaphore_signal(barrier, inc=1, device_id=peer, device_id_type=MESH)
    pl.semaphore_wait(barrier, len(peers))


class Sender:
    def __init__(self, send_sem, recv_sem):
        self.send_sem = send_sem
        self.recv_sem = recv_sem
        self.used = 0
        self.started = []

    def push(self, source, target, peer):
        copy = pltpu.make_async_remote_copy(
            src_ref=source,
            dst_ref=target,
            send_sem=self.send_sem.at[self.used],
            recv_sem=self.recv_sem.at[self.used],
            device_id=peer,
            device_id_type=MESH,
        )
        self.used += 1
        copy.start()
        self.started.append(copy)
        return copy

    def finish(self):
        for copy in self.started:
            copy.wait_send()


class Mover:
    def __init__(self, sem):
        self.sem = sem
        self.used = 0

    def move(self, source, target):
        copy = pltpu.make_async_copy(source, target, self.sem.at[self.used])
        self.used += 1
        copy.start()
        return copy


GATHER_COPIES = 35


def gather_peers():
    return ring_peers() + [near_peer(), cross_peer(), twin_peer()]


def gather_steps(sources, targets, holds, mover, sender):
    z, x, y_low, y_high, core = places()
    mine = y_high * 2 + core
    cross = (1 - y_high) * 2 + core
    count = len(sources)
    firsts = (2 * z + y_low, 8 + 2 * x + y_low, 16)
    others = (2 * z + 1 - y_low, 8 + 2 * x + 1 - y_low)
    crossed = [
        [
            sender.push(sources[at].at[unit], targets[at].at[mine, unit], cross_peer())
            for unit in others + (16,)
        ]
        for at in range(count)
    ]
    loads = [mover.move(sources[at], holds[at]) for at in range(count)]
    arrivals = [
        sender.push(sources[at], targets[at].at[mine], twin_peer()) for at in range(count)
    ]
    yield
    owns = []
    for at in range(count):
        loads[at].wait()
        owns.append(mover.move(holds[at], targets[at].at[mine]))

    def ring(at, part, unit, kept):
        piece = targets[at].at[cross, unit]
        for step in (1, 3, 2):
            peer = z_peer(step) if part == 0 else x_peer(step)
            kept.append((at, part, step, sender.push(piece, piece, peer)))

    first_ring, second_ring = [], []

    def second(at, nears):
        for part in range(2):
            nears[part].wait_recv()
            ring(at, part, others[part], second_ring)
            piece = targets[at].at[cross, others[part]]
            arrivals.append(sender.push(piece, piece, twin_peer()))

    waiting = None
    for at in range(count):
        nears = []
        for part in range(3):
            crossed[at][part].wait_recv()
            piece = targets[at].at[cross, firsts[part]]
            if part < 2:
                nears.append(sender.push(piece, piece, near_peer()))
                ring(at, part, firsts[part], first_ring)
            arrivals.append(sender.push(piece, piece, twin_peer()))
        yield
        if waiting is not None:
            second(*waiting)
        waiting = (at, nears)
    second(*waiting)
    yield
    for at in range(count):
        for kept, base in ((first_ring, y_low), (second_ring, 1 - y_low)):
            for where, part, step, copy in kept:
                if where != at:
                    continue
                copy.wait_recv()
                if part == 0:
                    unit = 2 * lax.rem(z - step + 4, 4) + base
                else:
                    unit = 8 + 2 * lax.rem(x - step + 4, 4) + base
                piece = targets[at].at[cross, unit]
                arrivals.append(sender.push(piece, piece, twin_peer()))
    for copy in arrivals:
        copy.wait_recv()
    for own in owns:
        own.wait()


def gather_kernel(source, small, target, small_out, hold, small_hold, own_sem, send_sem, recv_sem):
    z, x, y_low, y_high, core = places()
    mine = y_high * 2 + core
    mover = Mover(own_sem)
    load = mover.move(small, small_hold)
    greet(gather_peers() + [far_peer(), far_twin()])
    sender = Sender(send_sem, recv_sem)
    arrivals = [
        sender.push(small, small_out.at[mine], twin_peer()),
        sender.push(small, small_out.at[mine], far_peer()),
        sender.push(small, small_out.at[mine], far_twin()),
    ]
    load.wait()
    own = mover.move(small_hold, small_out.at[mine])
    for _ in gather_steps([source], [target], [hold], mover, sender):
        pass
    for copy in arrivals:
        copy.wait_recv()
    own.wait()
    sender.finish()


def gather_weights(part, small, collective):
    whole = [part, small]
    shapes = [jax.ShapeDtypeStruct((4,) + each.shape, each.dtype) for each in whole]
    return pl.pallas_call(
        gather_kernel,
        out_shape=shapes,
        in_specs=[pl.BlockSpec(memory_space=pl.ANY)] * 2,
        out_specs=[pl.BlockSpec(memory_space=pl.ANY)] * 2,
        scratch_shapes=[pltpu.VMEM(each.shape, each.dtype) for each in whole]
        + [
            pltpu.SemaphoreType.DMA((4,)),
            pltpu.SemaphoreType.DMA((GATHER_COPIES + 3,)),
            pltpu.SemaphoreType.DMA((GATHER_COPIES + 3,)),
        ],
        compiler_params=pltpu.CompilerParams(
            collective_id=collective, has_side_effects=True, vmem_limit_bytes=58 << 20
        ),
        cost_estimate=pl.CostEstimate(flops=0, bytes_accessed=20 << 20, transcendentals=0),
    )(*whole)


def product_kernel(cut, *refs):
    out = refs[-1]
    products = []
    for at in range(0, len(refs) - 1, 4):
        left = jnp.concatenate([refs[at][...], refs[at + 1][...]], axis=1)
        right = jnp.concatenate([refs[at + 2][...], refs[at + 3][...]], axis=0)
        products.append((left, right))
    if cut is None:
        out[...] = dot_nn(*products[0]).astype(jnp.bfloat16)
        return
    (left, right), (other_left, other_right) = products
    out[:, 0:cut] = dot_nn(left, right[:, 0:cut]).astype(jnp.bfloat16)
    shared = dot_nn(left, right[:, cut : cut + 128]) + dot_nn(other_left, other_right[:, 0:128])
    out[:, cut : cut + 128] = shared.astype(jnp.bfloat16)
    out[:, cut + 128 :] = dot_nn(other_left, other_right[:, 128:]).astype(jnp.bfloat16)


def weight_products(operands, width, cut=None):
    size = operands[0][0].shape[0]
    block = 272
    specs, flat = [], []
    for left, other_left, right, other_right in operands:
        specs += [pl.BlockSpec((block, left.shape[1]), lambda step: (step, 0))] * 2
        specs += [pl.BlockSpec(right.shape, lambda step: (0, 0))] * 2
        flat += [left, other_left, right, other_right]
    terms = pl.pallas_call(
        functools.partial(product_kernel, cut),
        grid=(size // block,),
        out_shape=jax.ShapeDtypeStruct((size, width), jnp.bfloat16),
        in_specs=specs,
        out_specs=pl.BlockSpec((block, width), lambda step: (step, 0)),
        compiler_params=pltpu.CompilerParams(vmem_limit_bytes=58 << 20),
        cost_estimate=pl.CostEstimate(
            flops=512 * size * width, bytes_accessed=2 * size * width, transcendentals=0
        ),
    )(*flat)
    return terms.reshape(2, UNITS, size // (2 * UNITS), width)


def push_rings(sender, terms, by_z, by_x):
    z, x, y_low, y_high, core = places()
    copies = []
    for step in (2, 1, 3):
        to_z, to_x = lax.rem(z + step, 4), lax.rem(x + step, 4)
        copies.append(
            sender.push(terms.at[:, pl.ds(2 * to_z, 2)], by_z.at[step - 1], z_peer(step))
        )
        copies.append(
            sender.push(terms.at[:, pl.ds(8 + 2 * to_x, 2)], by_x.at[step - 1], x_peer(step))
        )
    return copies


def widen(values):
    return values.astype(jnp.float32)


def halves(values, group):
    if group == 2:
        return values[0:32], values[32:64]
    return values[:, 0:2176], values[:, 2176:4352]


LAST_COPIES = 6 + 3 * (6 + 3 + 6 + 16 + 16) + 3 + 3 + 3 + 3 + 3 + 9


def last_kernel(*refs):
    terms, tail = refs[0:3], refs[3]
    far_z, far_x = (None,) + refs[4:6], (None,) + refs[6:8]
    totals, small_out = refs[8:11], refs[11]
    scratch = refs[12:]
    own, by, parted, met, merged, landed, summed = [
        scratch[3 * at : 3 * at + 3] for at in range(7)
    ]
    own_t, by_t, parted_t, met_t, merged_t, landed_t, summed_t, whole_t = scratch[21:29]
    units, small_unit = scratch[29:32], scratch[32]
    own_sem, send_sem, recv_sem = scratch[33:36]
    z, x, y_low, y_high, core = places()
    mover = Mover(own_sem)
    order = (2, 1, 0)
    loads = {}
    for group in order:
        loads[group] = [
            mover.move(terms[group].at[:, pl.ds(2 * z, 2)], own[group].at[0]),
            mover.move(terms[group].at[:, pl.ds(8 + 2 * x, 2)], own[group].at[1]),
        ]
        if group > 0:
            loads[group].append(mover.move(far_z[group], by[group].at[0]))
            loads[group].append(mover.move(far_x[group], by[group].at[1]))

    def tail_part(place):
        return tail.at[:, :, pl.ds(pl.multiple_of(place * 4 * TAIL, 128), 4 * TAIL)]

    load_tail = mover.move(tail_part(z), own_t)
    greet(ring_peers() + [near_peer(), cross_peer(), far_peer()])
    sender = Sender(send_sem, recv_sem)
    first = push_rings(sender, terms[0], by[0].at[0], by[0].at[1])
    first_t = [
        sender.push(tail_part(lax.rem(z + step, 4)), by_t.at[step - 1], z_peer(step))
        for step in (2, 1, 3)
    ]

    second = {}
    for group in order:
        for load in loads[group]:
            load.wait()
        if group == 0:
            for copy in first:
                copy.wait_recv()
        second[group] = []
        for ring in range(2):
            for unit in range(2):
                for side in range(2):
                    total = widen(own[group][ring, side, unit])
                    for step in range(3):
                        total = total + widen(by[group][ring, step, side, unit])
                    pair = halves(total.astype(jnp.bfloat16), group)
                    parted[group][ring, 2 * unit, side] = pair[0]
                    parted[group][ring, 2 * unit + 1, side] = pair[1]
            for step in (2, 1, 3):
                place = lax.rem(x + step, 4) if ring == 0 else lax.rem(z + step, 4)
                peer = x_peer(step) if ring == 0 else z_peer(step)
                second[group].append(
                    sender.push(
                        parted[group].at[ring, place], met[group].at[ring, step - 1], peer
                    )
                )
    load_tail.wait()
    for copy in first_t:
        copy.wait_recv()
    for place in range(4):
        columns = slice(TAIL * place, TAIL * (place + 1))
        total = widen(own_t[:, :, columns])
        for step in range(3):
            total = total + widen(by_t[step, :, :, columns])
        parted_t[place] = total.astype(jnp.bfloat16)
    second_t = [
        sender.push(parted_t.at[lax.rem(x + step, 4)], met_t.at[step - 1], x_peer(step))
        for step in (2, 1, 3)
    ]

    def across(source, target):
        return [
            sender.push(source.at[0], target.at[0], near_peer()),
            sender.push(source.at[1], target.at[1], cross_peer()),
            sender.push(source.at[1], target.at[2], far_peer()),
        ]

    third = {}
    for group in order:
        for copy in second[group]:
            copy.wait_recv()
        for ring in range(2):
            total = widen(parted[group][ring, x if ring == 0 else z])
            for step in range(3):
                total = total + widen(met[group][ring, step])
            merged[group][:, ring] = total.astype(jnp.bfloat16)
        third[group] = across(merged[group], landed[group])
    for copy in second_t:
        copy.wait_recv()
    total = widen(parted_t[x])
    for step in range(3):
        total = total + widen(met_t[step])
    merged_t[...] = total.astype(jnp.bfloat16)
    third_t = across(merged_t, landed_t)

    def spot(group, ring, at_z, at_x, side=None):
        unit = 2 * at_z + at_x // 2 if ring == 0 else 8 + 2 * at_x + at_z // 2
        half = lax.rem(at_x, 2) if ring == 0 else lax.rem(at_z, 2)
        if group == 2:
            start, size = ((0, 32), (0, 16), (16, 16))[0 if side is None else side + 1]
            rows = pl.ds(pl.multiple_of(half * 32 + start, 16), size)
            return totals[group].at[unit, rows]
        start, size = ((0, 2176), (0, 1152), (1152, 1024))[0 if side is None else side + 1]
        columns = pl.ds(pl.multiple_of(half * 2176 + start, 128), size)
        return totals[group].at[unit, :, columns]

    def step_on(ring, at_z, at_x, step):
        if ring == 0:
            return lax.rem(at_z + step, 4), at_x
        return at_z, lax.rem(at_x + step, 4)

    passed, ends, owns, nexts = [], [], [], []

    def spread_on(group, ring, source, at_z, at_x):
        place = spot(group, ring, at_z, at_x)
        for step in (1, 3):
            peer = z_peer(step) if ring == 0 else x_peer(step)
            copy = sender.push(source, place, peer)
            nexts.append((group, ring, step, at_z, at_x, copy))

    for group in order:
        for copy in third[group]:
            copy.wait_recv()
        near = widen(merged[group][0]) + widen(landed[group][0])
        away = widen(landed[group][1]) + widen(landed[group][2])
        summed[group][...] = (near + away).astype(jnp.bfloat16)
        for ring in range(2):
            place = spot(group, ring, z, x)
            piece = summed[group].at[ring]
            owns.append(mover.move(piece, place))
            for step in (1, 3, 2):
                peer = x_peer(step) if ring == 0 else z_peer(step)
                passed.append((group, ring, step, sender.push(piece, place, peer)))
            spread_on(group, ring, piece, z, x)
    for copy in third_t:
        copy.wait_recv()
    near = widen(merged_t[0]) + widen(landed_t[0])
    away = widen(landed_t[1]) + widen(landed_t[2])
    summed_t[...] = (near + away).astype(jnp.bfloat16)
    owns.append(mover.move(summed_t, whole_t.at[z, x]))
    for step in (1, 3, 2):
        passed.append((3, 0, step, sender.push(summed_t, whole_t.at[z, x], x_peer(step))))
    for step in (1, 3, 2):
        ends.append(sender.push(summed_t, whole_t.at[z, x], z_peer(step)))

    for group, ring, step, copy in passed:
        copy.wait_recv()
        if group == 3:
            place = whole_t.at[z, lax.rem(x - step + 4, 4)]
            for other in (1, 3, 2):
                ends.append(sender.push(place, place, z_peer(other)))
            continue
        at_z, at_x = step_on(1 - ring, z, x, 4 - step)
        spread_on(group, ring, spot(group, ring, at_z, at_x), at_z, at_x)
    for group, ring, step, at_z, at_x, copy in nexts:
        copy.wait_recv()
        from_z, from_x = step_on(ring, at_z, at_x, 4 - step)
        piece = spot(group, ring, from_z, from_x, 0 if step == 1 else 1)
        peer = z_peer(step) if ring == 0 else x_peer(step)
        ends.append(sender.push(piece, piece, peer))
    for copy in ends:
        copy.wait_recv()
    for copy in owns:
        copy.wait()

    def tile(at):
        return whole_t[at // 28, at // 7 % 4, :, 128 * (at % 7) : 128 * (at % 7 + 1)]

    for at in range(34):
        units[0][:, 128 * at : 128 * (at + 1)] = tile(at)
        units[1][:, 128 * at : 128 * (at + 1)] = tile(34 + at)
    for row in range(4):
        for at in range(9):
            width = min(128, 1088 - 128 * at)
            units[2][16 * row : 16 * row + 16, 128 * at : 128 * at + width] = tile(
                68 + 9 * row + at
            )[:, :width]
    for at in range(8):
        small_unit[:, 128 * at : 128 * (at + 1)] = tile(104 + at)
    lasts = [mover.move(units[group], totals[group].at[16]) for group in range(3)]
    lasts.append(mover.move(small_unit, small_out))
    for copy in lasts:
        copy.wait()
    sender.finish()


def last_exchange(terms, tail, far_z, far_x, collective):
    low = jnp.bfloat16

    def each(make):
        return [pltpu.VMEM(make(*pair), low) for pair in zip(SHAPES, PIECES)]

    scratch = (
        each(lambda unit, piece: (2, 2, 2) + unit)
        + each(lambda unit, piece: (2, 3, 2, 2) + unit)
        + each(lambda unit, piece: (2, 4, 2) + piece)
        + each(lambda unit, piece: (2, 3, 2) + piece)
        + each(lambda unit, piece: (2, 2) + piece)
        + each(lambda unit, piece: (3, 2) + piece)
        + each(lambda unit, piece: (2,) + piece)
        + [
            pltpu.VMEM((2, 16, 4 * TAIL), low),
            pltpu.VMEM((3, 2, 16, 4 * TAIL), low),
            pltpu.VMEM((4, 2, 16, TAIL), low),
            pltpu.VMEM((3, 2, 16, TAIL), low),
            pltpu.VMEM((2, 16, TAIL), low),
            pltpu.VMEM((3, 16, TAIL), low),
            pltpu.VMEM((16, TAIL), low),
            pltpu.VMEM((4, 4, 16, TAIL), low),
        ]
        + each(lambda unit, piece: unit)
        + [
            pltpu.VMEM((16, 1024), low),
            pltpu.SemaphoreType.DMA((24,)),
            pltpu.SemaphoreType.DMA((LAST_COPIES,)),
            pltpu.SemaphoreType.DMA((LAST_COPIES,)),
        ]
    )
    return pl.pallas_call(
        last_kernel,
        out_shape=[jax.ShapeDtypeStruct((UNITS,) + unit, low) for unit in SHAPES]
        + [jax.ShapeDtypeStruct((16, 1024), low)],
        in_specs=[pl.BlockSpec(memory_space=pl.ANY)] * 8,
        out_specs=[pl.BlockSpec(memory_space=pl.ANY)] * 4,
        scratch_shapes=scratch,
        compiler_params=pltpu.CompilerParams(
            collective_id=collective, has_side_effects=True, vmem_limit_bytes=48 << 20
        ),
        cost_estimate=pl.CostEstimate(flops=0, bytes_accessed=40 << 20, transcendentals=0),
    )(*terms, tail, *far_z, *far_x)


def reduce_grads(terms, small, far_z, far_x, collective):
    down = terms[2][:, 16].reshape(2, 4, 16, 1088)
    down = jnp.pad(down, ((0, 0), (0, 0), (0, 0), (0, 64)))
    down = jnp.transpose(down, (0, 2, 1, 3)).reshape(2, 16, 4608)
    extra = jnp.pad(small, ((0, 0), (0, 16 * 1024 - small.shape[1]))).reshape(2, 16, 1024)
    tail = jnp.concatenate(
        [terms[0][:, 16], terms[1][:, 16], down, extra.astype(jnp.bfloat16)], axis=-1
    )
    joint, fc, down, small = last_exchange(terms, tail, far_z, far_x, collective)
    joint = joint.reshape(272, 4352)
    outs = (
        joint[:, :3264].astype(jnp.float32),
        joint[:, 3264:].astype(jnp.float32),
        fc.reshape(272, 4352).astype(jnp.float32),
        down.reshape(1088, 1088).astype(jnp.float32),
    )
    return outs, small.reshape(-1)[:3264].astype(jnp.float32)


def mean_rows(values):
    return jnp.sum(values, axis=-1, keepdims=True) * (1.0 / values.shape[-1])


def normal_rows(values):
    centre = values - mean_rows(values)
    scale = lax.rsqrt(mean_rows(centre * centre) + 1e-05)
    return centre * scale, scale


def norm_back(grads, gain, unit, scale):
    scaled = grads * gain
    return scale * (scaled - mean_rows(scaled) - unit * mean_rows(scaled * unit))


def column_sums(values):
    return jnp.sum(values, axis=0, keepdims=True)


def turned(values):
    rows, width = values.shape
    full = jnp.concatenate([values, jnp.zeros((rows, 1152 - width), values.dtype)], axis=1)
    return full.T[0:width, :]


def before_kernel(tokens, gain, offset, weight, bias, packed, turned_ref, joint, joint_t):
    unit, _ = normal_rows(widen(tokens[...]))
    normed = (unit * widen(gain[...]) + widen(offset[...])).astype(jnp.bfloat16)
    turned_ref[...] = turned(normed)
    joint[...] = (dot_nn(normed, weight[...]) + widen(bias[...])).astype(jnp.bfloat16)
    blank = jnp.zeros((joint.shape[0], 64), jnp.bfloat16)
    joint_t[...] = jnp.concatenate([joint[...], blank], axis=1).T
    for head in range(HEADS):
        for part in range(3):
            start = 1088 * part + 64 * head
            packed[head, 64 * part : 64 * part + 64] = joint_t[start : start + 64]


def run_before(tokens, gain, offset, weight, bias):
    rows = tokens.shape[0]
    return pl.pallas_call(
        before_kernel,
        out_shape=(
            jax.ShapeDtypeStruct((HEADS, 192, rows), jnp.bfloat16),
            jax.ShapeDtypeStruct((1088, rows), jnp.bfloat16),
        ),
        scratch_shapes=[
            pltpu.VMEM((rows, 3264), jnp.bfloat16),
            pltpu.VMEM((3328, rows), jnp.bfloat16),
        ],
        compiler_params=pltpu.CompilerParams(vmem_limit_bytes=40 << 20),
        cost_estimate=pl.CostEstimate(
            flops=2 * rows * 1088 * 3264, bytes_accessed=8 << 20, transcendentals=0
        ),
    )(tokens, gain, offset, weight, bias)


def middle_kernel(
    heads,
    tokens,
    cotangent,
    w_out,
    b_out,
    gain,
    offset,
    b_down,
    fc,
    b_fc,
    down,
    result,
    grad_middle,
    grad_heads,
    normed_t,
    grad_branch,
    active_t,
    grad_hidden,
    d_fc,
    sums,
    attended,
    normed,
    unit,
    scale,
    total,
    grads,
):
    at = pl.program_id(0)

    @pl.when(at == 0)
    def _():
        filler = jnp.zeros((64, heads.shape[1]), jnp.bfloat16)
        attended[...] = jnp.concatenate([heads[...], filler], axis=0).T[:, 0:1088]
        middle = widen(tokens[...]) + (dot_nn(attended[...], w_out[...]) + widen(b_out[...]))
        unit[...], scale[...] = normal_rows(middle)
        normed[...] = (unit[...] * widen(gain[...]) + widen(offset[...])).astype(jnp.bfloat16)
        normed_t[...] = turned(normed[...])
        total[...] = middle + widen(b_down[...])
        grads[...] = jnp.zeros_like(grads)

    hidden = dot_nn(normed[...], fc[...]) + widen(b_fc[...])
    square = hidden * hidden
    bend = jnp.tanh(0.7978845608028654 * (hidden + 0.044715 * square * hidden))
    active = (0.5 * hidden * (1.0 + bend)).astype(jnp.bfloat16)
    slope = 0.5 * (1.0 + bend) + 0.5 * hidden * (1.0 - bend * bend) * (
        0.7978845608028654 * (1.0 + 3.0 * 0.044715 * square)
    )
    back = (dot_nt(cotangent[...], down[...]) * slope).astype(jnp.bfloat16)
    active_t[...] = active.T
    grad_hidden[...] = back
    d_fc[...] = column_sums(widen(back))
    total[...] += dot_nn(active, down[...])
    grads[...] += dot_nt(back, fc[...])

    @pl.when(at == pl.num_programs(0) - 1)
    def _():
        result[...] = total[...].astype(jnp.bfloat16)
        arrived = widen(cotangent[...])
        whole = grads[...]
        grad = arrived + norm_back(whole, widen(gain[...]), unit[...], scale[...])
        grad_middle[...] = grad
        low = grad.astype(jnp.bfloat16)
        grad_branch[:, 0:64] = jnp.zeros((low.shape[0], 64), jnp.bfloat16)
        grad_branch[:, 64:1152] = low
        sums[0:1, :] = column_sums(widen(low))
        sums[1:2, :] = column_sums(whole * unit[...])
        sums[2:3, :] = column_sums(whole)
        sums[3:4, :] = column_sums(arrived)
        attended[...] = dot_nt(low, w_out[...]).astype(jnp.bfloat16)
        grad_heads[...] = turned(attended[...])


def run_middle(heads, tokens, cotangent, w_out, b_out, gain, offset, b_down, fc, b_fc, down):
    rows = tokens.shape[0]
    low, wide = jnp.bfloat16, jnp.float32
    block = 256

    def fixed(shape):
        return pl.BlockSpec(shape, lambda step: (0,) * len(shape))

    vector = fixed((1, 1088))
    square = fixed((rows, 1088))
    across = pl.BlockSpec((rows, block), lambda step: (0, step))
    line = pl.BlockSpec((1, block), lambda step: (0, step))
    return pl.pallas_call(
        middle_kernel,
        grid=(4352 // block,),
        in_specs=[
            fixed((1088, rows)),
            square,
            square,
            fixed((1088, 1088)),
            vector,
            vector,
            vector,
            vector,
            pl.BlockSpec((1088, block), lambda step: (0, step)),
            line,
            pl.BlockSpec((block, 1088), lambda step: (step, 0)),
        ],
        out_specs=[
            square,
            square,
            fixed((1088, rows)),
            fixed((1088, rows)),
            fixed((rows, 1152)),
            pl.BlockSpec((block, rows), lambda step: (step, 0)),
            across,
            line,
            fixed((4, 1088)),
        ],
        out_shape=[
            jax.ShapeDtypeStruct((rows, 1088), low),
            jax.ShapeDtypeStruct((rows, 1088), wide),
            jax.ShapeDtypeStruct((1088, rows), low),
            jax.ShapeDtypeStruct((1088, rows), low),
            jax.ShapeDtypeStruct((rows, 1152), low),
            jax.ShapeDtypeStruct((4352, rows), low),
            jax.ShapeDtypeStruct((rows, 4352), low),
            jax.ShapeDtypeStruct((1, 4352), wide),
            jax.ShapeDtypeStruct((4, 1088), wide),
        ],
        scratch_shapes=[
            pltpu.VMEM((rows, 1088), low),
            pltpu.VMEM((rows, 1088), low),
            pltpu.VMEM((rows, 1088), wide),
            pltpu.VMEM((rows, 1), wide),
            pltpu.VMEM((rows, 1088), wide),
            pltpu.VMEM((rows, 1088), wide),
        ],
        compiler_params=pltpu.CompilerParams(vmem_limit_bytes=48 << 20),
        cost_estimate=pl.CostEstimate(
            flops=8 * rows * 1088 * 4352, bytes_accessed=24 << 20, transcendentals=rows * 4352
        ),
    )(heads, tokens, cotangent, w_out, b_out, gain, offset, b_down, fc, b_fc, down)


def after_kernel(packed, weight, tokens, gain, grad_middle, joint, grad_tokens, sums, line, joint_t):
    for head in range(HEADS):
        for part in range(3):
            start = 1088 * part + 64 * head
            joint_t[start : start + 64] = packed[head, 64 * part : 64 * part + 64]
    joint_t[3264:3328] = jnp.zeros((64, joint.shape[0]), jnp.bfloat16)
    joint[...] = joint_t[...].T
    unit, scale = normal_rows(widen(tokens[...]))
    grads = dot_nt(joint[:, 0:3264], weight[...])
    back = norm_back(grads, widen(gain[...]), unit, scale)
    grad_tokens[...] = grad_middle[...] + back
    sums[0:1, :] = column_sums(grads * unit)
    sums[1:2, :] = column_sums(grads)
    line[...] = column_sums(widen(joint[:, 0:3264]))


def run_after(packed, weight, tokens, gain, grad_middle):
    rows = tokens.shape[0]
    return pl.pallas_call(
        after_kernel,
        out_shape=(
            jax.ShapeDtypeStruct((rows, 3328), jnp.bfloat16),
            jax.ShapeDtypeStruct((rows, 1088), jnp.float32),
            jax.ShapeDtypeStruct((2, 1088), jnp.float32),
            jax.ShapeDtypeStruct((1, 3264), jnp.float32),
        ),
        scratch_shapes=[pltpu.VMEM((3328, rows), jnp.bfloat16)],
        compiler_params=pltpu.CompilerParams(vmem_limit_bytes=40 << 20),
        cost_estimate=pl.CostEstimate(
            flops=2 * rows * 1088 * 3264, bytes_accessed=10 << 20, transcendentals=0
        ),
    )(packed, weight, tokens, gain, grad_middle)


def local(
    tokens,
    cotangent,
    ln1_scale,
    ln1_bias,
    w_qkv,
    bias_q,
    bias_v,
    w_out,
    bias_out,
    ln2_scale,
    ln2_bias,
    w_fc,
    bias_fc,
    w_down,
    bias_down,
):
    ctx_count = lax.axis_size("ctx")
    vectors = (
        ln1_scale,
        ln1_bias,
        bias_q,
        bias_v,
        bias_out,
        ln2_scale,
        ln2_bias,
        bias_down,
        bias_fc,
    )
    small = jnp.concatenate(
        [jnp.stack(vectors[:8]), bias_fc.reshape(4, 272), jnp.zeros((4, 272), jnp.bfloat16)]
    )
    own_parts = [
        part.reshape(UNITS, part.shape[0] // UNITS, part.shape[1])
        for part in (w_qkv, w_out, w_fc, w_down)
    ]
    full_qkv, full_small = gather_weights(own_parts[0], small, 5)
    full_qkv = full_qkv.reshape(1088, 3264)
    lines = [full_small[:, at].reshape(1, 1088) for at in range(8)]
    (line_scale1, line_shift1, line_bq, line_bv, line_bout, line_scale2, line_shift2) = lines[:7]
    line_bdown = lines[7]
    line_bfc = full_small[:, 8:12].reshape(1, 4352)
    z, x, y_low, y_high, core = places()

    def swap(values):
        return lax.ppermute(values, "fsdp", [(0, 1), (1, 0), (2, 3), (3, 2)])

    def split(quarters):
        first, second = quarters[:, 0], quarters[:, 1]
        keep = jnp.where(core == 0, first, second)
        give = jnp.where(core == 0, second, first)
        keep = jnp.where(y_high == 0, keep, keep[::-1])
        give = jnp.where(y_high == 0, give, give[::-1])
        return keep, give

    def products(left, right):
        width, rows = left.shape
        keep, give = split(left.reshape(2, 2, width // 4, rows))
        keep, give = keep.reshape(width // 2, rows), give.reshape(width // 2, rows)
        return keep, swap(give), right, swap(right)

    bias_joint = jnp.concatenate([line_bq, jnp.zeros_like(line_bq), line_bv], axis=1)
    packed, normed_t = run_before(tokens[0], line_scale1, line_shift1, full_qkv, bias_joint)
    head_rows = spread_heads(packed, ctx_count, 1)
    (out_rows, wide_out, lse_rows), (full_out, full_fc, full_down) = run_forward(
        head_rows, own_parts[1:], 8
    )
    full_out = full_out.reshape(1088, 1088)
    full_fc = full_fc.reshape(1088, 4352)
    full_down = full_down.reshape(4352, 1088)
    attended_t = collect_heads(out_rows, ctx_count, 2).reshape(1088, -1)
    (
        result,
        grad_middle,
        grad_heads,
        normed2_t,
        grad_branch,
        active_t,
        grad_hidden,
        line_fc,
        sums_middle,
    ) = run_middle(
        attended_t,
        tokens[0],
        cotangent[0],
        full_out,
        line_bout,
        line_scale2,
        line_shift2,
        line_bdown,
        full_fc,
        line_bfc,
        full_down,
    )
    d_down = weight_products([products(active_t, cotangent[0])], 1088)
    d_fc = weight_products([products(normed2_t, grad_hidden)], 4352)
    out_products = products(attended_t, grad_branch)
    grad_rows = spread_heads(
        grad_heads.reshape(HEADS, HEAD_DIM, -1), ctx_count, 3
    )
    joint_rows_grad, far_z, far_x = run_backward(
        head_rows, grad_rows, wide_out, lse_rows, d_fc, d_down, 7
    )
    packed_grads = collect_heads(joint_rows_grad, ctx_count, 4)
    grad_joint, grad_inputs, sums_after, line_joint = run_after(
        packed_grads, full_qkv, tokens[0], line_scale1, grad_middle
    )
    d_joint = weight_products([products(normed_t, grad_joint), out_products], 4352, 3200)
    d_bout, d_scale2, d_shift2, d_bdown = [sums_middle[at] for at in range(4)]
    d_scale1, d_shift1 = sums_after[0], sums_after[1]
    d_bq, d_bv, d_bfc = line_joint[0, :1088], line_joint[0, 2176:], line_fc[0]
    narrow = (d_scale1, d_shift1, d_bq, d_bv, d_bout, d_scale2, d_shift2, d_bdown, d_bfc)
    sums = jnp.concatenate([vector.reshape(4, -1) for vector in narrow], axis=1)
    keep, give = split(sums.reshape(2, 2, 3264))
    sums = keep + swap(give)
    (t_qkv, t_out, t_fc, t_down), extras = reduce_grads(
        (d_joint, d_fc, d_down), sums, far_z, far_x, 6
    )
    (t_scale1, t_shift1, t_bq, t_bv, t_bout, t_scale2, t_shift2, t_bdown) = [
        extras[at * 272 : (at + 1) * 272] for at in range(8)
    ]
    t_bfc = extras[2176:]
    return (
        result[None],
        grad_inputs[None],
        t_scale1,
        t_shift1,
        t_qkv,
        t_bq,
        t_bv,
        t_out,
        t_bout,
        t_scale2,
        t_shift2,
        t_fc,
        t_bfc,
        t_down,
        t_bdown,
    )


def solution(mesh):
    placed = (
        P("fsdp", "ctx", None),
        P("fsdp", "ctx", None),
        P("fsdp"),
        P("fsdp"),
        P("fsdp", None),
        P("fsdp"),
        P("fsdp"),
        P("fsdp", None),
        P("fsdp"),
        P("fsdp"),
        P("fsdp"),
        P("fsdp", None),
        P("fsdp"),
        P("fsdp", None),
        P("fsdp"),
    )
    return jax.shard_map(
        local,
        mesh=mesh,
        in_specs=placed,
        out_specs=(
            P("fsdp", "ctx", None),
            P("fsdp", "ctx", None),
            P("fsdp"),
            P("fsdp"),
            P("fsdp", None),
            P("fsdp"),
            P("fsdp"),
            P("fsdp", None),
            P("fsdp"),
            P("fsdp"),
            P("fsdp"),
            P("fsdp", None),
            P("fsdp"),
            P("fsdp", None),
            P("fsdp"),
        ),
        check_vma=False,
    )
```
